128 devices in a mesh: replica: 64 (over y, z, x_lo, core), shard: 2 (over x_hi).
Axes of the slice: x: 4 (x_hi: 2, x_lo: 2; x = x_hi * 2 + x_lo), y: 4, z: 4, core: 2. Of those that a mesh axis runs over, the one named last changes fastest.
Arguments:
- tokens: bfloat16 [768, 196, 512], P(('replica', 'shard')), may hold values from -6 to 6
- image_counts: int32 [128], P(('replica', 'shard')), may hold values from 1 to 6, as said below
- shift_mask: int32 [4, 49, 49], replicated, may hold values from 0 to 1, as said below
- rel_index: int32 [49, 49], replicated, may hold values from 0 to 168, as said below
- norm1_gain: bfloat16 [512], P('shard'), may hold values from 0.25 to 1.75
- norm1_bias: bfloat16 [512], P('shard'), may hold values from -1.5 to 1.5
- qkv_weight: bfloat16 [512, 1536], P('shard'), may hold values from -0.25 to 0.25
- q_bias: bfloat16 [512], P('shard'), may hold values from -1.5 to 1.5
- v_bias: bfloat16 [512], P('shard'), may hold values from -1.5 to 1.5
- rel_table: bfloat16 [169, 16], P(None, 'shard'), may hold values from -4 to 4
- proj_weight: bfloat16 [512, 512], P('shard'), may hold values from -1 to 1
- proj_bias: bfloat16 [512], P('shard'), may hold values from -1.5 to 1.5
- norm2_gain: bfloat16 [512], P('shard'), may hold values from 0.25 to 1.75
- norm2_bias: bfloat16 [512], P('shard'), may hold values from -1.5 to 1.5
- fc1_weight: bfloat16 [512, 2048], P('shard'), may hold values from -0.25 to 0.25
- fc1_bias: bfloat16 [2048], P('shard'), may hold values from -1.5 to 1.5
- fc2_weight: bfloat16 [2048, 512], P('shard'), may hold values from -0.1875 to 0.1875
- fc2_bias: bfloat16 [512], P('shard'), may hold values from -1.5 to 1.5
- out_grad: bfloat16 [768, 196, 512], P(('replica', 'shard')), may hold values from -6 to 6
Outputs:
- block_out: bfloat16 [768, 196, 512], P(('replica', 'shard'))
- tokens_grad: float32 [768, 196, 512], P(('replica', 'shard'))
- norm1_gain_grad: float32 [512], P('shard')
- norm1_bias_grad: float32 [512], P('shard')
- qkv_weight_grad: float32 [512, 1536], P('shard')
- q_bias_grad: float32 [512], P('shard')
- v_bias_grad: float32 [512], P('shard')
- rel_table_grad: float32 [169, 16], P(None, 'shard')
- proj_weight_grad: float32 [512, 512], P('shard')
- proj_bias_grad: float32 [512], P('shard')
- norm2_gain_grad: float32 [512], P('shard')
- norm2_bias_grad: float32 [512], P('shard')
- fc1_weight_grad: float32 [512, 2048], P('shard')
- fc1_bias_grad: float32 [2048], P('shard')
- fc2_weight_grad: float32 [2048, 512], P('shard')
- fc2_bias_grad: float32 [512], P('shard')
The draws below stay inside these ranges and needn't reach their ends.
Inputs may be any that keep to these rules, and one draw needn't show every extreme that they name: `image_counts`: images held by each device in its first slots; some device holds 6 images and some device holds 1. `shift_mask`: 1 where a query may attend a key of the same window; symmetric, and 1 on the diagonal. `rel_index`: pairs with the same offset between query and key name the same table row, different offsets different rows.
All inputs are finite; a program needn't handle non-finite values.
Results may differ from the reference program's by a relative error of at most 0.013.
Values may be sent and summed in bfloat16 or wider, within the bound.
A program may use at most 192 MiB of HBM per device.

```python
import jax
import jax.numpy as jnp
from jax import lax

C = 512
HEADS = 16
MLP = 2048
WIN = 7
SIDE = 14
SHIFT = 3
IMG_CAP = 6
TABLE = 169
SLOTS = 768
N_REPLICA = 64
N_SHARD = 2


def draw_image_counts(key, part):
    key = jax.random.fold_in(key, 11)
    key_one, key_two, key_three = jax.random.split(key, 3)
    devices = N_REPLICA * N_SHARD
    counts = jax.random.randint(key_one, (devices,), 1, IMG_CAP + 1)
    leading = jax.random.randint(key_two, (), 0, devices)
    second = (leading + 1 + jax.random.randint(key_three, (), 0, devices - 1)) % devices
    counts = counts.at[leading].set(IMG_CAP).at[second].set(1)
    return counts.astype(jnp.int32)


def labels_along(key_low, key_high):
    lower = jax.random.randint(key_low, (), WIN - 2, WIN + 2)
    upper = lower + 2 + jax.random.randint(key_high, (), 0, SIDE - 3 - lower)
    cells = jnp.arange(SIDE, dtype=jnp.int32)
    return (cells >= lower).astype(jnp.int32) + (cells >= upper).astype(jnp.int32)


def draw_shift_mask(key, part):
    key = jax.random.fold_in(key, 23)
    split_keys = jax.random.split(key, 4)
    row_labels = labels_along(split_keys[0], split_keys[1])
    col_labels = labels_along(split_keys[2], split_keys[3])
    labels = row_labels[:, None] * 3 + col_labels[None, :]
    blocks_side = SIDE // WIN
    labels = labels.reshape(blocks_side, WIN, blocks_side, WIN).transpose(0, 2, 1, 3)
    labels = labels.reshape(blocks_side * blocks_side, WIN * WIN)
    return (labels[:, :, None] == labels[:, None, :]).astype(jnp.int32)


def draw_rel_index(key, part):
    key = jax.random.fold_in(key, 37)
    cells = jnp.arange(WIN * WIN, dtype=jnp.int32)
    row_of = cells // WIN
    col_of = cells % WIN
    offsets = (row_of[:, None] - row_of[None, :] + WIN - 1) * (2 * WIN - 1) + (col_of[:, None] - col_of[None, :] + WIN - 1)
    order = jax.random.permutation(key, (2 * WIN - 1) ** 2)
    return order[offsets].astype(jnp.int32)


def steps_of(stream_key, extent, cuts, low, top_value):
    level, own = 1.0, jax.random.fold_in(stream_key, 6)
    for position, blocks in cuts:
        steps = jnp.exp(jax.random.uniform(jax.random.fold_in(own, position), (blocks,), jnp.float32, low / len(cuts), top_value / len(cuts)))
        level = level * jnp.repeat(steps, extent[position] // blocks).reshape([-1 if axis == position else 1 for axis in range(len(extent))])
    return level


def normal_values(own_key, shape, scale, reach, shards=(), held_as=jnp.bfloat16):
    entries = scale * jax.random.normal(own_key, shape, jnp.float32)
    if shards:
        entries = entries * steps_of(own_key, shape, shards, -0.22, 0.18)
    return jnp.clip(entries, -reach, reach).astype(held_as)


def setup_inputs(seed: int = 0) -> dict:
    key_of = jax.random.split(jax.random.key(seed), 20)
    tokens = normal_values(key_of[0], (SLOTS, SIDE * SIDE, C), 1.0, 6.0, ((0, 128),))
    image_counts = draw_image_counts(jax.random.fold_in(key_of[19], 71), 0)
    shift_mask = draw_shift_mask(jax.random.fold_in(key_of[19], 71), 0)
    rel_index = draw_rel_index(jax.random.fold_in(key_of[19], 71), 0)
    norm1_gain = jnp.clip(1.0 + 0.15 * jax.random.normal(key_of[4], (C,), jnp.float32), 0.25, 1.75).astype(jnp.bfloat16)
    norm1_bias = normal_values(key_of[5], (C,), 0.3, 1.5, ((0, 2),))
    qkv_weight = normal_values(key_of[6], (C, 3 * C), C ** -0.5, 0.25, ((0, 2),))
    q_bias = normal_values(key_of[7], (C,), 0.3, 1.5, ((0, 2),))
    v_bias = normal_values(key_of[8], (C,), 0.3, 1.5, ((0, 2),))
    rel_table = normal_values(key_of[9], (TABLE, HEADS), 1.0, 4.0, ((1, 2),))
    proj_weight = normal_values(key_of[10], (C, C), (C // 16) ** -0.5, 1.0, ((0, 2),))
    proj_bias = normal_values(key_of[11], (C,), 0.3, 1.5, ((0, 2),))
    norm2_gain = jnp.clip(1.0 + 0.15 * jax.random.normal(key_of[12], (C,), jnp.float32), 0.25, 1.75).astype(jnp.bfloat16)
    norm2_bias = normal_values(key_of[13], (C,), 0.3, 1.5, ((0, 2),))
    fc1_weight = normal_values(key_of[14], (C, MLP), C ** -0.5, 0.25, ((0, 2),))
    fc1_bias = normal_values(key_of[15], (MLP,), 0.3, 1.5, ((0, 2),))
    fc2_weight = normal_values(key_of[16], (MLP, C), (MLP // 2) ** -0.5, 0.1875, ((0, 2),))
    fc2_bias = normal_values(key_of[17], (C,), 0.3, 1.5, ((0, 2),))
    out_grad = normal_values(key_of[18], (SLOTS, SIDE * SIDE, C), 1.0, 6.0, ((0, 128),))
    return {"tokens": tokens, "image_counts": image_counts, "shift_mask": shift_mask, "rel_index": rel_index, "norm1_gain": norm1_gain, "norm1_bias": norm1_bias, "qkv_weight": qkv_weight, "q_bias": q_bias, "v_bias": v_bias, "rel_table": rel_table, "proj_weight": proj_weight, "proj_bias": proj_bias, "norm2_gain": norm2_gain, "norm2_bias": norm2_bias, "fc1_weight": fc1_weight, "fc1_bias": fc1_bias, "fc2_weight": fc2_weight, "fc2_bias": fc2_bias, "out_grad": out_grad}


EPSILON = 1e-05
HIGH = lax.Precision.HIGHEST

@jax.custom_vjp
def low(v):
    return lax.optimization_barrier(v.astype(jnp.bfloat16)).astype(jnp.float32)

@jax.custom_vjp
def low_back(v):
    return v

def low_keep(v):
    return (low(v), None)

def low_pass(kept, grad):
    return (grad,)

def back_keep(v):
    return (v, None)

def back_low(kept, grad):
    return (low(grad),)
low.defvjp(low_keep, low_pass)
low_back.defvjp(back_keep, back_low)

def layer_norm(values, gain, shift):
    center = values - lax.optimization_barrier(jnp.mean(values, -1, keepdims=True))
    spread = lax.optimization_barrier(jnp.mean(center * center, -1, keepdims=True))
    return center * lax.rsqrt(spread + EPSILON) * gain + shift

def to_windows(values):
    images = values.shape[0]
    feats = values.shape[-1]
    blocks_side = SIDE // WIN
    grid = values.reshape(images, SIDE, SIDE, feats)
    grid = jnp.roll(grid, (-SHIFT, -SHIFT), (1, 2))
    grid = grid.reshape(images, blocks_side, WIN, blocks_side, WIN, feats).transpose(0, 1, 3, 2, 4, 5)
    return grid.reshape(images * blocks_side * blocks_side, WIN * WIN, feats)

def from_windows(values, images):
    feats = values.shape[-1]
    blocks_side = SIDE // WIN
    grid = values.reshape(images, blocks_side, blocks_side, WIN, WIN, feats).transpose(0, 1, 3, 2, 4, 5)
    grid = jnp.roll(grid.reshape(images, SIDE, SIDE, feats), (SHIFT, SHIFT), (1, 2))
    return grid.reshape(images, SIDE * SIDE, feats)

def matmul(left, right):
    return jnp.dot(left, right, precision=HIGH, preferred_element_type=jnp.float32)

def layer(inputs, params, mask_add, rel_index):
    gain_one, shift_one, qkv_mat, qbias, vbias, table, proj_mat, pbias, gain_two, shift_two, fc1_mat, fbias_one, fc2_mat, fbias_two = params
    images = inputs.shape[0]
    width = inputs.shape[-1]
    heads = table.shape[1]
    head_dim = width // heads
    normed = low(layer_norm(inputs, gain_one, shift_one))
    win_rows = to_windows(normed)
    windows = win_rows.shape[0]
    wtok = win_rows.shape[1]
    qkv = low_back(matmul(win_rows.reshape(-1, width), qkv_mat)).reshape(windows, wtok, 3 * width)
    qkv = qkv + jnp.concatenate([qbias, jnp.zeros_like(qbias), vbias])
    queries = low(qkv[..., :width] * head_dim ** (-0.5)).reshape(windows, wtok, heads, head_dim)
    key_rows = low(qkv[..., width:2 * width]).reshape(windows, wtok, heads, head_dim)
    value_rows = low(qkv[..., 2 * width:]).reshape(windows, wtok, heads, head_dim)
    raw = low_back(jnp.einsum('wqhd,wkhd->whqk', queries, key_rows, precision=HIGH))
    position_bias = table[rel_index].transpose(2, 0, 1)
    scores = raw.reshape(images, -1, heads, wtok, wtok) + position_bias[None, None] + mask_add[None, :, None]
    probs = low(jax.nn.softmax(scores, -1)).reshape(windows, heads, wtok, wtok)
    attended = low(low_back(jnp.einsum('whqk,wkhd->wqhd', probs, value_rows, precision=HIGH)))
    projected = low_back(matmul(attended.reshape(-1, width), proj_mat)) + pbias
    middle = inputs + from_windows(projected.reshape(windows, wtok, width), images)
    normed_two = low(layer_norm(middle, gain_two, shift_two)).reshape(-1, width)
    hidden_pre = low_back(matmul(normed_two, fc1_mat)) + fbias_one
    hidden_act = low(jax.nn.gelu(hidden_pre, approximate=False))
    branch = low_back(matmul(hidden_act, fc2_mat)) + fbias_two
    return middle + branch.reshape(inputs.shape)

def reference(tokens, image_counts, shift_mask, rel_index, norm1_gain, norm1_bias, qkv_weight, q_bias, v_bias, rel_table, proj_weight, proj_bias, norm2_gain, norm2_bias, fc1_weight, fc1_bias, fc2_weight, fc2_bias, out_grad):
    slots = tokens.shape[0]
    slot_ids = jnp.arange(slots, dtype=jnp.int32)
    valid = (slot_ids % IMG_CAP < image_counts[slot_ids // IMG_CAP]).astype(jnp.float32)[:, None, None]
    mask_add = jnp.where(shift_mask == 1, 0.0, -100.0).astype(jnp.float32)
    params = tuple((item.astype(jnp.float32) for item in (norm1_gain, norm1_bias, qkv_weight, q_bias, v_bias, rel_table, proj_weight, proj_bias, norm2_gain, norm2_bias, fc1_weight, fc1_bias, fc2_weight, fc2_bias)))
    inputs = tokens.astype(jnp.float32)
    batch_images = 16

    def forward(values, weights):

        def one_group(group):
            return layer(group, weights, mask_add, rel_index)
        groups = values.reshape(-1, batch_images, values.shape[1], values.shape[2])
        return lax.map(jax.checkpoint(one_group), groups).reshape(values.shape)
    result, back_fn = jax.vjp(forward, inputs, params)
    grad_inputs, grads = back_fn(out_grad.astype(jnp.float32) * valid)
    return ((result * valid).astype(jnp.bfloat16), grad_inputs, grads[0], grads[1], grads[2], grads[3], grads[4], grads[5], grads[6], grads[7], grads[8], grads[9], grads[10], grads[11], grads[12], grads[13])
```

```python
from functools import partial

import jax
import jax.numpy as jnp
import numpy as np
from jax import lax
from jax.experimental import pallas as pl
from jax.experimental.pallas import tpu as pltpu
from jax.sharding import PartitionSpec as P

WIN = 7
SIDE = 14
SHIFT = 3
EPSILON = 1e-05
MASKED = -1e30
WTOK = WIN * WIN
ROWS = 56
WPAD = 64
BLOCK = 512
F32 = jnp.float32
BF16 = jnp.bfloat16


def nn(left, right):
    return jnp.dot(left, right, preferred_element_type=F32)


def nt(left, right):
    return lax.dot_general(left, right, (((1,), (1,)), ((), ())), preferred_element_type=F32)


def tn(left, right):
    return lax.dot_general(left, right, (((0,), (0,)), ((), ())), preferred_element_type=F32)


def window_places():
    place = np.zeros((4 * ROWS, SIDE * SIDE), np.float32)
    for window in range(4):
        for cell in range(WTOK):
            i = window // 2 * WIN + cell // WIN
            j = window % 2 * WIN + cell % WIN
            source = (i + SHIFT) % SIDE * SIDE + (j + SHIFT) % SIDE
            place[window * ROWS + cell, source] = 1
    return place


def normalize(values):
    center = values - jnp.mean(values, -1, keepdims=True)
    rate = lax.rsqrt(jnp.mean(center * center, -1, keepdims=True) + EPSILON)
    return center * rate, rate


def norm_back(grad, unit, rate, gain):
    scaled = grad * gain
    return rate * (
        scaled
        - jnp.mean(scaled, -1, keepdims=True)
        - unit * jnp.mean(scaled * unit, -1, keepdims=True)
    )


def normal_parts(v):
    size = jnp.abs(v) * 0.7071067811865476
    bell = jnp.exp(-0.5 * v * v)
    t = 1.0 / (1.0 + 0.3275911 * size)
    tail = t * (
        0.254829592
        + t * (-0.284496736 + t * (1.421413741 + t * (-1.453152027 + t * 1.061405429)))
    )
    half = 0.5 * tail * bell
    return jnp.where(v < 0, half, 1.0 - half), 0.3989422804014327 * bell


def col_sum(values):
    return jnp.sum(values, 0, keepdims=True)


def pad_window(values):
    return jnp.concatenate([values, jnp.zeros((WPAD - ROWS, values.shape[1]), F32)], 0)


def layer_kernel(
    heads,
    count_ref,
    tok_ref,
    up_ref,
    place_ref,
    back_ref,
    hmask_ref,
    bias_ref,
    w_ref,
    vec_ref,
    out_ref,
    tg_ref,
    acts_ref,
    small_ref,
    pair_ref,
    qkv_s,
    prob_s,
    att_s,
    gatt_s,
    dqkv_s,
):
    image = pl.program_id(0)
    valid = (image < count_ref[0]).astype(F32)
    width = tok_ref.shape[2]
    scale = (width // heads) ** (-0.5)
    lanes = 128
    per = 4
    groups = heads // per

    @pl.when(image == 0)
    def _():
        small_ref[...] = jnp.zeros_like(small_ref)
        pair_ref[...] = jnp.zeros_like(pair_ref)

    def vec(row, count=1):
        return vec_ref[row : row + count, :].reshape(1, count * BLOCK)

    def note(row, values):
        small_ref[row : row + 1, :] += col_sum(values)

    def keep(block, values):
        acts_ref[0, :, block * BLOCK : (block + 1) * BLOCK] = values

    hmask = hmask_ref[...]
    hmask_f = hmask.astype(F32)

    def spread(part):
        return jnp.concatenate([part] * per, 0) * hmask

    def fold(full):
        full = full * hmask_f
        total = full[:WPAD]
        for h in range(1, per):
            total = total + full[h * WPAD : (h + 1) * WPAD]
        return total[:ROWS]

    inputs = nn(place_ref[...], tok_ref[0])
    unit_one, rate_one = normalize(inputs)
    normed = (unit_one * vec(0) + vec(1)).astype(BF16)
    keep(0, normed)
    for n in range(3):
        part = nn(normed, w_ref[n])
        if n == 0:
            part = (part + vec(2)) * scale
        if n == 2:
            part = part + vec(3)
        for w in range(4):
            qkv_s[w, :, n * BLOCK : (n + 1) * BLOCK] = pad_window(
                part[w * ROWS : (w + 1) * ROWS]
            ).astype(BF16)

    for w in range(4):
        for g in range(groups):
            at = slice(g * lanes, (g + 1) * lanes)
            wide = slice(g * per * WPAD, (g + 1) * per * WPAD)
            q = qkv_s[w, :, g * lanes : (g + 1) * lanes]
            k = qkv_s[w, :, BLOCK + g * lanes : BLOCK + (g + 1) * lanes]
            v = qkv_s[w, :, 2 * BLOCK + g * lanes : 2 * BLOCK + (g + 1) * lanes]
            scores = nt(k, spread(q)) + bias_ref[w, :, wide]
            raised = jnp.exp(scores - jnp.max(scores, 0, keepdims=True))
            probs = raised * (1.0 / jnp.sum(raised, 0, keepdims=True))
            prob_s[w, :, wide] = probs
            att_s[w * ROWS : (w + 1) * ROWS, at] = fold(tn(probs.astype(BF16), v))
    attended = att_s[...].astype(BF16)
    keep(4, attended)
    middle = inputs + (nn(attended, w_ref[3]) + vec(4))

    unit_two, rate_two = normalize(middle)
    normed_two = (unit_two * vec(5) + vec(6)).astype(BF16)
    keep(6, normed_two)
    upstream = nn(place_ref[...], up_ref[0]) * valid
    up_low = upstream.astype(BF16)
    keep(15, up_low)
    note(7, upstream)
    branch = None
    grad_two = None
    for c in range(4):
        pre = nn(normed_two, w_ref[4 + c]) + vec(8 + c)
        below, density = normal_parts(pre)
        act = (pre * below).astype(BF16)
        keep(11 + c, act)
        grad_pre = nt(up_low, w_ref[8 + c]) * (below + pre * density)
        note(8 + c, grad_pre)
        pre_low = grad_pre.astype(BF16)
        keep(7 + c, pre_low)
        first = nn(act, w_ref[8 + c])
        second = nt(pre_low, w_ref[4 + c])
        branch = first if c == 0 else branch + first
        grad_two = second if c == 0 else grad_two + second
    result = middle + (branch + vec(7))
    out_ref[0] = nn(back_ref[...], (result * valid).astype(BF16)).astype(BF16)
    note(5, grad_two * unit_two)
    note(6, grad_two)
    grad_middle = upstream + norm_back(grad_two, unit_two, rate_two, vec(5))
    note(4, grad_middle)
    proj_low = grad_middle.astype(BF16)
    keep(5, proj_low)
    grad_att = nt(proj_low, w_ref[3])
    for w in range(4):
        gatt_s[w] = pad_window(grad_att[w * ROWS : (w + 1) * ROWS]).astype(BF16)

    for w in range(4):
        rows = slice(w * ROWS, (w + 1) * ROWS)
        for g in range(groups):
            at = slice(g * lanes, (g + 1) * lanes)
            wide = slice(g * per * WPAD, (g + 1) * per * WPAD)
            q = qkv_s[w, :, g * lanes : (g + 1) * lanes]
            k = qkv_s[w, :, BLOCK + g * lanes : BLOCK + (g + 1) * lanes]
            v = qkv_s[w, :, 2 * BLOCK + g * lanes : 2 * BLOCK + (g + 1) * lanes]
            probs = prob_s[w, :, wide]
            spread_grad = spread(gatt_s[w, :, at])
            grad_v = nn(probs.astype(BF16), spread_grad)
            grad_probs = nt(v, spread_grad)
            weighted = probs * grad_probs
            grad_scores = weighted - probs * jnp.sum(weighted, 0, keepdims=True)
            pair_ref[:, wide] += grad_scores
            scores_low = grad_scores.astype(BF16)
            grad_k = nn(scores_low, spread(q))
            grad_q = fold(tn(scores_low, k)) * scale
            dqkv_s[rows, g * lanes : (g + 1) * lanes] = grad_q
            dqkv_s[rows, BLOCK + g * lanes : BLOCK + (g + 1) * lanes] = grad_k[:ROWS]
            dqkv_s[rows, 2 * BLOCK + g * lanes : 2 * BLOCK + (g + 1) * lanes] = grad_v[:ROWS]
    grad_one = None
    for n in range(3):
        part = dqkv_s[:, n * BLOCK : (n + 1) * BLOCK]
        if n == 0:
            note(2, part)
        if n == 2:
            note(3, part)
        low = part.astype(BF16)
        keep(1 + n, low)
        term = nt(low, w_ref[n])
        grad_one = term if n == 0 else grad_one + term
    note(0, grad_one * unit_one)
    note(1, grad_one)
    total = grad_middle + norm_back(grad_one, unit_one, rate_one, vec(0))
    high = total.astype(BF16)
    rest = (total - high.astype(F32)).astype(BF16)
    tg_ref[0] = nn(back_ref[...], high) + nn(back_ref[...], rest)


def run_layer(tokens, out_grad, count, bias, weights, vectors, heads):
    images, tokens_image, width = tokens.shape
    place = window_places()
    hmask = np.zeros((4 * WPAD, 128), np.float32)
    for h in range(4):
        hmask[h * WPAD : (h + 1) * WPAD, h * 32 : (h + 1) * 32] = 1
    hidden = weights.shape[0]

    def whole(array):
        zeros = (0,) * array.ndim
        return pl.BlockSpec(array.shape, lambda b: zeros, pipeline_mode=pl.Buffered(1))

    def per_image(*shape):
        return pl.BlockSpec((1,) + shape, lambda b: (b,) + (0,) * len(shape))

    consts = [jnp.asarray(place, BF16), jnp.asarray(place.T, BF16), jnp.asarray(hmask, BF16)]
    shared = consts + [bias, weights, vectors]
    rows = 4 * ROWS
    return pl.pallas_call(
        partial(layer_kernel, heads),
        grid=(images,),
        in_specs=[
            pl.BlockSpec(memory_space=pltpu.SMEM),
            per_image(tokens_image, width),
            per_image(tokens_image, width),
        ]
        + [whole(item) for item in shared],
        out_specs=[
            per_image(tokens_image, width),
            per_image(tokens_image, width),
            per_image(rows, 16 * BLOCK),
            pl.BlockSpec((12, BLOCK), lambda b: (0, 0)),
            pl.BlockSpec((WPAD, heads * WPAD), lambda b: (0, 0)),
        ],
        out_shape=[
            jax.ShapeDtypeStruct(tokens.shape, BF16),
            jax.ShapeDtypeStruct(tokens.shape, F32),
            jax.ShapeDtypeStruct((images, rows, 16 * BLOCK), BF16),
            jax.ShapeDtypeStruct((12, BLOCK), F32),
            jax.ShapeDtypeStruct((WPAD, heads * WPAD), F32),
        ],
        scratch_shapes=[
            pltpu.VMEM((4, WPAD, 3 * BLOCK), BF16),
            pltpu.VMEM((4, WPAD, heads * WPAD), F32),
            pltpu.VMEM((rows, BLOCK), F32),
            pltpu.VMEM((4, WPAD, BLOCK), BF16),
            pltpu.VMEM((rows, 3 * BLOCK), F32),
        ],
        compiler_params=pltpu.CompilerParams(vmem_limit_bytes=56 * 1024 * 1024),
        name="layer",
    )(count, tokens, out_grad, *shared)


def grads_kernel(left_ref, right_ref, out_ref):
    out_ref[0] = tn(left_ref[...], right_ref[...]).astype(BF16)


def run_grads(acts):
    acts = acts.reshape(-1, acts.shape[2])

    def left(m):
        return 0, jnp.where(m < 3, 0, jnp.where(m == 3, 4, jnp.where(m < 8, 6, m + 3)))

    def right(m):
        return 0, jnp.where(m < 3, m + 1, jnp.where(m == 3, 5, jnp.where(m < 8, m + 3, 15)))

    rows = acts.shape[0]
    return pl.pallas_call(
        grads_kernel,
        grid=(12,),
        in_specs=[pl.BlockSpec((rows, BLOCK), left), pl.BlockSpec((rows, BLOCK), right)],
        out_specs=pl.BlockSpec((1, BLOCK, BLOCK), lambda m: (m, 0, 0)),
        out_shape=jax.ShapeDtypeStruct((12, BLOCK, BLOCK), BF16),
        compiler_params=pltpu.CompilerParams(vmem_limit_bytes=40 * 1024 * 1024),
        name="weight_grads",
    )(acts, acts)


def pair_onehot(rel_index, rows):
    index = jnp.pad(
        rel_index.T, ((0, WPAD - WTOK), (0, WPAD - WTOK)), constant_values=-1
    ).reshape(-1)
    return (index[:, None] == jnp.arange(rows, dtype=jnp.int32)[None, :]).astype(BF16)


def score_bias(table, rel_index, shift_mask):
    rows, heads = table.shape
    bias = lax.dot_general(
        table, pair_onehot(rel_index, rows), (((0,), (1,)), ((), ())), preferred_element_type=F32
    )
    bias = bias.reshape(heads, WPAD, WPAD).transpose(1, 0, 2)
    mask = jnp.where(shift_mask == 1, 0.0, -100.0).astype(F32).transpose(0, 2, 1)
    mask = jnp.pad(mask, ((0, 0), (0, 0), (0, WPAD - WTOK)))
    mask = jnp.pad(mask, ((0, 0), (0, WPAD - WTOK), (0, 0)), constant_values=MASKED)
    return (bias[None] + mask[:, :, None, :]).reshape(4, WPAD, heads * WPAD)


def table_grad_of(pair, rel_index, rows):
    heads = pair.shape[1] // WPAD
    pair = pair.reshape(WPAD, heads, WPAD).transpose(1, 0, 2).reshape(heads, -1)
    high = pair.astype(BF16)
    rest = (pair - high.astype(F32)).astype(BF16)
    both = lax.dot_general(
        pair_onehot(rel_index, rows),
        jnp.concatenate([high, rest], 0),
        (((0,), (1,)), ((), ())),
        preferred_element_type=F32,
    )
    return both[:, :heads] + both[:, heads:]


MESH = pl.DeviceIdType.MESH
SIDE_CHIPS = 4


class Place:
    def __init__(self):
        replica = lax.axis_index("replica")
        self.hi = lax.axis_index("shard")
        self.core = lax.rem(replica, 2)
        self.at = {
            "x": self.hi * 2 + lax.rem(replica // 2, 2),
            "z": lax.rem(replica // 4, SIDE_CHIPS),
            "y": replica // 16,
        }
        self.lo = lax.rem(replica // 2, 2)

    def id_of(self, core=None, **at):
        place = dict(self.at, **at)
        core = self.core if core is None else core
        lo, hi = lax.rem(place["x"], 2), place["x"] // 2
        return (((place["y"] * SIDE_CHIPS + place["z"]) * 2 + lo) * 2 + core, hi)

    def other_core(self):
        return self.id_of(core=1 - self.core)

    def along(self, axis, step):
        return self.id_of(**{axis: lax.rem(self.at[axis] + step, SIDE_CHIPS)})


def greet(devices):
    barrier = pltpu.get_barrier_semaphore()
    for device in devices:
        pl.semaphore_signal(barrier, inc=1, device_id=device, device_id_type=MESH)
    pl.semaphore_wait(barrier, len(devices))


class Sender:
    def __init__(self, send_sem, recv_sem):
        self.send_sem, self.recv_sem, self.sent = send_sem, recv_sem, []

    def __call__(self, source, target, device):
        number = len(self.sent)
        copy = pltpu.make_async_remote_copy(
            src_ref=source,
            dst_ref=target,
            send_sem=self.send_sem.at[number],
            recv_sem=self.recv_sem.at[number],
            device_id=device,
            device_id_type=MESH,
        )
        copy.start()
        self.sent.append(copy)
        return copy

    def finish(self):
        for copy in self.sent:
            copy.wait_send()


def gather_kernel(qkv_ref, proj_ref, fc1_ref, fc2_ref, vec_ref, w_ref, v_ref, local_sem, send_sem, recv_sem):
    me = Place()
    hi, other = me.hi, 1 - me.hi
    local = []

    def load(source, target):
        copy = pltpu.make_async_copy(source, target, local_sem.at[len(local)])
        copy.start()
        local.append(copy)

    def rows_of(block):
        return pl.ds(block * 256, 256)

    for n in range(3):
        load(qkv_ref.at[:, pl.ds(n * BLOCK, BLOCK)], w_ref.at[hi, rows_of(n)])
    load(proj_ref, w_ref.at[hi, rows_of(3)])
    for m in range(4):
        for half in range(2):
            load(
                fc1_ref.at[:, pl.ds(half * 1024 + m * 256, 256)],
                w_ref.at[hi, rows_of(4 + m), pl.ds(half * 256, 256)],
            )
    load(fc2_ref, w_ref.at[hi, pl.ds(8 * 256, 1024)])
    load(vec_ref, v_ref.at[hi])

    facing = me.id_of(x=3 - me.at["x"])
    peers = [facing, me.other_core()]
    peers += [me.along(axis, step) for axis in ("y", "z") for step in (1, 2, 3)]
    greet(peers)
    send = Sender(send_sem, recv_sem)
    for copy in local:
        copy.wait()

    flows = []
    for flow, (first, second) in enumerate((("z", "y"), ("y", "z"))):
        base = flow * 1536 + me.core * 768
        outer = base + me.at[second] * 192
        flows.append((base, outer, outer + me.at[first] * 48, first, second))
    crossing = [
        send(w_ref.at[hi, pl.ds(piece, 48)], w_ref.at[hi, pl.ds(piece, 48)], facing)
        for _, _, piece, _, _ in flows
    ]
    vectors = send(v_ref.at[hi], v_ref.at[hi], facing)

    def share(start, size, axis):
        part = w_ref.at[other, pl.ds(start, size)]
        return [send(part, part, me.along(axis, step)) for step in (1, 2, 3)]

    firsts = []
    for copy, (base, outer, piece, first, second) in zip(crossing, flows):
        copy.wait_recv()
        firsts.append(share(piece, 48, first))
    seconds = []
    for copies, (base, outer, piece, first, second) in zip(firsts, flows):
        for copy in copies:
            copy.wait_recv()
        seconds.append(share(outer, 192, second))
    lasts = []
    for copies, (base, outer, piece, first, second) in zip(seconds, flows):
        for copy in copies:
            copy.wait_recv()
        part = w_ref.at[other, pl.ds(base, 768)]
        lasts.append(send(part, part, me.other_core()))
    for copy in lasts:
        copy.wait_recv()
    vectors.wait_recv()
    send.finish()


def gather_weights(qkv, proj, fc1, fc2, vectors):
    vmem = pl.BlockSpec(memory_space=pltpu.VMEM)
    return pl.pallas_call(
        gather_kernel,
        in_specs=[pl.BlockSpec(memory_space=pl.ANY)] * 5,
        out_specs=[vmem, vmem],
        out_shape=[
            jax.ShapeDtypeStruct((2, 12 * 256, BLOCK), BF16),
            jax.ShapeDtypeStruct((2,) + vectors.shape, BF16),
        ],
        scratch_shapes=[
            pltpu.SemaphoreType.DMA((14,)),
            pltpu.SemaphoreType.DMA((17,)),
            pltpu.SemaphoreType.DMA((17,)),
        ],
        compiler_params=pltpu.CompilerParams(
            collective_id=0, has_side_effects=True, vmem_limit_bytes=30 * 1024 * 1024
        ),
        name="gather_weights",
    )(qkv, proj, fc1, fc2, vectors)


ORDERS = (("x", "y", "z"), ("y", "z", "x"), ("z", "x", "y"))
STAGE_ROWS = (256, 64, 16)


def add_up(target, at, sources, rows, step):
    def body(i, carry):
        total = None
        for ref, first in sources:
            value = ref[pl.ds(pl.multiple_of(first + i * step, 16), step), :].astype(F32)
            total = value if total is None else total + value
        target[pl.ds(pl.multiple_of(at + i * step, 16), step), :] = total.astype(target.dtype)
        return carry

    lax.fori_loop(0, rows // step, body, 0)


def sum_kernel(
    g_ref, small_ref, f_ref, small_out, pair, sums, got_one, got_two, got_three, sum_two, sum_three,
    small_pair, small_x, small_y, small_z, send_sem, recv_sem,
):
    me = Place()
    peers = [me.other_core()]
    peers += [me.along(axis, step) for axis in ("x", "y", "z") for step in (1, 2, 3)]
    greet(peers)
    send = Sender(send_sem, recv_sem)
    mine, theirs = me.core, 1 - me.core

    pairs = [
        send(g_ref.at[pl.ds((4 * p + 2 * theirs) * 512, 1024)], pair.at[p], me.other_core())
        for p in range(3)
    ]
    small_pair[pl.ds(me.core, 1)] = small_ref[...][None]
    own = small_pair.at[me.core]
    small_copy = send(own, own, me.other_core())

    def exchange(stage, p, source):
        axis = ORDERS[p][stage]
        rows = STAGE_ROWS[stage]
        got = (got_one, got_two, got_three)[stage]
        copies = []
        for step in (1, 2, 3):
            chunk = lax.rem(me.at[axis] + step, SIDE_CHIPS)
            copies.append(
                send(source.at[pl.ds(chunk * rows, rows)], got.at[p, step - 1], me.along(axis, step))
            )
        return copies

    small_bufs = {"x": small_x, "y": small_y, "z": small_z}

    def small_exchange(axis, value):
        buf = small_bufs[axis]
        buf[pl.ds(me.at[axis], 1)] = value[None]
        part = buf.at[me.at[axis]]
        return [send(part, part, me.along(axis, step)) for step in (1, 2, 3)]

    def small_sum(axis, copies):
        for copy in copies:
            copy.wait_recv()
        buf = small_bufs[axis]
        return (buf[0] + buf[1]) + (buf[2] + buf[3])

    stage = []
    for p in range(3):
        pairs[p].wait_recv()
        size = (256, 32, 128)[p]
        own_rows = (4 * p + 2 * mine) * 512

        def body(i, carry, p=p, size=size, own_rows=own_rows):
            per = 256 // size
            block, rest = i // (2 * per), lax.rem(i, 2 * per)
            hi, sub = rest // per, lax.rem(rest, per)
            if p == 0:
                target = (hi * 2 + block) * 256
            else:
                target = (block * per + sub) * (2 * size) + hi * size
            from_row = (block * 2 + hi) * 256 + sub * size
            value = g_ref[pl.ds(pl.multiple_of(own_rows + from_row, 16), size), :].astype(F32)
            value += pair[p, pl.ds(pl.multiple_of(from_row, 16), size), :].astype(F32)
            sums[p, pl.ds(pl.multiple_of(target, 16), size), :] = value.astype(BF16)
            return carry

        lax.fori_loop(0, 1024 // size, body, 0)
        stage.append(exchange(0, p, sums.at[p]))
    small_copy.wait_recv()
    small_copies = small_exchange("x", small_pair[0] + small_pair[1])

    held = (sums, sum_two, sum_three)
    got = (got_one, got_two, got_three)
    strides = [{}, {}, {}]
    for p in range(3):
        extent, size = {"x": 2, "y": 4, "z": 4}, 16
        for axis in reversed(ORDERS[p]):
            strides[p][axis] = size
            size *= extent[axis]
    near = {"x": me.lo, "y": me.at["y"], "z": me.at["z"]}

    def start_of(p, smallest):
        start = me.core * 512
        for axis, size in strides[p].items():
            if size >= smallest:
                start = start + near[axis] * size
        return start

    for number in range(3):
        rows = STAGE_ROWS[number]
        following = []
        for p in range(3):
            for copy in stage[p]:
                copy.wait_recv()
            sources = [(held[number].at[p], me.at[ORDERS[p][number]] * rows)]
            sources += [(got[number].at[p, slot], 0) for slot in range(3)]
            step = min(rows, 64)
            if number < 2:
                add_up(held[number + 1].at[p], 0, sources, rows, step)
                following.append(exchange(number + 1, p, held[number + 1].at[p]))
            else:
                add_up(f_ref.at[p], start_of(p, 16), sources, rows, step)
        stage = following
        small_total = small_sum("xyz"[number], small_copies)
        if number < 2:
            small_copies = small_exchange("xyz"[number + 1], small_total)
        else:
            small_out[...] = small_total

    def share(p, axis):
        size = strides[p][axis]
        part = f_ref.at[p, pl.ds(start_of(p, size), size)]
        if axis == "x":
            x = me.at["x"]
            return [send(part, part, me.id_of(x=x + 1 - 2 * lax.rem(x, 2)))]
        return [send(part, part, me.along(axis, step)) for step in (1, 2, 3)]

    stage = [share(p, ORDERS[p][2]) for p in range(3)]
    for number in (1, 0, -1):
        following = []
        for p in range(3):
            for copy in stage[p]:
                copy.wait_recv()
            if number >= 0:
                following.append(share(p, ORDERS[p][number]))
            else:
                part = f_ref.at[p, pl.ds(me.core * 512, 512)]
                following.append([send(part, part, me.other_core())])
        stage = following
    for copies in stage:
        copies[0].wait_recv()
    send.finish()


def sum_grads(grads, small):
    vmem = pl.BlockSpec(memory_space=pltpu.VMEM)
    rows = small.shape[0]
    return pl.pallas_call(
        sum_kernel,
        in_specs=[vmem, vmem],
        out_specs=[vmem, vmem],
        out_shape=[
            jax.ShapeDtypeStruct((3, 1024, BLOCK), BF16),
            jax.ShapeDtypeStruct(small.shape, F32),
        ],
        scratch_shapes=[
            pltpu.VMEM((3, 1024, BLOCK), BF16),
            pltpu.VMEM((3, 1024, BLOCK), BF16),
            pltpu.VMEM((3, 3, 256, BLOCK), BF16),
            pltpu.VMEM((3, 3, 64, BLOCK), BF16),
            pltpu.VMEM((3, 3, 16, BLOCK), BF16),
            pltpu.VMEM((3, 256, BLOCK), BF16),
            pltpu.VMEM((3, 64, BLOCK), BF16),
            pltpu.VMEM((2, rows, BLOCK), F32),
            pltpu.VMEM((4, rows, BLOCK), F32),
            pltpu.VMEM((4, rows, BLOCK), F32),
            pltpu.VMEM((4, rows, BLOCK), F32),
            pltpu.SemaphoreType.DMA((64,)),
            pltpu.SemaphoreType.DMA((64,)),
        ],
        compiler_params=pltpu.CompilerParams(
            collective_id=1, has_side_effects=True, vmem_limit_bytes=40 * 1024 * 1024
        ),
        name="sum_grads",
    )(grads.reshape(12 * 512, BLOCK), small)


def hidden_order(values):
    return values.reshape(-1, 2, 4, 256).transpose(0, 2, 1, 3).reshape(-1, 2048)


def hidden_back(values):
    return values.reshape(-1, 4, 2, 256).transpose(0, 2, 1, 3).reshape(-1, 2048)


def local(
    tokens, image_counts, shift_mask, rel_index, norm1_gain, norm1_bias, qkv_weight, q_bias, v_bias,
    rel_table, proj_weight, proj_bias, norm2_gain, norm2_bias, fc1_weight, fc1_bias, fc2_weight,
    fc2_bias, out_grad,
):
    width = tokens.shape[2]
    table_rows, heads_here = rel_table.shape
    heads = heads_here * 2
    vectors = jnp.concatenate(
        [norm1_gain, norm1_bias, q_bias, v_bias, proj_bias, norm2_gain, norm2_bias, fc2_bias]
        + [fc1_bias, rel_table.T.reshape(-1)]
    )
    used = vectors.shape[0]
    vectors = jnp.pad(vectors, (0, 16 * BLOCK - used)).reshape(16, BLOCK)
    weights, both = gather_weights(qkv_weight, proj_weight, fc1_weight, fc2_weight, vectors)
    weights = weights.reshape(2, 12, 256, BLOCK).transpose(1, 0, 2, 3).reshape(12, BLOCK, BLOCK)
    flat = both.reshape(2, -1)
    eight = flat[:, :2048].reshape(2, 8, 256).transpose(1, 0, 2).reshape(8, BLOCK)
    hidden_bias = hidden_order(flat[:, 2048:3072].reshape(1, 2048)).reshape(4, BLOCK)
    table = flat[:, 3072:used].reshape(heads, table_rows).T
    vecs = jnp.concatenate([eight, hidden_bias]).astype(F32)
    bias = score_bias(table, rel_index, shift_mask)
    block_out, tokens_grad, acts, small, pair = run_layer(
        tokens, out_grad, image_counts, bias, weights, vecs, heads
    )
    grads = run_grads(acts)
    table_grad = table_grad_of(pair, rel_index, table_rows).T.reshape(-1)
    small = jnp.concatenate([small.reshape(-1), table_grad])
    small_used = small.shape[0]
    small = jnp.pad(small, (0, 24 * BLOCK - small_used)).reshape(24, BLOCK)
    grads, small = sum_grads(grads, small)
    grads = grads.reshape(12, 256, BLOCK).astype(F32)
    hi = lax.axis_index("shard")
    flat = small.reshape(-1)

    def half(values):
        size = values.shape[0] // 2
        return lax.dynamic_slice(values, (hi * size,), (size,))

    n1g, n1b, qb, vb, pb, n2g, n2b, f2b = (half(small[row]) for row in range(8))
    f1b = half(hidden_back(flat[8 * BLOCK : 12 * BLOCK].reshape(1, 2048))[0])
    table_out = half(flat[12 * BLOCK : small_used]).reshape(heads_here, table_rows).T
    qkv_out = grads[:3].transpose(1, 0, 2).reshape(256, 3 * BLOCK)
    fc1_out = hidden_back(grads[4:8].transpose(1, 0, 2).reshape(256, 4 * BLOCK))
    fc2_out = grads[8:].reshape(1024, BLOCK)
    return (
        block_out, tokens_grad, n1g, n1b, qkv_out, qb, vb, table_out, grads[3], pb, n2g, n2b,
        fc1_out, f1b, fc2_out, f2b,
    )


def solution(mesh):
    split = P(("replica", "shard"), None, None)
    vector, matrix, table = P("shard"), P("shard", None), P(None, "shard")
    return jax.shard_map(
        local,
        mesh=mesh,
        in_specs=(
            split, P(("replica", "shard")), P(), P(), vector, vector, matrix, vector, vector, table,
            matrix, vector, vector, vector, matrix, vector, matrix, vector, split,
        ),
        out_specs=(
            split, split, vector, vector, matrix, vector, vector, table, matrix, vector, vector,
            vector, matrix, vector, matrix, vector,
        ),
        check_vma=False,
    )
```

```python
from functools import partial

import jax
import jax.numpy as jnp
import numpy as np
from jax import lax
from jax.experimental import pallas as pl
from jax.experimental.pallas import tpu as pltpu
from jax.sharding import PartitionSpec as P

WIN = 7
SIDE = 14
SHIFT = 3
EPSILON = 1e-05
MASKED = -1e30
WTOK = WIN * WIN
ROWS = 56
WPAD = 64
BLOCK = 512
F32 = jnp.float32
BF16 = jnp.bfloat16


def nn(left, right):
    return jnp.dot(left, right, preferred_element_type=F32)


def nt(left, right):
    return lax.dot_general(left, right, (((1,), (1,)), ((), ())), preferred_element_type=F32)


def tn(left, right):
    return lax.dot_general(left, right, (((0,), (0,)), ((), ())), preferred_element_type=F32)


def window_places():
    place = np.zeros((4 * ROWS, SIDE * SIDE), np.float32)
    for window in range(4):
        for cell in range(WTOK):
            i = window // 2 * WIN + cell // WIN
            j = window % 2 * WIN + cell % WIN
            source = (i + SHIFT) % SIDE * SIDE + (j + SHIFT) % SIDE
            place[window * ROWS + cell, source] = 1
    return place


def normalize(values):
    center = values - jnp.mean(values, -1, keepdims=True)
    rate = lax.rsqrt(jnp.mean(center * center, -1, keepdims=True) + EPSILON)
    return center * rate, rate


def norm_back(grad, unit, rate, gain):
    scaled = grad * gain
    return rate * (
        scaled
        - jnp.mean(scaled, -1, keepdims=True)
        - unit * jnp.mean(scaled * unit, -1, keepdims=True)
    )


def normal_parts(v):
    size = jnp.abs(v) * 0.7071067811865476
    bell = jnp.exp(-0.5 * v * v)
    t = 1.0 / (1.0 + 0.3275911 * size)
    tail = t * (
        0.254829592
        + t * (-0.284496736 + t * (1.421413741 + t * (-1.453152027 + t * 1.061405429)))
    )
    half = 0.5 * tail * bell
    return jnp.where(v < 0, half, 1.0 - half), 0.3989422804014327 * bell


def col_sum(values):
    return jnp.sum(values, 0, keepdims=True)


def pad_window(values):
    return jnp.concatenate([values, jnp.zeros((WPAD - ROWS, values.shape[1]), F32)], 0)


def layer_kernel(
    heads,
    count_ref,
    tok_ref,
    up_ref,
    place_ref,
    back_ref,
    hmask_ref,
    bias_ref,
    rel_ref,
    vec_ref,
    w_any,
    out_ref,
    tg_ref,
    acts_ref,
    small_ref,
    w_ref,
    w_sem,
    pair_ref,
    fold_s,
    qkv_s,
    prob_s,
    att_s,
    gatt_s,
    dqkv_s,
):
    image = pl.program_id(0)
    valid = (image < count_ref[0]).astype(F32)
    width = tok_ref.shape[2]
    scale = (width // heads) ** (-0.5)
    lanes = 128
    per = 4
    groups = heads // per

    def weight_copies(blocks):
        return [
            pltpu.make_async_copy(
                w_any.at[half, pl.ds(n * 256, 256)],
                w_ref.at[n, pl.ds(half * 256, 256)],
                w_sem.at[n, half],
            )
            for n in blocks
            for half in range(2)
        ]

    @pl.when(image == 0)
    def _():
        for copy in weight_copies(range(12)):
            copy.start()
        small_ref[...] = jnp.zeros_like(small_ref)
        pair_ref[...] = jnp.zeros_like(pair_ref)
        for copy in weight_copies(range(3)):
            copy.wait()

    def vec(row):
        return jnp.concatenate([vec_ref[0, row : row + 1, :], vec_ref[1, row : row + 1, :]], 1)

    def note(row, values):
        small_ref[row : row + 1, :] += col_sum(values)

    def keep(block, values):
        acts_ref[0, :, block * BLOCK : (block + 1) * BLOCK] = values

    hmask = hmask_ref[...]
    hmask_f = hmask.astype(F32)

    def spread(part):
        return jnp.concatenate([part] * per, 0) * hmask

    def fold(full):
        full = full * hmask_f
        total = full[:WPAD]
        for h in range(1, per):
            total = total + full[h * WPAD : (h + 1) * WPAD]
        return total[:ROWS]

    inputs = nn(place_ref[...], tok_ref[0])
    unit_one, rate_one = normalize(inputs)
    normed = (unit_one * vec(0) + vec(1)).astype(BF16)
    keep(0, normed)
    for n in range(3):
        part = nn(normed, w_ref[n])
        if n == 0:
            part = (part + vec(2)) * scale
        if n == 2:
            part = part + vec(3)
        for w in range(4):
            qkv_s[w, :, n * BLOCK : (n + 1) * BLOCK] = pad_window(
                part[w * ROWS : (w + 1) * ROWS]
            ).astype(BF16)

    @pl.when(image == 0)
    def _():
        for copy in weight_copies(range(3, 12)):
            copy.wait()

    for w in range(4):
        for g in range(groups):
            at = slice(g * lanes, (g + 1) * lanes)
            wide = slice(g * per * WPAD, (g + 1) * per * WPAD)
            q = qkv_s[w, :, g * lanes : (g + 1) * lanes]
            k = qkv_s[w, :, BLOCK + g * lanes : BLOCK + (g + 1) * lanes]
            v = qkv_s[w, :, 2 * BLOCK + g * lanes : 2 * BLOCK + (g + 1) * lanes]
            scores = nt(k, spread(q)) + bias_ref[w, :, wide]
            raised = jnp.exp(scores - jnp.max(scores, 0, keepdims=True))
            probs = raised * (1.0 / jnp.sum(raised, 0, keepdims=True))
            prob_s[w, :, wide] = probs
            att_s[w * ROWS : (w + 1) * ROWS, at] = fold(tn(probs.astype(BF16), v))
    attended = att_s[...].astype(BF16)
    keep(4, attended)
    middle = inputs + (nn(attended, w_ref[3]) + vec(4))

    unit_two, rate_two = normalize(middle)
    normed_two = (unit_two * vec(5) + vec(6)).astype(BF16)
    keep(6, normed_two)
    upstream = nn(place_ref[...], up_ref[0]) * valid
    up_low = upstream.astype(BF16)
    keep(15, up_low)
    note(7, upstream)
    branch = None
    grad_two = None
    for c in range(4):
        pre = nn(normed_two, w_ref[4 + c]) + vec(8 + c)
        below, density = normal_parts(pre)
        act = (pre * below).astype(BF16)
        keep(11 + c, act)
        grad_pre = nt(up_low, w_ref[8 + c]) * (below + pre * density)
        note(8 + c, grad_pre)
        pre_low = grad_pre.astype(BF16)
        keep(7 + c, pre_low)
        first = nn(act, w_ref[8 + c])
        second = nt(pre_low, w_ref[4 + c])
        branch = first if c == 0 else branch + first
        grad_two = second if c == 0 else grad_two + second
    result = middle + (branch + vec(7))
    out_ref[0] = nn(back_ref[...], (result * valid).astype(BF16)).astype(BF16)
    note(5, grad_two * unit_two)
    note(6, grad_two)
    grad_middle = upstream + norm_back(grad_two, unit_two, rate_two, vec(5))
    note(4, grad_middle)
    proj_low = grad_middle.astype(BF16)
    keep(5, proj_low)
    grad_att = nt(proj_low, w_ref[3])
    for w in range(4):
        gatt_s[w] = pad_window(grad_att[w * ROWS : (w + 1) * ROWS]).astype(BF16)

    for w in range(4):
        rows = slice(w * ROWS, (w + 1) * ROWS)
        for g in range(groups):
            at = slice(g * lanes, (g + 1) * lanes)
            wide = slice(g * per * WPAD, (g + 1) * per * WPAD)
            q = qkv_s[w, :, g * lanes : (g + 1) * lanes]
            k = qkv_s[w, :, BLOCK + g * lanes : BLOCK + (g + 1) * lanes]
            v = qkv_s[w, :, 2 * BLOCK + g * lanes : 2 * BLOCK + (g + 1) * lanes]
            probs = prob_s[w, :, wide]
            spread_grad = spread(gatt_s[w, :, at])
            grad_v = nn(probs.astype(BF16), spread_grad)
            grad_probs = nt(v, spread_grad)
            weighted = probs * grad_probs
            grad_scores = weighted - probs * jnp.sum(weighted, 0, keepdims=True)
            pair_ref[:, wide] += grad_scores
            scores_low = grad_scores.astype(BF16)
            grad_k = nn(scores_low, spread(q))
            grad_q = fold(tn(scores_low, k)) * scale
            dqkv_s[rows, g * lanes : (g + 1) * lanes] = grad_q
            dqkv_s[rows, BLOCK + g * lanes : BLOCK + (g + 1) * lanes] = grad_k[:ROWS]
            dqkv_s[rows, 2 * BLOCK + g * lanes : 2 * BLOCK + (g + 1) * lanes] = grad_v[:ROWS]
    grad_one = None
    for n in range(3):
        part = dqkv_s[:, n * BLOCK : (n + 1) * BLOCK]
        if n == 0:
            note(2, part)
        if n == 2:
            note(3, part)
        low = part.astype(BF16)
        keep(1 + n, low)
        term = nt(low, w_ref[n])
        grad_one = term if n == 0 else grad_one + term
    note(0, grad_one * unit_one)
    note(1, grad_one)
    total = grad_middle + norm_back(grad_one, unit_one, rate_one, vec(0))
    high = total.astype(BF16)
    rest = (total - high.astype(F32)).astype(BF16)
    tg_ref[0] = nn(back_ref[...], high) + nn(back_ref[...], rest)

    @pl.when(image == pl.num_programs(0) - 1)
    def _():
        half = WPAD // 2
        for h in range(heads):
            at = slice(h * WPAD, (h + 1) * WPAD)
            both = jnp.concatenate([pair_ref[:half, at], pair_ref[half:, at]], 1)
            fold_s[pl.ds(h, half, stride=heads), :] = both

        def body(j, total):
            values = fold_s[pl.ds(pl.multiple_of(j * heads, heads), heads), :]
            high = values.astype(BF16)
            rest = (values - high.astype(F32)).astype(BF16)
            return total + nt(jnp.concatenate([high, rest], 0), pair_rows(rel_ref, j))

        total = lax.fori_loop(0, half, body, jnp.zeros((2 * heads, 256), F32))
        table = total[:heads] + total[heads:]
        small_ref[12 : 12 + heads // 2, :256] = table[: heads // 2]
        small_ref[12 : 12 + heads // 2, 256:] = table[heads // 2 :]


def pair_rows(rel_ref, j):
    rows = lax.broadcasted_iota(jnp.int32, (256, 128), 0).astype(F32)
    return jnp.where(rows == rel_ref[pl.ds(j, 1), :], 1.0, 0.0).astype(BF16)


def run_layer(tokens, out_grad, count, bias, rel_rows, weights, vectors, heads):
    images, tokens_image, width = tokens.shape
    place = window_places()
    hmask = np.zeros((4 * WPAD, 128), np.float32)
    for h in range(4):
        hmask[h * WPAD : (h + 1) * WPAD, h * 32 : (h + 1) * 32] = 1

    def whole(array):
        zeros = (0,) * array.ndim
        return pl.BlockSpec(array.shape, lambda b: zeros, pipeline_mode=pl.Buffered(1))

    def per_image(*shape):
        return pl.BlockSpec((1,) + shape, lambda b: (b,) + (0,) * len(shape))

    consts = [jnp.asarray(place, BF16), jnp.asarray(place.T, BF16), jnp.asarray(hmask, BF16)]
    shared = consts + [bias, rel_rows, vectors]
    rows = 4 * ROWS
    return pl.pallas_call(
        partial(layer_kernel, heads),
        grid=(images,),
        in_specs=[
            pl.BlockSpec(memory_space=pltpu.SMEM),
            per_image(tokens_image, width),
            per_image(tokens_image, width),
        ]
        + [whole(item) for item in shared]
        + [pl.BlockSpec(memory_space=pl.ANY)],
        out_specs=[
            per_image(tokens_image, width),
            per_image(tokens_image, width),
            per_image(rows, 16 * BLOCK),
            pl.BlockSpec((24, BLOCK), lambda b: (0, 0)),
        ],
        out_shape=[
            jax.ShapeDtypeStruct(tokens.shape, BF16),
            jax.ShapeDtypeStruct(tokens.shape, F32),
            jax.ShapeDtypeStruct((images, rows, 16 * BLOCK), BF16),
            jax.ShapeDtypeStruct((24, BLOCK), F32),
        ],
        scratch_shapes=[
            pltpu.VMEM((12, BLOCK, BLOCK), BF16),
            pltpu.SemaphoreType.DMA((12, 2)),
            pltpu.VMEM((WPAD, heads * WPAD), F32),
            pltpu.VMEM((heads * WPAD // 2, 128), F32),
            pltpu.VMEM((4, WPAD, 3 * BLOCK), BF16),
            pltpu.VMEM((4, WPAD, heads * WPAD), F32),
            pltpu.VMEM((rows, BLOCK), F32),
            pltpu.VMEM((4, WPAD, BLOCK), BF16),
            pltpu.VMEM((rows, 3 * BLOCK), F32),
        ],
        compiler_params=pltpu.CompilerParams(vmem_limit_bytes=56 * 1024 * 1024),
        name="layer",
    )(count, tokens, out_grad, *shared, weights)


def grads_kernel(left_ref, right_ref, out_ref):
    out_ref[0] = tn(left_ref[...], right_ref[...]).astype(BF16)


def run_grads(acts):
    acts = acts.reshape(-1, acts.shape[2])

    def left(m):
        return 0, jnp.where(m < 3, 0, jnp.where(m == 3, 4, jnp.where(m < 8, 6, m + 3)))

    def right(m):
        return 0, jnp.where(m < 3, m + 1, jnp.where(m == 3, 5, jnp.where(m < 8, m + 3, 15)))

    rows = acts.shape[0]
    return pl.pallas_call(
        grads_kernel,
        grid=(12,),
        in_specs=[pl.BlockSpec((rows, BLOCK), left), pl.BlockSpec((rows, BLOCK), right)],
        out_specs=pl.BlockSpec((1, BLOCK, BLOCK), lambda m: (m, 0, 0)),
        out_shape=jax.ShapeDtypeStruct((12, BLOCK, BLOCK), BF16),
        compiler_params=pltpu.CompilerParams(vmem_limit_bytes=40 * 1024 * 1024),
        name="weight_grads",
    )(acts, acts)


MESH = pl.DeviceIdType.MESH
SIDE_CHIPS = 4


class Place:
    def __init__(self):
        replica = lax.axis_index("replica")
        self.hi = lax.axis_index("shard")
        self.core = lax.rem(replica, 2)
        self.at = {
            "x": self.hi * 2 + lax.rem(replica // 2, 2),
            "z": lax.rem(replica // 4, SIDE_CHIPS),
            "y": replica // 16,
        }
        self.lo = lax.rem(replica // 2, 2)

    def id_of(self, core=None, **at):
        place = dict(self.at, **at)
        core = self.core if core is None else core
        lo, hi = lax.rem(place["x"], 2), place["x"] // 2
        return (((place["y"] * SIDE_CHIPS + place["z"]) * 2 + lo) * 2 + core, hi)

    def other_core(self):
        return self.id_of(core=1 - self.core)

    def along(self, axis, step):
        return self.id_of(**{axis: lax.rem(self.at[axis] + step, SIDE_CHIPS)})


def greet(devices):
    barrier = pltpu.get_barrier_semaphore()
    for device in devices:
        pl.semaphore_signal(barrier, inc=1, device_id=device, device_id_type=MESH)
    pl.semaphore_wait(barrier, len(devices))


class Sender:
    def __init__(self, send_sem, recv_sem):
        self.send_sem, self.recv_sem, self.sent = send_sem, recv_sem, []

    def __call__(self, source, target, device):
        number = len(self.sent)
        copy = pltpu.make_async_remote_copy(
            src_ref=source,
            dst_ref=target,
            send_sem=self.send_sem.at[number],
            recv_sem=self.recv_sem.at[number],
            device_id=device,
            device_id_type=MESH,
        )
        copy.start()
        self.sent.append(copy)
        return copy

    def finish(self):
        for copy in self.sent:
            copy.wait_send()


def gather_kernel(
    qkv_ref, proj_ref, fc1_ref, fc2_ref, *refs
):
    vec_refs = refs[:8]
    hidden_ref, table_ref, index_ref, mask_ref = refs[8:12]
    w_ref, v_ref, bias_ref, rel_ref = refs[12:16]
    square, square_mask, pairs, local_sem, send_sem, recv_sem = refs[16:]
    me = Place()
    hi, other = me.hi, 1 - me.hi
    local = []

    def load(source, target):
        copy = pltpu.make_async_copy(source, target, local_sem.at[len(local)])
        copy.start()
        local.append(copy)

    def rows_of(block):
        return pl.ds(block * 256, 256)

    for n in range(3):
        load(qkv_ref.at[:, pl.ds(n * BLOCK, BLOCK)], w_ref.at[hi, rows_of(n)])
    load(proj_ref, w_ref.at[hi, rows_of(3)])
    for m in range(4):
        for half in range(2):
            load(
                fc1_ref.at[:, pl.ds(half * 1024 + m * 256, 256)],
                w_ref.at[hi, rows_of(4 + m), pl.ds(half * 256, 256)],
            )
    load(fc2_ref, w_ref.at[hi, pl.ds(8 * 256, 1024)])

    facing = me.id_of(x=3 - me.at["x"])
    peers = [facing, me.other_core()]
    peers += [me.along(axis, step) for axis in ("y", "z") for step in (1, 2, 3)]
    greet(peers)
    send = Sender(send_sem, recv_sem)

    rows = [ref[...].astype(F32).reshape(1, 256) for ref in vec_refs]
    rows += [hidden_ref[pl.ds(m * 256, 256)].astype(F32).reshape(1, 256) for m in range(4)]
    rows.append(jnp.zeros((4, 256), F32))
    v_ref[pl.ds(hi, 1), 0:16] = jnp.concatenate(rows, 0)[None]
    table_rows, heads_here = table_ref.shape
    square[...] = jnp.zeros_like(square)
    square[0:table_rows, 0:heads_here] = table_ref[...].astype(F32)
    v_ref[pl.ds(hi, 1), 16:24] = jnp.concatenate([square[0:128].T, square[128:256].T], 1)[None, 0:8]
    for copy in local:
        copy.wait()

    flows = []
    for flow, (first, second) in enumerate((("z", "y"), ("y", "z"))):
        base = flow * 1536 + me.core * 768
        outer = base + me.at[second] * 192
        flows.append((base, outer, outer + me.at[first] * 48, first, second))
    crossing = [
        send(w_ref.at[hi, pl.ds(piece, 48)], w_ref.at[hi, pl.ds(piece, 48)], facing)
        for _, _, piece, _, _ in flows
    ]
    vectors = send(v_ref.at[hi], v_ref.at[hi], facing)

    def share(start, size, axis):
        part = w_ref.at[other, pl.ds(start, size)]
        return [send(part, part, me.along(axis, step)) for step in (1, 2, 3)]

    square[0:128] = jnp.full((128, 128), -1.0, F32)
    square[0:WTOK, 0:WTOK] = index_ref[...].astype(F32)
    turned = square[0:128].T
    half = WPAD // 2
    rel_ref[...] = jnp.concatenate([turned[:half, :WPAD], turned[half:WPAD, :WPAD]], 1)
    for w in range(4):
        below = lax.broadcasted_iota(jnp.int32, (WPAD, WPAD), 0)
        square_mask[w] = jnp.where(below < WTOK, 0.0, MASKED)
        square_mask[w, 0:WTOK, 0:WTOK] = jnp.where(mask_ref[w] == 1, 0.0, -100.0)

    firsts = []
    for copy, (base, outer, piece, first, second) in zip(crossing, flows):
        copy.wait_recv()
        firsts.append(share(piece, 48, first))
    vectors.wait_recv()
    table = jnp.concatenate([v_ref[0, 16:24], v_ref[1, 16:24]], 0).astype(BF16)
    heads = table.shape[0]

    def body(j, carry):
        pairs[pl.ds(pl.multiple_of(j * heads, heads), heads), :] = nn(table, pair_rows(rel_ref, j))
        return carry

    lax.fori_loop(0, half, body, 0)
    for h in range(heads):
        at = slice(h * WPAD, (h + 1) * WPAD)
        both = pairs[pl.ds(h, half, stride=heads), :]
        for w in range(4):
            bias_ref[w, :half, at] = both[:, :WPAD] + square_mask[w, :half]
            bias_ref[w, half:, at] = both[:, WPAD:] + square_mask[w, half:]

    seconds = []
    for copies, (base, outer, piece, first, second) in zip(firsts, flows):
        for copy in copies:
            copy.wait_recv()
        seconds.append(share(outer, 192, second))
    lasts = []
    for copies, (base, outer, piece, first, second) in zip(seconds, flows):
        for copy in copies:
            copy.wait_recv()
        part = w_ref.at[other, pl.ds(base, 768)]
        lasts.append(send(part, part, me.other_core()))
    for copy in lasts:
        copy.wait_recv()
    send.finish()


def gather_weights(matrices, vectors, hidden_bias, table, rel_index, shift_mask):
    vmem = pl.BlockSpec(memory_space=pltpu.VMEM)
    heads = table.shape[1] * 2
    small = vectors + [hidden_bias, table, rel_index, shift_mask]
    return pl.pallas_call(
        gather_kernel,
        in_specs=[pl.BlockSpec(memory_space=pl.ANY)] * 4 + [vmem] * len(small),
        out_specs=[vmem] * 4,
        out_shape=[
            jax.ShapeDtypeStruct((2, 12 * 256, BLOCK), BF16),
            jax.ShapeDtypeStruct((2, 24, 256), F32),
            jax.ShapeDtypeStruct((4, WPAD, heads * WPAD), F32),
            jax.ShapeDtypeStruct((WPAD // 2, 2 * WPAD), F32),
        ],
        scratch_shapes=[
            pltpu.VMEM((256, 128), F32),
            pltpu.VMEM((4, WPAD, WPAD), F32),
            pltpu.VMEM((heads * WPAD // 2, 2 * WPAD), F32),
            pltpu.SemaphoreType.DMA((14,)),
            pltpu.SemaphoreType.DMA((17,)),
            pltpu.SemaphoreType.DMA((17,)),
        ],
        compiler_params=pltpu.CompilerParams(
            collective_id=0, has_side_effects=True, vmem_limit_bytes=30 * 1024 * 1024
        ),
        name="gather_weights",
    )(*matrices, *small)


ORDERS = (("x", "y", "z"), ("y", "z", "x"), ("z", "x", "y"))
STAGE_ROWS = (256, 64, 16)


def add_up(target, at, sources, rows, step):
    def body(i, carry):
        total = None
        for ref, first in sources:
            value = ref[pl.ds(pl.multiple_of(first + i * step, 16), step), :].astype(F32)
            total = value if total is None else total + value
        target[pl.ds(pl.multiple_of(at + i * step, 16), step), :] = total.astype(target.dtype)
        return carry

    lax.fori_loop(0, rows // step, body, 0)


def sum_kernel(
    g_ref, small_ref, f_ref, small_out, pair, sums, got_one, got_two, got_three, sum_two, sum_three,
    small_pair, small_x, small_y, small_z, send_sem, recv_sem,
):
    me = Place()
    peers = [me.other_core()]
    peers += [me.along(axis, step) for axis in ("x", "y", "z") for step in (1, 2, 3)]
    greet(peers)
    send = Sender(send_sem, recv_sem)
    mine, theirs = me.core, 1 - me.core

    pairs = [
        send(g_ref.at[pl.ds((4 * p + 2 * theirs) * 512, 1024)], pair.at[p], me.other_core())
        for p in range(3)
    ]
    small_pair[pl.ds(me.core, 1)] = small_ref[...][None]
    own = small_pair.at[me.core]
    small_copy = send(own, own, me.other_core())

    def exchange(stage, p, source):
        axis = ORDERS[p][stage]
        rows = STAGE_ROWS[stage]
        got = (got_one, got_two, got_three)[stage]
        copies = []
        for step in (1, 2, 3):
            chunk = lax.rem(me.at[axis] + step, SIDE_CHIPS)
            copies.append(
                send(source.at[pl.ds(chunk * rows, rows)], got.at[p, step - 1], me.along(axis, step))
            )
        return copies

    small_bufs = {"x": small_x, "y": small_y, "z": small_z}

    def small_exchange(axis, value):
        buf = small_bufs[axis]
        buf[pl.ds(me.at[axis], 1)] = value[None]
        part = buf.at[me.at[axis]]
        return [send(part, part, me.along(axis, step)) for step in (1, 2, 3)]

    def small_sum(axis, copies):
        for copy in copies:
            copy.wait_recv()
        buf = small_bufs[axis]
        return (buf[0] + buf[1]) + (buf[2] + buf[3])

    stage = []
    for p in range(3):
        pairs[p].wait_recv()
        size = (256, 32, 128)[p]
        own_rows = (4 * p + 2 * mine) * 512

        def body(i, carry, p=p, size=size, own_rows=own_rows):
            per = 256 // size
            block, rest = i // (2 * per), lax.rem(i, 2 * per)
            hi, sub = rest // per, lax.rem(rest, per)
            if p == 0:
                target = (hi * 2 + block) * 256
            else:
                target = (block * per + sub) * (2 * size) + hi * size
            from_row = (block * 2 + hi) * 256 + sub * size
            value = g_ref[pl.ds(pl.multiple_of(own_rows + from_row, 16), size), :].astype(F32)
            value += pair[p, pl.ds(pl.multiple_of(from_row, 16), size), :].astype(F32)
            sums[p, pl.ds(pl.multiple_of(target, 16), size), :] = value.astype(BF16)
            return carry

        lax.fori_loop(0, 1024 // size, body, 0)
        stage.append(exchange(0, p, sums.at[p]))
    small_copy.wait_recv()
    small_copies = small_exchange("x", small_pair[0] + small_pair[1])

    held = (sums, sum_two, sum_three)
    got = (got_one, got_two, got_three)
    strides = [{}, {}, {}]
    for p in range(3):
        extent, size = {"x": 2, "y": 4, "z": 4}, 16
        for axis in reversed(ORDERS[p]):
            strides[p][axis] = size
            size *= extent[axis]
    near = {"x": me.lo, "y": me.at["y"], "z": me.at["z"]}

    def start_of(p, smallest):
        start = me.core * 512
        for axis, size in strides[p].items():
            if size >= smallest:
                start = start + near[axis] * size
        return start

    for number in range(3):
        rows = STAGE_ROWS[number]
        following = []
        for p in range(3):
            for copy in stage[p]:
                copy.wait_recv()
            sources = [(held[number].at[p], me.at[ORDERS[p][number]] * rows)]
            sources += [(got[number].at[p, slot], 0) for slot in range(3)]
            step = min(rows, 64)
            if number < 2:
                add_up(held[number + 1].at[p], 0, sources, rows, step)
                following.append(exchange(number + 1, p, held[number + 1].at[p]))
            else:
                add_up(f_ref.at[p], start_of(p, 16), sources, rows, step)
        stage = following
        small_total = small_sum("xyz"[number], small_copies)
        if number < 2:
            small_copies = small_exchange("xyz"[number + 1], small_total)
        else:
            small_out[...] = jnp.where(me.hi == 0, small_total[:, :256], small_total[:, 256:])

    def share(p, axis):
        size = strides[p][axis]
        part = f_ref.at[p, pl.ds(start_of(p, size), size)]
        if axis == "x":
            x = me.at["x"]
            return [send(part, part, me.id_of(x=x + 1 - 2 * lax.rem(x, 2)))]
        return [send(part, part, me.along(axis, step)) for step in (1, 2, 3)]

    stage = [share(p, ORDERS[p][2]) for p in range(3)]
    for number in (1, 0, -1):
        following = []
        for p in range(3):
            for copy in stage[p]:
                copy.wait_recv()
            if number >= 0:
                following.append(share(p, ORDERS[p][number]))
            else:
                part = f_ref.at[p, pl.ds(me.core * 512, 512)]
                following.append([send(part, part, me.other_core())])
        stage = following
    for copies in stage:
        copies[0].wait_recv()
    send.finish()


def sum_grads(grads, small):
    vmem = pl.BlockSpec(memory_space=pltpu.VMEM)
    rows = small.shape[0]
    return pl.pallas_call(
        sum_kernel,
        in_specs=[vmem, vmem],
        out_specs=[vmem, vmem],
        out_shape=[
            jax.ShapeDtypeStruct((3, 1024, BLOCK), BF16),
            jax.ShapeDtypeStruct((rows, 256), F32),
        ],
        scratch_shapes=[
            pltpu.VMEM((3, 1024, BLOCK), BF16),
            pltpu.VMEM((3, 1024, BLOCK), BF16),
            pltpu.VMEM((3, 3, 256, BLOCK), BF16),
            pltpu.VMEM((3, 3, 64, BLOCK), BF16),
            pltpu.VMEM((3, 3, 16, BLOCK), BF16),
            pltpu.VMEM((3, 256, BLOCK), BF16),
            pltpu.VMEM((3, 64, BLOCK), BF16),
            pltpu.VMEM((2, rows, BLOCK), F32),
            pltpu.VMEM((4, rows, BLOCK), F32),
            pltpu.VMEM((4, rows, BLOCK), F32),
            pltpu.VMEM((4, rows, BLOCK), F32),
            pltpu.SemaphoreType.DMA((64,)),
            pltpu.SemaphoreType.DMA((64,)),
        ],
        compiler_params=pltpu.CompilerParams(
            collective_id=1, has_side_effects=True, vmem_limit_bytes=40 * 1024 * 1024
        ),
        name="sum_grads",
    )(grads.reshape(12 * 512, BLOCK), small)


def finish_kernel(
    f_ref, small_ref, n1g, n1b, qkv, qb, vb, table, proj, pb, n2g, n2b, fc1, f1b, fc2, f2b, wide, turn, sem
):
    copies = []

    def store(source, target):
        copy = pltpu.make_async_copy(source, target, sem.at[len(copies)])
        copy.start()
        copies.append(copy)

    for n in range(12):
        wide[n] = f_ref[n].astype(F32)
        if n < 3:
            store(wide.at[n], qkv.at[:, pl.ds(n * BLOCK, BLOCK)])
        elif n == 3:
            store(wide.at[n], proj)
        elif n < 8:
            for half in range(2):
                store(
                    wide.at[n, :, pl.ds(half * 256, 256)],
                    fc1.at[:, pl.ds(half * 1024 + (n - 4) * 256, 256)],
                )
        else:
            store(wide.at[n], fc2.at[pl.ds((n - 8) * 256, 256)])
    for row, ref in enumerate((n1g, n1b, qb, vb, pb, n2g, n2b, f2b)):
        ref[...] = small_ref[row : row + 1, :].reshape(256)
    for m in range(4):
        f1b[pl.ds(m * 256, 256)] = small_ref[8 + m : 9 + m, :].reshape(256)
    turn[...] = jnp.zeros_like(turn)
    turn[0:8, :] = small_ref[12:20, :]
    table[...] = jnp.concatenate([turn[:, 0:128].T, turn[:, 128:256].T], 0)[
        : table.shape[0], : table.shape[1]
    ]
    for copy in copies:
        copy.wait()


def finish(grads, small, table_rows, heads_here):
    vmem = pl.BlockSpec(memory_space=pltpu.VMEM)
    far = pl.BlockSpec(memory_space=pl.ANY)
    vector, hidden = ((256,), vmem), ((1024,), vmem)
    outs = [
        vector, vector, ((256, 3 * BLOCK), far), vector, vector, ((table_rows, heads_here), vmem),
        ((256, BLOCK), far), vector, vector, vector, ((256, 4 * BLOCK), far), hidden,
        ((1024, BLOCK), far), vector,
    ]
    return pl.pallas_call(
        finish_kernel,
        in_specs=[vmem, vmem],
        out_specs=[spec for _, spec in outs],
        out_shape=[jax.ShapeDtypeStruct(shape, F32) for shape, _ in outs],
        scratch_shapes=[
            pltpu.VMEM((12, 256, BLOCK), F32),
            pltpu.VMEM((128, 256), F32),
            pltpu.SemaphoreType.DMA((16,)),
        ],
        compiler_params=pltpu.CompilerParams(vmem_limit_bytes=30 * 1024 * 1024),
        name="finish",
    )(grads, small)


def local(
    tokens, image_counts, shift_mask, rel_index, norm1_gain, norm1_bias, qkv_weight, q_bias, v_bias,
    rel_table, proj_weight, proj_bias, norm2_gain, norm2_bias, fc1_weight, fc1_bias, fc2_weight,
    fc2_bias, out_grad,
):
    table_rows, heads_here = rel_table.shape
    weights, vecs, bias, rel_rows = gather_weights(
        [qkv_weight, proj_weight, fc1_weight, fc2_weight],
        [norm1_gain, norm1_bias, q_bias, v_bias, proj_bias, norm2_gain, norm2_bias, fc2_bias],
        fc1_bias, rel_table, rel_index, shift_mask,
    )
    block_out, tokens_grad, acts, small = run_layer(
        tokens, out_grad, image_counts, bias, rel_rows, weights, vecs, heads_here * 2
    )
    grads, small = sum_grads(run_grads(acts), small)
    outs = finish(grads.reshape(12, 256, BLOCK), small, table_rows, heads_here)
    return (block_out, tokens_grad, *outs)


def solution(mesh):
    split = P(("replica", "shard"), None, None)
    vector, matrix, table = P("shard"), P("shard", None), P(None, "shard")
    return jax.shard_map(
        local,
        mesh=mesh,
        in_specs=(
            split, P(("replica", "shard")), P(), P(), vector, vector, matrix, vector, vector, table,
            matrix, vector, vector, vector, matrix, vector, matrix, vector, split,
        ),
        out_specs=(
            split, split, vector, vector, matrix, vector, vector, table, matrix, vector, vector,
            vector, matrix, vector, matrix, vector,
        ),
        check_vma=False,
    )
```

```python
from functools import partial

import jax
import jax.numpy as jnp
from jax import lax
from jax.experimental import pallas as pl
from jax.experimental.pallas import tpu as pltpu
from jax.sharding import PartitionSpec as P

WIN = 7
SIDE = 14
SHIFT = 3
EPSILON = 1e-05
MASKED = -1e30
WTOK = WIN * WIN
ROWS = 56
WPAD = 64
BLOCK = 512
F32 = jnp.float32
BF16 = jnp.bfloat16


def nn(left, right):
    return jnp.dot(left, right, preferred_element_type=F32)


def nt(left, right):
    return lax.dot_general(left, right, (((1,), (1,)), ((), ())), preferred_element_type=F32)


def tn(left, right):
    return lax.dot_general(left, right, (((0,), (0,)), ((), ())), preferred_element_type=F32)


def normalize(values):
    center = values - jnp.mean(values, -1, keepdims=True)
    rate = lax.rsqrt(jnp.mean(center * center, -1, keepdims=True) + EPSILON)
    return center * rate, rate


def norm_back(grad, unit, rate, gain):
    scaled = grad * gain
    return rate * (
        scaled
        - jnp.mean(scaled, -1, keepdims=True)
        - unit * jnp.mean(scaled * unit, -1, keepdims=True)
    )


def normal_parts(v):
    size = jnp.abs(v) * 0.7071067811865476
    bell = jnp.exp(-0.5 * v * v)
    t = 1.0 / (1.0 + 0.3275911 * size)
    tail = t * (
        0.254829592
        + t * (-0.284496736 + t * (1.421413741 + t * (-1.453152027 + t * 1.061405429)))
    )
    half = 0.5 * tail * bell
    return jnp.where(v < 0, half, 1.0 - half), 0.3989422804014327 * bell


def col_sum(values):
    return jnp.sum(values, 0, keepdims=True)


MESH = pl.DeviceIdType.MESH
SIDE_CHIPS = 4


class Place:
    def __init__(self):
        replica = lax.axis_index("replica")
        self.hi = lax.axis_index("shard")
        self.core = lax.rem(replica, 2)
        self.at = {
            "x": self.hi * 2 + lax.rem(replica // 2, 2),
            "z": lax.rem(replica // 4, SIDE_CHIPS),
            "y": replica // 16,
        }
        self.lo = lax.rem(replica // 2, 2)

    def id_of(self, core=None, **at):
        place = dict(self.at, **at)
        core = self.core if core is None else core
        lo, hi = lax.rem(place["x"], 2), place["x"] // 2
        return (((place["y"] * SIDE_CHIPS + place["z"]) * 2 + lo) * 2 + core, hi)

    def other_core(self):
        return self.id_of(core=1 - self.core)

    def along(self, axis, step):
        return self.id_of(**{axis: lax.rem(self.at[axis] + step, SIDE_CHIPS)})


def greet(devices):
    barrier = pltpu.get_barrier_semaphore()
    for device in devices:
        pl.semaphore_signal(barrier, inc=1, device_id=device, device_id_type=MESH)
    pl.semaphore_wait(barrier, len(devices))


def pad_window(values):
    return jnp.concatenate([values, jnp.zeros((WPAD - ROWS, values.shape[1]), F32)], 0)


def source_of(row):
    window = jnp.floor((row + 0.5) / ROWS)
    cell = row - window * ROWS
    across = jnp.floor((window + 0.5) / 2)
    down = jnp.floor((cell + 0.5) / WIN)
    i = across * WIN + down + SHIFT
    j = (window - 2 * across) * WIN + (cell - down * WIN) + SHIFT
    i = jnp.where(i >= SIDE, i - SIDE, i)
    j = jnp.where(j >= SIDE, j - SIDE, j)
    return jnp.where(cell < WTOK, i * SIDE + j, -1.0)


def iota(shape, axis):
    return lax.broadcasted_iota(jnp.int32, shape, axis).astype(F32)


def place_matrix():
    rows, tokens = 4 * ROWS, SIDE * SIDE
    return jnp.where(source_of(iota((rows, tokens), 0)) == iota((rows, tokens), 1), 1.0, 0.0)


def back_matrix():
    rows, tokens = 4 * ROWS, SIDE * SIDE
    return jnp.where(source_of(iota((tokens, rows), 1)) == iota((tokens, rows), 0), 1.0, 0.0)


def head_mask():
    shape = (4 * WPAD, 128)
    row, lane = iota(shape, 0), iota(shape, 1)
    return jnp.where(jnp.floor((row + 0.5) / WPAD) == jnp.floor((lane + 0.5) / 32), 1.0, 0.0)


def pair_rows(rel_ref, j):
    return jnp.where(iota((256, 128), 0) == rel_ref[pl.ds(j, 1), :], 1.0, 0.0).astype(BF16)


def spread(part, hmask):
    return jnp.concatenate([part] * 4, 0) * hmask


def fold(full, hmask):
    full = full * hmask.astype(F32)
    total = full[:WPAD]
    for h in range(1, 4):
        total = total + full[h * WPAD : (h + 1) * WPAD]
    return total[:ROWS]


def both_halves(vec_ref, row):
    return jnp.concatenate([vec_ref[0, row : row + 1, :], vec_ref[1, row : row + 1, :]], 1)


def remote(source, target, send_sem, recv_sem, number, device):
    return pltpu.make_async_remote_copy(
        src_ref=source,
        dst_ref=target,
        send_sem=send_sem.at[number],
        recv_sem=recv_sem.at[number],
        device_id=device,
        device_id_type=MESH,
    )


def start(copies):
    for copy in copies:
        copy.start()


def arrived(copies):
    for copy in copies:
        copy.wait_recv()


def sent(copies):
    for copy in copies:
        copy.wait_send()


class Gather:
    SEMAPHORES = 33

    def __init__(self, me, w_ref, v_ref, send_sem, recv_sem):
        self.me, self.w, self.v = me, w_ref, v_ref
        self.sems = (send_sem, recv_sem)

    def flows(self, group):
        count = 1 + group
        for flow, (first, second) in enumerate((("z", "y"), ("y", "z"))):
            block = 4 * group + 2 * count * flow + self.me.core * count
            yield 16 * group + 8 * flow, pl.ds(block, count), first, second

    def copy(self, number, part, device):
        return remote(part, part, *self.sems, number, device)

    def facing(self):
        return self.me.id_of(x=3 - self.me.at["x"])

    def cross(self, group):
        me = self.me
        return [
            self.copy(
                number,
                self.w.at[blocks, me.hi, pl.ds(me.at[second] * 64 + me.at[first] * 16, 16)],
                self.facing(),
            )
            for number, blocks, first, second in self.flows(group)
        ]

    def vectors(self):
        return [self.copy(32, self.v.at[self.me.hi], self.facing())]

    def first(self, group):
        me = self.me
        return [
            self.copy(
                number + step,
                self.w.at[blocks, 1 - me.hi, pl.ds(me.at[second] * 64 + me.at[first] * 16, 16)],
                me.along(first, step),
            )
            for number, blocks, first, second in self.flows(group)
            for step in (1, 2, 3)
        ]

    def second(self, group):
        me = self.me
        return [
            self.copy(
                number + 3 + step,
                self.w.at[blocks, 1 - me.hi, pl.ds(me.at[second] * 64, 64)],
                me.along(second, step),
            )
            for number, blocks, first, second in self.flows(group)
            for step in (1, 2, 3)
        ]

    def last(self, group):
        return [
            self.copy(number + 7, self.w.at[blocks, 1 - self.me.hi], self.me.other_core())
            for number, blocks, _, _ in self.flows(group)
        ]


def front_kernel(
    images,
    count_ref,
    qkv_w, proj_w, fc1_w, fc2_w, n1g, n1b, qb, vb, pb, n2g, n2b, f2b, f1b, table_w, index_w, mask_w,
    tok_ref, up_ref,
    qkv_ref, prob_ref, att_ref, out_ref, gmid_ref, fc_ref, small_ref, vec_out, rel_ref, low_ref,
    vec_ref, w_ref, acts, bias_ref, place_ref, back_ref, hmask_ref, att_s,
    v0, v1, v2, v3, v4, v5, v6, v7, v8, table_v, index_v, mask_v, square, square_mask, pairs,
    w_sem, in_sem, low_sem, send_sem, recv_sem,
):
    step = pl.program_id(0)
    me = Place()
    hi = me.hi
    gather = Gather(me, w_ref, vec_ref, send_sem, recv_sem)
    heads = table_w.shape[1] * 2
    scale = (tok_ref.shape[2] // heads) ** (-0.5)

    def own_weights(group):
        pairs = []
        if group == 0:
            for n in range(3):
                pairs.append((qkv_w.at[:, pl.ds(n * BLOCK, BLOCK)], w_ref.at[n, hi]))
            pairs.append((proj_w, w_ref.at[3, hi]))
        else:
            for m in range(4):
                for half in range(2):
                    pairs.append(
                        (
                            fc1_w.at[:, pl.ds(half * 1024 + m * 256, 256)],
                            w_ref.at[4 + m, hi, :, pl.ds(half * 256, 256)],
                        )
                    )
                pairs.append((fc2_w.at[pl.ds(m * 256, 256)], w_ref.at[8 + m, hi]))
        return [
            pltpu.make_async_copy(source, target, w_sem.at[4 * group + i])
            for i, (source, target) in enumerate(pairs)
        ]

    def own_small():
        sources = (n1g, n1b, qb, vb, pb, n2g, n2b, f2b, f1b, table_w, index_w, mask_w)
        targets = (v0, v1, v2, v3, v4, v5, v6, v7, v8, table_v, index_v, mask_v)
        return [
            pltpu.make_async_copy(source, target, in_sem.at[i])
            for i, (source, target) in enumerate(zip(sources, targets))
        ]

    def low_copy():
        return pltpu.make_async_copy(w_ref.at[pl.ds(0, 4)], low_ref, low_sem.at[0])

    def weight(n):
        return w_ref[n].reshape(BLOCK, BLOCK)

    def vec(row):
        return both_halves(vec_ref, row)

    def note(row, values):
        small_ref[row : row + 1, :] += col_sum(values)

    @pl.when(step == 0)
    def _():
        small_copies = own_small()
        start(own_weights(0))
        start(small_copies)
        start(own_weights(1))
        peers = [gather.facing(), me.other_core()]
        peers += [me.along(axis, s) for axis in ("y", "z") for s in (1, 2, 3)]
        greet(peers)
        for copy in own_weights(0):
            copy.wait()
        start(gather.cross(0))
        for copy in small_copies:
            copy.wait()
        rows = [ref[...].astype(F32).reshape(1, 256) for ref in (v0, v1, v2, v3, v4, v5, v6, v7)]
        rows += [v8[pl.ds(m * 256, 256)].astype(F32).reshape(1, 256) for m in range(4)]
        rows.append(jnp.zeros((4, 256), F32))
        vec_ref[pl.ds(hi, 1), 0:16] = jnp.concatenate(rows, 0)[None]
        table_rows, heads_here = table_v.shape
        square[...] = jnp.zeros_like(square)
        square[0:table_rows, 0:heads_here] = table_v[...].astype(F32)
        vec_ref[pl.ds(hi, 1), 16:24] = jnp.concatenate(
            [square[0:128].T, square[128:256].T], 1
        )[None, 0:8]
        start(gather.vectors())
        for copy in own_weights(1):
            copy.wait()
        arrived(gather.cross(0))
        start(gather.first(0))
        start(gather.cross(1))
        square[0:128] = jnp.full((128, 128), -1.0, F32)
        square[0:WTOK, 0:WTOK] = index_v[...].astype(F32)
        turned = square[0:128].T
        half = WPAD // 2
        rel_ref[...] = jnp.concatenate([turned[:half, :WPAD], turned[half:WPAD, :WPAD]], 1)
        for w in range(4):
            square_mask[w] = jnp.where(iota((WPAD, WPAD), 0) < WTOK, 0.0, MASKED)
            square_mask[w, 0:WTOK, 0:WTOK] = jnp.where(mask_v[w] == 1, 0.0, -100.0)
        place_ref[...] = place_matrix().astype(BF16)
        back_ref[...] = back_matrix().astype(BF16)
        hmask_ref[...] = head_mask().astype(BF16)
        small_ref[...] = jnp.zeros_like(small_ref)
        arrived(gather.first(0))
        start(gather.second(0))
        arrived(gather.vectors())
        table = jnp.concatenate([vec_ref[0, 16:24], vec_ref[1, 16:24]], 0).astype(BF16)

        def body(j, carry):
            pairs[pl.ds(pl.multiple_of(j * heads, heads), heads), :] = nn(table, pair_rows(rel_ref, j))
            return carry

        lax.fori_loop(0, half, body, 0)
        for h in range(heads):
            at = slice(h * WPAD, (h + 1) * WPAD)
            both = pairs[pl.ds(h, half, stride=heads), :]
            for w in range(4):
                bias_ref[w, :half, at] = both[:, :WPAD] + square_mask[w, :half]
                bias_ref[w, half:, at] = both[:, WPAD:] + square_mask[w, half:]
        arrived(gather.second(0))
        start(gather.last(0))
        arrived(gather.cross(1))
        start(gather.first(1))
        vec_out[...] = vec_ref[...]
        arrived(gather.last(0))
        low_copy().start()

    @pl.when(step == 1)
    def _():
        arrived(gather.first(1))
        start(gather.second(1))

    @pl.when(step == SECOND_STEP)
    def _():
        arrived(gather.second(1))
        start(gather.last(1))

    @pl.when(step == images)
    def _():
        arrived(gather.last(1))

    @pl.when(step < images)
    def _():
        hmask = hmask_ref[...]
        unit, _ = normalize(nn(place_ref[...], tok_ref[0]))
        normed = (unit * vec(0) + vec(1)).astype(BF16)
        for n in range(3):
            part = nn(normed, weight(n))
            if n == 0:
                part = (part + vec(2)) * scale
            if n == 2:
                part = part + vec(3)
            for w in range(4):
                qkv_ref[0, w, :, n * BLOCK : (n + 1) * BLOCK] = pad_window(
                    part[w * ROWS : (w + 1) * ROWS]
                ).astype(BF16)
        for w in range(4):
            for g in range(heads // 4):
                at = slice(g * 128, (g + 1) * 128)
                wide = slice(g * 4 * WPAD, (g + 1) * 4 * WPAD)
                q = qkv_ref[0, w, :, g * 128 : (g + 1) * 128]
                k = qkv_ref[0, w, :, BLOCK + g * 128 : BLOCK + (g + 1) * 128]
                v = qkv_ref[0, w, :, 2 * BLOCK + g * 128 : 2 * BLOCK + (g + 1) * 128]
                scores = nt(k, spread(q, hmask)) + bias_ref[w, :, wide]
                raised = jnp.exp(scores - jnp.max(scores, 0, keepdims=True))
                probs = raised * (1.0 / jnp.sum(raised, 0, keepdims=True))
                prob_ref[0, w, :, wide] = probs
                att_s[w * ROWS : (w + 1) * ROWS, at] = fold(tn(probs.astype(BF16), v), hmask)
        att_ref[step] = att_s[...].astype(BF16)

    @pl.when((step >= images) & (step < 2 * images))
    def _():
        image = step - images
        valid = (image < count_ref[0]).astype(F32)
        rows = pl.ds(pl.multiple_of(image * (4 * ROWS), 16), 4 * ROWS)

        def keep(block, values):
            acts[block, rows, :] = values

        middle = nn(place_ref[...], tok_ref[0]) + (nn(att_ref[image], weight(3)) + vec(4))
        unit, rate = normalize(middle)
        normed = (unit * vec(5) + vec(6)).astype(BF16)
        keep(0, normed)
        upstream = nn(place_ref[...], up_ref[0]) * valid
        up_low = upstream.astype(BF16)
        keep(9, up_low)
        note(7, upstream)
        branch = None
        grad = None
        for c in range(4):
            pre = nn(normed, weight(4 + c)) + vec(8 + c)
            below, density = normal_parts(pre)
            act = (pre * below).astype(BF16)
            keep(5 + c, act)
            grad_pre = nt(up_low, weight(8 + c)) * (below + pre * density)
            note(8 + c, grad_pre)
            pre_low = grad_pre.astype(BF16)
            keep(1 + c, pre_low)
            first = nn(act, weight(8 + c))
            second = nt(pre_low, weight(4 + c))
            branch = first if c == 0 else branch + first
            grad = second if c == 0 else grad + second
        result = middle + (branch + vec(7))
        out_ref[0] = nn(back_ref[...], (result * valid).astype(BF16)).astype(BF16)
        note(5, grad * unit)
        note(6, grad)
        grad_middle = upstream + norm_back(grad, unit, rate, vec(5))
        note(4, grad_middle)
        gmid_ref[0] = grad_middle

    @pl.when(step >= 2 * images)
    def _():
        block = step - 2 * images
        left = jnp.where(block < 4, 0, block + 1)
        right = jnp.where(block < 4, block + 1, 9)
        fc_ref[0] = tn(acts[left], acts[right]).astype(BF16)

    @pl.when(step == pl.num_programs(0) - 1)
    def _():
        for group in range(2):
            for copies in (gather.cross, gather.first, gather.second, gather.last):
                sent(copies(group))
        sent(gather.vectors())
        low_copy().wait()


SECOND_STEP = 3


def run_front(matrices, vectors, hidden_bias, table, rel_index, shift_mask, tokens, out_grad, count):
    images, tokens_image, width = tokens.shape
    heads = table.shape[1] * 2
    rows = 4 * ROWS
    far = pl.BlockSpec(memory_space=pltpu.HBM)
    small = vectors + [hidden_bias, table, rel_index, shift_mask]

    def per_image(shape, index):
        return pl.BlockSpec((1,) + shape, lambda b: (index(b),) + (0,) * len(shape))

    def whole(shape):
        return pl.BlockSpec(shape, lambda b: (0,) * len(shape), pipeline_mode=pl.Buffered(1))

    def early(b):
        return jnp.minimum(b, images - 1)

    def late(b):
        return jnp.clip(b - images, 0, images - 1)

    def twice(b):
        return jnp.where(b < images, b, late(b))

    return pl.pallas_call(
        partial(front_kernel, images),
        grid=(2 * images + 8,),
        in_specs=[pl.BlockSpec(memory_space=pltpu.SMEM)]
        + [far] * (4 + len(small))
        + [per_image((tokens_image, width), twice), per_image((tokens_image, width), late)],
        out_specs=[
            per_image((4, WPAD, 3 * BLOCK), early),
            per_image((4, WPAD, heads * WPAD), early),
            whole((images, rows, width)),
            per_image((tokens_image, width), late),
            per_image((rows, width), late),
            per_image((BLOCK, BLOCK), lambda b: jnp.maximum(b - 2 * images, 0)),
            whole((24, BLOCK)),
            whole((2, 24, 256)),
            whole((WPAD // 2, 2 * WPAD)),
            far,
        ],
        out_shape=[
            jax.ShapeDtypeStruct((images, 4, WPAD, 3 * BLOCK), BF16),
            jax.ShapeDtypeStruct((images, 4, WPAD, heads * WPAD), F32),
            jax.ShapeDtypeStruct((images, rows, width), BF16),
            jax.ShapeDtypeStruct(tokens.shape, BF16),
            jax.ShapeDtypeStruct((images, rows, width), F32),
            jax.ShapeDtypeStruct((8, BLOCK, BLOCK), BF16),
            jax.ShapeDtypeStruct((24, BLOCK), F32),
            jax.ShapeDtypeStruct((2, 24, 256), F32),
            jax.ShapeDtypeStruct((WPAD // 2, 2 * WPAD), F32),
            jax.ShapeDtypeStruct((4, 2, 256, BLOCK), BF16),
        ],
        scratch_shapes=[
            pltpu.VMEM((2, 24, 256), F32),
            pltpu.VMEM((12, 2, 256, BLOCK), BF16),
            pltpu.VMEM((10, images * rows, BLOCK), BF16),
            pltpu.VMEM((4, WPAD, heads * WPAD), F32),
            pltpu.VMEM((rows, tokens_image), BF16),
            pltpu.VMEM((tokens_image, rows), BF16),
            pltpu.VMEM((4 * WPAD, 128), BF16),
            pltpu.VMEM((rows, BLOCK), F32),
        ]
        + [pltpu.VMEM(item.shape, item.dtype) for item in small]
        + [
            pltpu.VMEM((256, 128), F32),
            pltpu.VMEM((4, WPAD, WPAD), F32),
            pltpu.VMEM((heads * WPAD // 2, 2 * WPAD), F32),
            pltpu.SemaphoreType.DMA((16,)),
            pltpu.SemaphoreType.DMA((len(small),)),
            pltpu.SemaphoreType.DMA((1,)),
            pltpu.SemaphoreType.DMA((Gather.SEMAPHORES,)),
            pltpu.SemaphoreType.DMA((Gather.SEMAPHORES,)),
        ],
        compiler_params=pltpu.CompilerParams(
            collective_id=0, has_side_effects=True, vmem_limit_bytes=56 * 1024 * 1024
        ),
        name="front",
    )(count, *matrices, *small, tokens, out_grad)


class Reduce:
    SEMAPHORES = 36

    def __init__(self, me, source, own, pair, sums, got, sum_one, got_one, sum_two, got_two, f_ref, first_block, sems, base):
        self.me, self.source, self.own, self.pair, self.sums = me, source, own, pair, sums
        self.got, self.sum_one, self.got_one = got, sum_one, got_one
        self.sum_two, self.got_two, self.f_ref = sum_two, got_two, f_ref
        self.first_block, self.sems, self.base = first_block, sems, base
        self.count = pair.shape[1]

    def axes(self, p):
        return (("y", "z"), ("z", "y"))[p]

    def copy(self, p, number, source, target, device):
        return remote(source, target, *self.sems, self.base + 18 * p + number, device)

    def blocks(self, p, core):
        return pl.ds((2 * p + core) * self.count, self.count)

    def target(self, p):
        return pl.ds(self.first_block + (2 * p + self.me.core) * self.count, self.count)

    def cores(self, p):
        return [
            self.copy(
                p, 0, self.source.at[self.blocks(p, 1 - self.me.core)], self.pair.at[p], self.me.other_core()
            )
        ]

    def add_cores(self, p):
        arrived(self.cores(p))
        for b in range(self.count):
            for half in range(2):
                if self.own is None:
                    block = self.source[pl.ds((2 * p + self.me.core) * self.count + b, 1), half][0]
                else:
                    block = self.own[p, b, half]
                total = block.astype(F32) + self.pair[p, b, half].astype(F32)
                self.sums[p, b, half] = total.astype(BF16)

    def scatter(self, p, stage):
        me, axis = self.me, self.axes(p)[stage]
        rows = (64, 16)[stage]
        source, target = ((self.sums, self.got), (self.sum_one, self.got_one))[stage]
        return [
            self.copy(
                p,
                1 + 3 * stage + s - 1,
                source.at[p, :, :, pl.ds(lax.rem(me.at[axis] + s, SIDE_CHIPS) * rows, rows)],
                target.at[p, s - 1],
                me.along(axis, s),
            )
            for s in (1, 2, 3)
        ]

    def add(self, p, stage):
        arrived(self.scatter(p, stage))
        rows = (64, 16)[stage]
        source, got, target = (
            (self.sums, self.got, self.sum_one),
            (self.sum_one, self.got_one, self.sum_two),
        )[stage]
        at = pl.ds(pl.multiple_of(self.me.at[self.axes(p)[stage]] * rows, 16), rows)
        for b in range(self.count):
            for half in range(2):
                total = source[p, b, half, at, :].astype(F32)
                for s in range(3):
                    total = total + got[p, s, b, half].astype(F32)
                target[p, b, half] = total.astype(BF16)

    def across(self, p):
        me = self.me
        copies = []
        for s in (1, 2, 3):
            peer = lax.rem(me.at["x"] + s, SIDE_CHIPS)
            copies.append(
                self.copy(
                    p, 6 + s, self.sum_two.at[p, :, peer // 2], self.got_two.at[p, me.at["x"]], me.along("x", s)
                )
            )
        return copies

    def keep_own(self, p):
        for b in range(self.count):
            self.got_two[p, pl.ds(self.me.at["x"], 1), b] = self.sum_two[p, b, pl.ds(self.me.hi, 1)]

    def place(self, p):
        first, second = self.axes(p)
        return self.me.at[first] * 64, self.me.at[first] * 64 + self.me.at[second] * 16

    def add_across(self, p):
        arrived(self.across(p))
        _, row = self.place(p)
        at = pl.ds(pl.multiple_of(row, 16), 16)
        for b in range(self.count):
            parts = [self.got_two[p, x, b].astype(F32) for x in range(4)]
            total = (parts[0] + parts[1]) + (parts[2] + parts[3])
            block = self.first_block + (2 * p + self.me.core) * self.count + b
            self.f_ref[pl.ds(block, 1), at] = total.astype(BF16)[None]

    def back(self, p, stage):
        outer, inner = self.place(p)
        axis = self.axes(p)[stage]
        at = pl.ds(outer, 64) if stage == 0 else pl.ds(inner, 16)
        part = self.f_ref.at[self.target(p), at]
        return [
            self.copy(p, 10 + 3 * (1 - stage) + s - 1, part, part, self.me.along(axis, s)) for s in (1, 2, 3)
        ]

    def last(self, p):
        part = self.f_ref.at[self.target(p)]
        return [self.copy(p, 16, part, part, self.me.other_core())]

    def step(self, number):
        for p in range(2):
            if number == 0:
                start(self.cores(p))
            elif number == 1:
                self.add_cores(p)
                start(self.scatter(p, 0))
            elif number == 2:
                self.add(p, 0)
                start(self.scatter(p, 1))
            elif number == 3:
                self.add(p, 1)
                start(self.across(p))
                self.keep_own(p)
            elif number == 4:
                self.add_across(p)
                start(self.back(p, 1))
            elif number == 5:
                arrived(self.back(p, 1))
                start(self.back(p, 0))
            elif number == 6:
                arrived(self.back(p, 0))
                start(self.last(p))
            else:
                arrived(self.last(p))

    def all_sent(self):
        for p in range(2):
            sent(self.cores(p))
            for stage in range(2):
                sent(self.scatter(p, stage))
                sent(self.back(p, stage))
            sent(self.across(p))
            sent(self.last(p))


def back_kernel(
    images,
    heads,
    qkv_ref, prob_ref, att_ref, gmid_ref, tok_ref, w_ref, vec_ref, rel_ref, small_in, fc_ref,
    tg_ref, f_out, small_out,
    f_ref, place_ref, back_ref, hmask_ref, small_ref, pair_ref, fold_s, gatt_s, dqkv_s, acts, low_ref,
    fc_own, fc_pair, fc_sums, fc_got, fc_sum_one, fc_got_one, fc_sum_two, fc_got_two,
    lo_pair, lo_sums, lo_got, lo_sum_one, lo_got_one, lo_sum_two, lo_got_two,
    small_pair, small_x, small_y, small_z, own_sem, out_sem, send_sem, recv_sem,
):
    step = pl.program_id(0)
    me = Place()
    scale = (tok_ref.shape[2] // heads) ** (-0.5)
    sems = (send_sem, recv_sem)
    high = Reduce(
        me, fc_ref, fc_own, fc_pair, fc_sums, fc_got, fc_sum_one, fc_got_one, fc_sum_two, fc_got_two, f_ref, 4, sems, 0
    )
    low = Reduce(
        me, low_ref, None, lo_pair, lo_sums, lo_got, lo_sum_one, lo_got_one, lo_sum_two, lo_got_two, f_ref, 0, sems, 36
    )

    def own_copies():
        return [
            pltpu.make_async_copy(fc_ref.at[high.blocks(p, me.core)], fc_own.at[p], own_sem.at[p])
            for p in range(2)
        ]

    def weight(n):
        return w_ref[n].reshape(BLOCK, BLOCK)

    def vec(row):
        return both_halves(vec_ref, row)

    def note(row, values):
        small_ref[row : row + 1, :] += col_sum(values)

    @pl.when(step == 0)
    def _():
        start(own_copies())
        peers = [me.other_core()]
        peers += [me.along(axis, s) for axis in ("x", "y", "z") for s in (1, 2, 3)]
        greet(peers)
        high.step(0)
        place_ref[...] = place_matrix().astype(BF16)
        back_ref[...] = back_matrix().astype(BF16)
        hmask_ref[...] = head_mask().astype(BF16)
        small_ref[...] = small_in[...]
        pair_ref[...] = jnp.zeros_like(pair_ref)

    @pl.when(step == 1)
    def _():
        for copy in own_copies():
            copy.wait()
        high.step(1)

    for number, at_step in HIGH_STEPS:
        @pl.when(step == at_step)
        def _(number=number):
            high.step(number)

    @pl.when(step < images)
    def _():
        hmask = hmask_ref[...]
        rows = pl.ds(pl.multiple_of(step * (4 * ROWS), 16), 4 * ROWS)

        def keep(block, values):
            acts[block, rows, :] = values

        keep(4, att_ref[0])
        unit, rate = normalize(nn(place_ref[...], tok_ref[0]))
        keep(0, (unit * vec(0) + vec(1)).astype(BF16))
        grad_middle = gmid_ref[0]
        proj_low = grad_middle.astype(BF16)
        keep(5, proj_low)
        grad_att = nt(proj_low, weight(3))
        for w in range(4):
            gatt_s[w] = pad_window(grad_att[w * ROWS : (w + 1) * ROWS]).astype(BF16)
        for w in range(4):
            here = slice(w * ROWS, (w + 1) * ROWS)
            for g in range(heads // 4):
                at = slice(g * 128, (g + 1) * 128)
                wide = slice(g * 4 * WPAD, (g + 1) * 4 * WPAD)
                q = qkv_ref[0, w, :, g * 128 : (g + 1) * 128]
                k = qkv_ref[0, w, :, BLOCK + g * 128 : BLOCK + (g + 1) * 128]
                v = qkv_ref[0, w, :, 2 * BLOCK + g * 128 : 2 * BLOCK + (g + 1) * 128]
                probs = prob_ref[0, w, :, wide]
                spread_grad = spread(gatt_s[w, :, at], hmask)
                grad_v = nn(probs.astype(BF16), spread_grad)
                grad_probs = nt(v, spread_grad)
                weighted = probs * grad_probs
                grad_scores = weighted - probs * jnp.sum(weighted, 0, keepdims=True)
                pair_ref[:, wide] += grad_scores
                scores_low = grad_scores.astype(BF16)
                grad_k = nn(scores_low, spread(q, hmask))
                grad_q = fold(tn(scores_low, k), hmask) * scale
                dqkv_s[here, g * 128 : (g + 1) * 128] = grad_q
                dqkv_s[here, BLOCK + g * 128 : BLOCK + (g + 1) * 128] = grad_k[:ROWS]
                dqkv_s[here, 2 * BLOCK + g * 128 : 2 * BLOCK + (g + 1) * 128] = grad_v[:ROWS]
        grad = None
        for n in range(3):
            part = dqkv_s[:, n * BLOCK : (n + 1) * BLOCK]
            if n == 0:
                note(2, part)
            if n == 2:
                note(3, part)
            part = part.astype(BF16)
            keep(1 + n, part)
            term = nt(part, weight(n))
            grad = term if n == 0 else grad + term
        note(0, grad * unit)
        note(1, grad)
        total = grad_middle + norm_back(grad, unit, rate, vec(0))
        upper = total.astype(BF16)
        rest = (total - upper.astype(F32)).astype(BF16)
        tg_ref[0] = nn(back_ref[...], upper) + nn(back_ref[...], rest)

    small_bufs = {"x": small_x, "y": small_y, "z": small_z}
    small_base = 72

    def small_cores():
        part = small_pair.at[me.core]
        return [remote(part, part, *sems, small_base, me.other_core())]

    def small_copies(axis):
        part = small_bufs[axis].at[me.at[axis]]
        first = small_base + 1 + 3 * "xyz".index(axis)
        return [remote(part, part, *sems, first + s - 1, me.along(axis, s)) for s in (1, 2, 3)]

    def small_start(axis, values):
        small_bufs[axis][pl.ds(me.at[axis], 1)] = values[None]
        start(small_copies(axis))

    def small_sum(axis):
        arrived(small_copies(axis))
        buf = small_bufs[axis]
        return (buf[0] + buf[1]) + (buf[2] + buf[3])

    @pl.when(step == images)
    def _():
        for p in range(2):
            for n in (2 * p, 2 * p + 1):
                left, right = ((0, 1), (0, 2), (0, 3), (4, 5))[n]
                low_ref[n] = tn(acts[left], acts[right]).astype(BF16).reshape(2, 256, BLOCK)
            start(low.cores(p))
        half = WPAD // 2
        for h in range(heads):
            at = slice(h * WPAD, (h + 1) * WPAD)
            both = jnp.concatenate([pair_ref[:half, at], pair_ref[half:, at]], 1)
            fold_s[pl.ds(h, half, stride=heads), :] = both

        def body(j, total):
            values = fold_s[pl.ds(pl.multiple_of(j * heads, heads), heads), :]
            upper = values.astype(BF16)
            rest = (values - upper.astype(F32)).astype(BF16)
            return total + nt(jnp.concatenate([upper, rest], 0), pair_rows(rel_ref, j))

        total = lax.fori_loop(0, half, body, jnp.zeros((2 * heads, 256), F32))
        table = total[:heads] + total[heads:]
        small_ref[12 : 12 + heads // 2, :256] = table[: heads // 2]
        small_ref[12 : 12 + heads // 2, 256:] = table[heads // 2 :]
        small_pair[pl.ds(me.core, 1)] = small_ref[...][None]
        start(small_cores())
        low.step(1)
        for number in TAIL_HIGH[0]:
            high.step(number)
        arrived(small_cores())
        small_start("x", small_pair[0] + small_pair[1])
        low.step(2)
        for number in TAIL_HIGH[1]:
            high.step(number)
        small_start("y", small_sum("x"))
        low.step(3)
        for number in TAIL_HIGH[2]:
            high.step(number)
        small_start("z", small_sum("y"))
        high_out = pltpu.make_async_copy(f_ref.at[pl.ds(4, 8)], f_out.at[pl.ds(4, 8)], out_sem.at[0])
        high_out.start()
        low.step(4)
        low.step(5)
        small_total = small_sum("z")
        small_out[...] = jnp.where(me.hi == 0, small_total[:, :256], small_total[:, 256:])
        low.step(6)
        low.step(7)
        low_out = pltpu.make_async_copy(f_ref.at[pl.ds(0, 4)], f_out.at[pl.ds(0, 4)], out_sem.at[1])
        low_out.start()
        high_out.wait()
        low_out.wait()
        high.all_sent()
        low.all_sent()
        sent(small_cores())
        for axis in "xyz":
            sent(small_copies(axis))


HIGH_STEPS = ((2, 3), (3, 4), (4, 5))
TAIL_HIGH = ((5,), (6,), (7,))


def run_back(qkv, prob, att, gmid, tokens, weights, vecs, rel_rows, small, fc):
    images, tokens_image, width = tokens.shape
    heads = prob.shape[3] // WPAD
    rows = 4 * ROWS
    vmem = pl.BlockSpec(memory_space=pltpu.VMEM)
    far = pl.BlockSpec(memory_space=pltpu.HBM)

    def per_image(shape):
        return pl.BlockSpec(
            (1,) + shape, lambda b: (jnp.minimum(b, images - 1),) + (0,) * len(shape)
        )

    def whole(array):
        return pl.BlockSpec(array.shape, lambda b: (0,) * array.ndim, pipeline_mode=pl.Buffered(1))

    def reduce_scratch(count):
        return [
            pltpu.VMEM((2, count, 2, 256, BLOCK), BF16),
            pltpu.VMEM((2, count, 2, 256, BLOCK), BF16),
            pltpu.VMEM((2, 3, count, 2, 64, BLOCK), BF16),
            pltpu.VMEM((2, count, 2, 64, BLOCK), BF16),
            pltpu.VMEM((2, 3, count, 2, 16, BLOCK), BF16),
            pltpu.VMEM((2, count, 2, 16, BLOCK), BF16),
            pltpu.VMEM((2, 4, count, 16, BLOCK), BF16),
        ]

    return pl.pallas_call(
        partial(back_kernel, images, heads),
        grid=(images + 1,),
        in_specs=[
            per_image(qkv.shape[1:]),
            per_image(prob.shape[1:]),
            per_image(att.shape[1:]),
            per_image(gmid.shape[1:]),
            per_image((tokens_image, width)),
            whole(weights),
            whole(vecs),
            whole(rel_rows),
            whole(small),
            far,
        ],
        out_specs=[per_image((tokens_image, width)), far, vmem],
        out_shape=[
            jax.ShapeDtypeStruct(tokens.shape, F32),
            jax.ShapeDtypeStruct((12, 256, BLOCK), BF16),
            jax.ShapeDtypeStruct((24, 256), F32),
        ],
        scratch_shapes=[
            pltpu.VMEM((12, 256, BLOCK), BF16),
            pltpu.VMEM((rows, tokens_image), BF16),
            pltpu.VMEM((tokens_image, rows), BF16),
            pltpu.VMEM((4 * WPAD, 128), BF16),
            pltpu.VMEM((24, BLOCK), F32),
            pltpu.VMEM((WPAD, heads * WPAD), F32),
            pltpu.VMEM((heads * WPAD // 2, 128), F32),
            pltpu.VMEM((4, WPAD, BLOCK), BF16),
            pltpu.VMEM((rows, 3 * BLOCK), F32),
            pltpu.VMEM((6, images * rows, BLOCK), BF16),
            pltpu.VMEM((4, 2, 256, BLOCK), BF16),
            pltpu.VMEM((2, 2, 2, 256, BLOCK), BF16),
        ]
        + reduce_scratch(2)
        + reduce_scratch(1)
        + [
            pltpu.VMEM((2, 24, BLOCK), F32),
            pltpu.VMEM((4, 24, BLOCK), F32),
            pltpu.VMEM((4, 24, BLOCK), F32),
            pltpu.VMEM((4, 24, BLOCK), F32),
            pltpu.SemaphoreType.DMA((2,)),
            pltpu.SemaphoreType.DMA((2,)),
            pltpu.SemaphoreType.DMA((82,)),
            pltpu.SemaphoreType.DMA((82,)),
        ],
        compiler_params=pltpu.CompilerParams(
            collective_id=1, has_side_effects=True, vmem_limit_bytes=56 * 1024 * 1024
        ),
        name="back",
    )(qkv, prob, att, gmid, tokens, weights, vecs, rel_rows, small, fc)


def finish_kernel(
    f_ref, small_ref, n1g, n1b, qkv, qb, vb, table, proj, pb, n2g, n2b, fc1, f1b, fc2, f2b, wide, turn, sem
):
    copies = []

    def store(source, target):
        copy = pltpu.make_async_copy(source, target, sem.at[len(copies)])
        copy.start()
        copies.append(copy)

    for n in range(12):
        wide[n] = f_ref[n].astype(F32)
        if n < 3:
            store(wide.at[n], qkv.at[:, pl.ds(n * BLOCK, BLOCK)])
        elif n == 3:
            store(wide.at[n], proj)
        elif n < 8:
            for half in range(2):
                store(
                    wide.at[n, :, pl.ds(half * 256, 256)],
                    fc1.at[:, pl.ds(half * 1024 + (n - 4) * 256, 256)],
                )
        else:
            store(wide.at[n], fc2.at[pl.ds((n - 8) * 256, 256)])
    for row, ref in enumerate((n1g, n1b, qb, vb, pb, n2g, n2b, f2b)):
        ref[...] = small_ref[row : row + 1, :].reshape(256)
    for m in range(4):
        f1b[pl.ds(m * 256, 256)] = small_ref[8 + m : 9 + m, :].reshape(256)
    turn[...] = jnp.zeros_like(turn)
    turn[0:8, :] = small_ref[12:20, :]
    table[...] = jnp.concatenate([turn[:, 0:128].T, turn[:, 128:256].T], 0)[
        : table.shape[0], : table.shape[1]
    ]
    for copy in copies:
        copy.wait()


def finish(grads, small, table_rows, heads_here):
    vmem = pl.BlockSpec(memory_space=pltpu.VMEM)
    far = pl.BlockSpec(memory_space=pl.ANY)
    vector, hidden = ((256,), vmem), ((1024,), vmem)
    outs = [
        vector, vector, ((256, 3 * BLOCK), far), vector, vector, ((table_rows, heads_here), vmem),
        ((256, BLOCK), far), vector, vector, vector, ((256, 4 * BLOCK), far), hidden,
        ((1024, BLOCK), far), vector,
    ]
    return pl.pallas_call(
        finish_kernel,
        in_specs=[vmem, vmem],
        out_specs=[spec for _, spec in outs],
        out_shape=[jax.ShapeDtypeStruct(shape, F32) for shape, _ in outs],
        scratch_shapes=[
            pltpu.VMEM((12, 256, BLOCK), F32),
            pltpu.VMEM((128, 256), F32),
            pltpu.SemaphoreType.DMA((16,)),
        ],
        compiler_params=pltpu.CompilerParams(vmem_limit_bytes=30 * 1024 * 1024),
        name="finish",
    )(grads, small)


def local(
    tokens, image_counts, shift_mask, rel_index, norm1_gain, norm1_bias, qkv_weight, q_bias, v_bias,
    rel_table, proj_weight, proj_bias, norm2_gain, norm2_bias, fc1_weight, fc1_bias, fc2_weight,
    fc2_bias, out_grad,
):
    table_rows, heads_here = rel_table.shape
    qkv, prob, att, block_out, gmid, fc, small, vecs, rel_rows, low_weights = run_front(
        [qkv_weight, proj_weight, fc1_weight, fc2_weight],
        [norm1_gain, norm1_bias, q_bias, v_bias, proj_bias, norm2_gain, norm2_bias, fc2_bias],
        fc1_bias, rel_table, rel_index, shift_mask, tokens, out_grad, image_counts,
    )
    tokens_grad, grads, small = run_back(
        qkv, prob, att, gmid, tokens, low_weights, vecs, rel_rows, small, fc.reshape(8, 2, 256, BLOCK)
    )
    outs = finish(grads, small, table_rows, heads_here)
    return (block_out, tokens_grad, *outs)


def solution(mesh):
    split = P(("replica", "shard"), None, None)
    vector, matrix, table = P("shard"), P("shard", None), P(None, "shard")
    return jax.shard_map(
        local,
        mesh=mesh,
        in_specs=(
            split, P(("replica", "shard")), P(), P(), vector, vector, matrix, vector, vector, table,
            matrix, vector, vector, vector, matrix, vector, matrix, vector, split,
        ),
        out_specs=(
            split, split, vector, vector, matrix, vector, vector, table, matrix, vector, vector,
            vector, matrix, vector, matrix, vector,
        ),
        check_vma=False,
    )
```

```python
from functools import partial

import jax
import jax.numpy as jnp
from jax import lax
from jax.experimental import pallas as pl
from jax.experimental.pallas import tpu as pltpu
from jax.sharding import PartitionSpec as P

WIN = 7
SIDE = 14
SHIFT = 3
EPSILON = 1e-05
MASKED = -1e30
WTOK = WIN * WIN
ROWS = 56
WPAD = 64
BLOCK = 512
F32 = jnp.float32
BF16 = jnp.bfloat16


def nn(left, right):
    return jnp.dot(left, right, preferred_element_type=F32)


def nt(left, right):
    return lax.dot_general(left, right, (((1,), (1,)), ((), ())), preferred_element_type=F32)


def tn(left, right):
    return lax.dot_general(left, right, (((0,), (0,)), ((), ())), preferred_element_type=F32)


def normalize(values):
    center = values - jnp.mean(values, -1, keepdims=True)
    rate = lax.rsqrt(jnp.mean(center * center, -1, keepdims=True) + EPSILON)
    return center * rate, rate


def norm_back(grad, unit, rate, gain):
    scaled = grad * gain
    return rate * (
        scaled
        - jnp.mean(scaled, -1, keepdims=True)
        - unit * jnp.mean(scaled * unit, -1, keepdims=True)
    )


def normal_parts(v):
    size = jnp.abs(v) * 0.7071067811865476
    bell = jnp.exp(-0.5 * v * v)
    t = 1.0 / (1.0 + 0.3275911 * size)
    tail = t * (
        0.254829592
        + t * (-0.284496736 + t * (1.421413741 + t * (-1.453152027 + t * 1.061405429)))
    )
    half = 0.5 * tail * bell
    return jnp.where(v < 0, half, 1.0 - half), 0.3989422804014327 * bell


def col_sum(values):
    return jnp.sum(values, 0, keepdims=True)


MESH = pl.DeviceIdType.MESH
SIDE_CHIPS = 4


class Place:
    def __init__(self):
        replica = lax.axis_index("replica")
        self.hi = lax.axis_index("shard")
        self.core = lax.rem(replica, 2)
        self.at = {
            "x": self.hi * 2 + lax.rem(replica // 2, 2),
            "z": lax.rem(replica // 4, SIDE_CHIPS),
            "y": replica // 16,
        }
        self.lo = lax.rem(replica // 2, 2)

    def id_of(self, core=None, **at):
        place = dict(self.at, **at)
        core = self.core if core is None else core
        lo, hi = lax.rem(place["x"], 2), place["x"] // 2
        return (((place["y"] * SIDE_CHIPS + place["z"]) * 2 + lo) * 2 + core, hi)

    def other_core(self):
        return self.id_of(core=1 - self.core)

    def along(self, axis, step):
        return self.id_of(**{axis: lax.rem(self.at[axis] + step, SIDE_CHIPS)})


def greet(devices):
    barrier = pltpu.get_barrier_semaphore()
    for device in devices:
        pl.semaphore_signal(barrier, inc=1, device_id=device, device_id_type=MESH)
    pl.semaphore_wait(barrier, len(devices))


def pad_window(values):
    return jnp.concatenate([values, jnp.zeros((WPAD - ROWS, values.shape[1]), F32)], 0)


def source_of(row):
    window = jnp.floor((row + 0.5) / ROWS)
    cell = row - window * ROWS
    across = jnp.floor((window + 0.5) / 2)
    down = jnp.floor((cell + 0.5) / WIN)
    i = across * WIN + down + SHIFT
    j = (window - 2 * across) * WIN + (cell - down * WIN) + SHIFT
    i = jnp.where(i >= SIDE, i - SIDE, i)
    j = jnp.where(j >= SIDE, j - SIDE, j)
    return jnp.where(cell < WTOK, i * SIDE + j, -1.0)


def iota(shape, axis):
    return lax.broadcasted_iota(jnp.int32, shape, axis).astype(F32)


def place_matrix():
    rows, tokens = 4 * ROWS, SIDE * SIDE
    return jnp.where(source_of(iota((rows, tokens), 0)) == iota((rows, tokens), 1), 1.0, 0.0)


def back_matrix():
    rows, tokens = 4 * ROWS, SIDE * SIDE
    return jnp.where(source_of(iota((tokens, rows), 1)) == iota((tokens, rows), 0), 1.0, 0.0)


def head_mask():
    shape = (4 * WPAD, 128)
    row, lane = iota(shape, 0), iota(shape, 1)
    return jnp.where(jnp.floor((row + 0.5) / WPAD) == jnp.floor((lane + 0.5) / 32), 1.0, 0.0)


def pair_rows(rel_ref, j):
    return jnp.where(iota((256, 128), 0) == rel_ref[pl.ds(j, 1), :], 1.0, 0.0).astype(BF16)


def spread(part, hmask):
    return jnp.concatenate([part] * 4, 0) * hmask


def fold(full, hmask):
    full = full * hmask.astype(F32)
    total = full[:WPAD]
    for h in range(1, 4):
        total = total + full[h * WPAD : (h + 1) * WPAD]
    return total[:ROWS]


def both_halves(vec_ref, row):
    return jnp.concatenate([vec_ref[0, row : row + 1, :], vec_ref[1, row : row + 1, :]], 1)


def remote(source, target, send_sem, recv_sem, number, device):
    return pltpu.make_async_remote_copy(
        src_ref=source,
        dst_ref=target,
        send_sem=send_sem.at[number],
        recv_sem=recv_sem.at[number],
        device_id=device,
        device_id_type=MESH,
    )


def start(copies):
    for copy in copies:
        copy.start()


def arrived(copies):
    for copy in copies:
        copy.wait_recv()


def sent(copies):
    for copy in copies:
        copy.wait_send()


class Gather:
    SEMAPHORES = 33

    def __init__(self, me, w_ref, v_ref, send_sem, recv_sem):
        self.me, self.w, self.v = me, w_ref, v_ref
        self.sems = (send_sem, recv_sem)

    def flows(self, group):
        count = 1 + group
        for flow, (first, second) in enumerate((("z", "y"), ("y", "z"))):
            block = 4 * group + 2 * count * flow + self.me.core * count
            yield 16 * group + 8 * flow, pl.ds(block, count), first, second

    def copy(self, number, part, device):
        return remote(part, part, *self.sems, number, device)

    def facing(self):
        return self.me.id_of(x=3 - self.me.at["x"])

    def cross(self, group):
        me = self.me
        return [
            self.copy(
                number,
                self.w.at[blocks, me.hi, pl.ds(me.at[second] * 64 + me.at[first] * 16, 16)],
                self.facing(),
            )
            for number, blocks, first, second in self.flows(group)
        ]

    def vectors(self):
        return [self.copy(32, self.v.at[self.me.hi], self.facing())]

    def first(self, group):
        me = self.me
        return [
            self.copy(
                number + step,
                self.w.at[blocks, 1 - me.hi, pl.ds(me.at[second] * 64 + me.at[first] * 16, 16)],
                me.along(first, step),
            )
            for number, blocks, first, second in self.flows(group)
            for step in (1, 2, 3)
        ]

    def second(self, group):
        me = self.me
        return [
            self.copy(
                number + 3 + step,
                self.w.at[blocks, 1 - me.hi, pl.ds(me.at[second] * 64, 64)],
                me.along(second, step),
            )
            for number, blocks, first, second in self.flows(group)
            for step in (1, 2, 3)
        ]

    def last(self, group):
        return [
            self.copy(number + 7, self.w.at[blocks, 1 - self.me.hi], self.me.other_core())
            for number, blocks, _, _ in self.flows(group)
        ]


def front_kernel(
    images,
    count_ref,
    qkv_w, proj_w, fc1_w, fc2_w, n1g, n1b, qb, vb, pb, n2g, n2b, f2b, f1b, table_w, index_w, mask_w,
    tok_ref, up_ref,
    qkv_ref, prob_ref, normed_ref, att_ref, out_ref, gmid_ref, fc_ref, small_ref, vec_out, rel_ref, low_ref,
    vec_ref, w_ref, acts, bias_ref, place_ref, hmask_ref, att_s, qkv_s, prob_s, acts_s,
    v0, v1, v2, v3, v4, v5, v6, v7, v8, table_v, index_v, mask_v, square, square_mask, pairs,
    w_sem, in_sem, low_sem, send_sem, recv_sem,
):
    step = pl.program_id(0)
    me = Place()
    hi = me.hi
    gather = Gather(me, w_ref, vec_ref, send_sem, recv_sem)
    heads = table_w.shape[0] * 2
    scale = (tok_ref.shape[2] // heads) ** (-0.5)

    def own_weights(group):
        pairs = []
        if group == 0:
            for n in range(3):
                pairs.append((qkv_w.at[:, pl.ds(n * BLOCK, BLOCK)], w_ref.at[n, hi]))
            pairs.append((proj_w, w_ref.at[3, hi]))
        else:
            for m in range(4):
                for half in range(2):
                    pairs.append(
                        (
                            fc1_w.at[:, pl.ds(half * 1024 + m * 256, 256)],
                            w_ref.at[4 + m, hi, :, pl.ds(half * 256, 256)],
                        )
                    )
                pairs.append((fc2_w.at[pl.ds(m * 256, 256)], w_ref.at[8 + m, hi]))
        return [
            pltpu.make_async_copy(source, target, w_sem.at[4 * group + i])
            for i, (source, target) in enumerate(pairs)
        ]

    def own_small():
        sources = (n1g, n1b, qb, vb, pb, n2g, n2b, f2b, f1b, table_w, index_w, mask_w)
        targets = (v0, v1, v2, v3, v4, v5, v6, v7, v8, table_v, index_v, mask_v)
        return [
            pltpu.make_async_copy(source, target, in_sem.at[i])
            for i, (source, target) in enumerate(zip(sources, targets))
        ]

    def low_copy():
        return pltpu.make_async_copy(w_ref.at[pl.ds(0, 4)], low_ref, low_sem.at[0])

    def weight(n):
        return w_ref[n].reshape(BLOCK, BLOCK)

    def vec(row):
        return both_halves(vec_ref, row)

    def note(row, values):
        small_ref[row : row + 1, :] += col_sum(values)

    @pl.when(step == 0)
    def _():
        small_copies = own_small()
        start(own_weights(0))
        start(small_copies)
        start(own_weights(1))
        peers = [gather.facing(), me.other_core()]
        peers += [me.along(axis, s) for axis in ("y", "z") for s in (1, 2, 3)]
        greet(peers)
        for copy in own_weights(0):
            copy.wait()
        start(gather.cross(0))
        for copy in small_copies:
            copy.wait()
        rows = [ref[...].astype(F32).reshape(1, 256) for ref in (v0, v1, v2, v3, v4, v5, v6, v7)]
        rows += [v8[pl.ds(m * 256, 256)].astype(F32).reshape(1, 256) for m in range(4)]
        rows.append(jnp.zeros((4, 256), F32))
        vec_ref[pl.ds(hi, 1), 0:16] = jnp.concatenate(rows, 0)[None]
        heads_here, table_rows = table_v.shape
        vec_ref[pl.ds(hi, 1), 16:24] = jnp.zeros((1, 8, 256), F32)
        vec_ref[pl.ds(hi, 1), 16:24, 0:table_rows] = table_v[...].astype(F32)[None]
        start(gather.vectors())
        for copy in own_weights(1):
            copy.wait()
        start(gather.cross(1))
        arrived(gather.cross(0))
        start(gather.first(0))
        arrived(gather.cross(1))
        start(gather.first(1))
        square[...] = jnp.full((128, 128), -1.0, F32)
        square[0:WTOK, 0:WTOK] = index_v[...].astype(F32)
        turned = square[...].T
        half = WPAD // 2
        rel_ref[...] = jnp.concatenate([turned[:half, :WPAD], turned[half:WPAD, :WPAD]], 1)
        for w in range(4):
            square_mask[w] = jnp.where(iota((WPAD, WPAD), 0) < WTOK, 0.0, MASKED)
            square_mask[w, 0:WTOK, 0:WTOK] = jnp.where(mask_v[:, w, :] == 1, 0.0, -100.0)
        place_ref[...] = place_matrix().astype(BF16)
        hmask_ref[...] = head_mask().astype(BF16)
        small_ref[...] = jnp.zeros_like(small_ref)
        arrived(gather.first(0))
        start(gather.second(0))
        arrived(gather.first(1))
        start(gather.second(1))
        arrived(gather.vectors())
        vec_out[...] = vec_ref[...]
        table = jnp.concatenate([vec_ref[0, 16:24], vec_ref[1, 16:24]], 0).astype(BF16)

        def body(j, carry):
            pairs[pl.ds(pl.multiple_of(j * heads, heads), heads), :] = nn(table, pair_rows(rel_ref, j))
            return carry

        lax.fori_loop(0, half, body, 0, unroll=4)
        arrived(gather.second(0))
        start(gather.last(0))
        for h in range(heads):
            at = slice(h * WPAD, (h + 1) * WPAD)
            both = pairs[pl.ds(h, half, stride=heads), :]
            for w in range(4):
                bias_ref[w, :half, at] = both[:, :WPAD] + square_mask[w, :half]
                bias_ref[w, half:, at] = both[:, WPAD:] + square_mask[w, half:]
        arrived(gather.last(0))
        low_copy().start()

    @pl.when(step == SECOND_STEP)
    def _():
        arrived(gather.second(1))
        start(gather.last(1))

    @pl.when(step == images)
    def _():
        arrived(gather.last(1))

    @pl.when(step < images)
    def _():
        hmask = hmask_ref[...]
        unit, _ = normalize(nn(place_ref[...], tok_ref[0]))
        normed = (unit * vec(0) + vec(1)).astype(BF16)
        for n in range(3):
            part = nn(normed, weight(n))
            if n == 0:
                part = (part + vec(2)) * scale
            if n == 2:
                part = part + vec(3)
            for w in range(4):
                qkv_s[w, :, n * BLOCK : (n + 1) * BLOCK] = pad_window(
                    part[w * ROWS : (w + 1) * ROWS]
                ).astype(BF16)
        for w in range(4):
            for g in range(heads // 4):
                at = slice(g * 128, (g + 1) * 128)
                wide = slice(g * 4 * WPAD, (g + 1) * 4 * WPAD)
                q = qkv_s[w, :, g * 128 : (g + 1) * 128]
                k = qkv_s[w, :, BLOCK + g * 128 : BLOCK + (g + 1) * 128]
                v = qkv_s[w, :, 2 * BLOCK + g * 128 : 2 * BLOCK + (g + 1) * 128]
                scores = nt(k, spread(q, hmask)) + bias_ref[w, :, wide]
                raised = jnp.exp(scores - jnp.max(scores, 0, keepdims=True))
                probs = raised * (1.0 / jnp.sum(raised, 0, keepdims=True))
                prob_s[w, :, wide] = probs
                att_s[w * ROWS : (w + 1) * ROWS, at] = fold(tn(probs.astype(BF16), v), hmask)
        att_ref[step] = att_s[...].astype(BF16)
        normed_ref[0] = normed
        qkv_ref[0] = qkv_s[...]
        prob_ref[0] = prob_s[...]

    @pl.when((step >= images) & (step < 2 * images))
    def _():
        image = step - images
        valid = (image < count_ref[0]).astype(F32)
        rows = pl.ds(pl.multiple_of(image * (4 * ROWS), 16), 4 * ROWS)

        def keep(block, values):
            acts_s[block] = values

        middle = nn(place_ref[...], tok_ref[0]) + (nn(att_ref[image], weight(3)) + vec(4))
        unit, rate = normalize(middle)
        normed = (unit * vec(5) + vec(6)).astype(BF16)
        keep(0, normed)
        upstream = nn(place_ref[...], up_ref[0]) * valid
        up_low = upstream.astype(BF16)
        keep(9, up_low)
        note(7, upstream)
        branch = None
        grad = None
        for c in range(4):
            pre = nn(normed, weight(4 + c)) + vec(8 + c)
            below, density = normal_parts(pre)
            act = (pre * below).astype(BF16)
            keep(5 + c, act)
            grad_pre = nt(up_low, weight(8 + c)) * (below + pre * density)
            note(8 + c, grad_pre)
            pre_low = grad_pre.astype(BF16)
            keep(1 + c, pre_low)
            first = nn(act, weight(8 + c))
            second = nt(pre_low, weight(4 + c))
            branch = first if c == 0 else branch + first
            grad = second if c == 0 else grad + second
        result = middle + (branch + vec(7))
        note(5, grad * unit)
        note(6, grad)
        grad_middle = upstream + norm_back(grad, unit, rate, vec(5))
        note(4, grad_middle)
        gmid_ref[0] = grad_middle
        out_ref[0] = (result * valid).astype(BF16)
        for block in range(10):
            acts[block, rows, :] = acts_s[block]

    @pl.when(step >= 2 * images)
    def _():
        block = step - 2 * images
        left = jnp.where(block < 4, 0, block + 1)
        right = jnp.where(block < 4, block + 1, 9)
        fc_ref[0] = tn(acts[left], acts[right]).astype(BF16)

    @pl.when(step == pl.num_programs(0) - 1)
    def _():
        for group in range(2):
            for copies in (gather.cross, gather.first, gather.second, gather.last):
                sent(copies(group))
        sent(gather.vectors())
        low_copy().wait()


SECOND_STEP = 3


def run_front(matrices, vectors, hidden_bias, table, rel_index, shift_mask, tokens, out_grad, count):
    images, tokens_image, width = tokens.shape
    heads = table.shape[0] * 2
    rows = 4 * ROWS
    far = pl.BlockSpec(memory_space=pltpu.HBM)
    small = vectors + [hidden_bias, table, rel_index, shift_mask]

    def per_image(shape, index):
        return pl.BlockSpec((1,) + shape, lambda b: (index(b),) + (0,) * len(shape))

    def whole(shape):
        return pl.BlockSpec(shape, lambda b: (0,) * len(shape), pipeline_mode=pl.Buffered(1))

    def early(b):
        return jnp.minimum(b, images - 1)

    def late(b):
        return jnp.clip(b - images, 0, images - 1)

    def twice(b):
        return jnp.where(b < images, b, late(b))

    return pl.pallas_call(
        partial(front_kernel, images),
        grid=(2 * images + 8,),
        in_specs=[pl.BlockSpec(memory_space=pltpu.SMEM)]
        + [far] * (4 + len(small))
        + [per_image((tokens_image, width), twice), per_image((tokens_image, width), late)],
        out_specs=[
            per_image((4, WPAD, 3 * BLOCK), early),
            per_image((4, WPAD, heads * WPAD), early),
            per_image((rows, width), early),
            whole((images, rows, width)),
            per_image((rows, width), late),
            per_image((rows, width), late),
            per_image((BLOCK, BLOCK), lambda b: jnp.maximum(b - 2 * images, 0)),
            whole((24, BLOCK)),
            whole((2, 24, 256)),
            whole((WPAD // 2, 2 * WPAD)),
            far,
        ],
        out_shape=[
            jax.ShapeDtypeStruct((images, 4, WPAD, 3 * BLOCK), BF16),
            jax.ShapeDtypeStruct((images, 4, WPAD, heads * WPAD), F32),
            jax.ShapeDtypeStruct((images, rows, width), BF16),
            jax.ShapeDtypeStruct((images, rows, width), BF16),
            jax.ShapeDtypeStruct((images, rows, width), BF16),
            jax.ShapeDtypeStruct((images, rows, width), F32),
            jax.ShapeDtypeStruct((8, BLOCK, BLOCK), BF16),
            jax.ShapeDtypeStruct((24, BLOCK), F32),
            jax.ShapeDtypeStruct((2, 24, 256), F32),
            jax.ShapeDtypeStruct((WPAD // 2, 2 * WPAD), F32),
            jax.ShapeDtypeStruct((4, 2, 256, BLOCK), BF16),
        ],
        scratch_shapes=[
            pltpu.VMEM((2, 24, 256), F32),
            pltpu.VMEM((12, 2, 256, BLOCK), BF16),
            pltpu.VMEM((10, images * rows, BLOCK), BF16),
            pltpu.VMEM((4, WPAD, heads * WPAD), F32),
            pltpu.VMEM((rows, tokens_image), BF16),
            pltpu.VMEM((4 * WPAD, 128), BF16),
            pltpu.VMEM((rows, BLOCK), F32),
            pltpu.VMEM((4, WPAD, 3 * BLOCK), BF16),
            pltpu.VMEM((4, WPAD, heads * WPAD), F32),
            pltpu.VMEM((10, rows, BLOCK), BF16),
        ]
        + [pltpu.VMEM(item.shape, item.dtype) for item in small]
        + [
            pltpu.VMEM((128, 128), F32),
            pltpu.VMEM((4, WPAD, WPAD), F32),
            pltpu.VMEM((heads * WPAD // 2, 2 * WPAD), F32),
            pltpu.SemaphoreType.DMA((16,)),
            pltpu.SemaphoreType.DMA((len(small),)),
            pltpu.SemaphoreType.DMA((1,)),
            pltpu.SemaphoreType.DMA((Gather.SEMAPHORES,)),
            pltpu.SemaphoreType.DMA((Gather.SEMAPHORES,)),
        ],
        compiler_params=pltpu.CompilerParams(
            collective_id=0, has_side_effects=True, vmem_limit_bytes=56 * 1024 * 1024
        ),
        name="front",
    )(count, *matrices, *small, tokens, out_grad)


class Reduce:
    SEMAPHORES = 36

    def __init__(self, me, source, own, pair, sums, got, sum_one, got_one, sum_two, got_two, f_ref, first_block, sems, base):
        self.me, self.source, self.own, self.pair, self.sums = me, source, own, pair, sums
        self.got, self.sum_one, self.got_one = got, sum_one, got_one
        self.sum_two, self.got_two, self.f_ref = sum_two, got_two, f_ref
        self.first_block, self.sems, self.base = first_block, sems, base
        self.count = pair.shape[1]

    def axes(self, p):
        return (("y", "z"), ("z", "y"))[p]

    def copy(self, p, number, source, target, device):
        return remote(source, target, *self.sems, self.base + 18 * p + number, device)

    def blocks(self, p, core):
        return pl.ds((2 * p + core) * self.count, self.count)

    def target(self, p):
        return pl.ds(self.first_block + (2 * p + self.me.core) * self.count, self.count)

    def cores(self, p):
        return [
            self.copy(
                p, 0, self.source.at[self.blocks(p, 1 - self.me.core)], self.pair.at[p], self.me.other_core()
            )
        ]

    def add_cores(self, p):
        arrived(self.cores(p))
        for b in range(self.count):
            for half in range(2):
                if self.own is None:
                    block = self.source[pl.ds((2 * p + self.me.core) * self.count + b, 1), half][0]
                else:
                    block = self.own[p, b, half]
                total = block.astype(F32) + self.pair[p, b, half].astype(F32)
                self.sums[p, b, half] = total.astype(BF16)

    def scatter(self, p, stage):
        me, axis = self.me, self.axes(p)[stage]
        rows = (64, 16)[stage]
        source, target = ((self.sums, self.got), (self.sum_one, self.got_one))[stage]
        return [
            self.copy(
                p,
                1 + 3 * stage + s - 1,
                source.at[p, :, :, pl.ds(lax.rem(me.at[axis] + s, SIDE_CHIPS) * rows, rows)],
                target.at[p, s - 1],
                me.along(axis, s),
            )
            for s in (1, 2, 3)
        ]

    def add(self, p, stage):
        arrived(self.scatter(p, stage))
        rows = (64, 16)[stage]
        source, got, target = (
            (self.sums, self.got, self.sum_one),
            (self.sum_one, self.got_one, self.sum_two),
        )[stage]
        at = pl.ds(pl.multiple_of(self.me.at[self.axes(p)[stage]] * rows, 16), rows)
        for b in range(self.count):
            for half in range(2):
                total = source[p, b, half, at, :].astype(F32)
                for s in range(3):
                    total = total + got[p, s, b, half].astype(F32)
                target[p, b, half] = total.astype(BF16)

    def across(self, p):
        me = self.me
        copies = []
        for s in (1, 2, 3):
            peer = lax.rem(me.at["x"] + s, SIDE_CHIPS)
            copies.append(
                self.copy(
                    p, 6 + s, self.sum_two.at[p, :, peer // 2], self.got_two.at[p, me.at["x"]], me.along("x", s)
                )
            )
        return copies

    def keep_own(self, p):
        for b in range(self.count):
            self.got_two[p, pl.ds(self.me.at["x"], 1), b] = self.sum_two[p, b, pl.ds(self.me.hi, 1)]

    def place(self, p):
        first, second = self.axes(p)
        return self.me.at[first] * 64, self.me.at[first] * 64 + self.me.at[second] * 16

    def add_across(self, p):
        arrived(self.across(p))
        _, row = self.place(p)
        at = pl.ds(pl.multiple_of(row, 16), 16)
        for b in range(self.count):
            parts = [self.got_two[p, x, b].astype(F32) for x in range(4)]
            total = (parts[0] + parts[1]) + (parts[2] + parts[3])
            block = self.first_block + (2 * p + self.me.core) * self.count + b
            self.f_ref[pl.ds(block, 1), at] = total.astype(BF16)[None]

    def back(self, p, stage):
        outer, inner = self.place(p)
        axis = self.axes(p)[stage]
        at = pl.ds(outer, 64) if stage == 0 else pl.ds(inner, 16)
        part = self.f_ref.at[self.target(p), at]
        return [
            self.copy(p, 10 + 3 * (1 - stage) + s - 1, part, part, self.me.along(axis, s)) for s in (1, 2, 3)
        ]

    def last(self, p):
        part = self.f_ref.at[self.target(p)]
        return [self.copy(p, 16, part, part, self.me.other_core())]

    def step(self, number):
        for p in range(2):
            if number == 0:
                start(self.cores(p))
            elif number == 1:
                self.add_cores(p)
                start(self.scatter(p, 0))
            elif number == 2:
                self.add(p, 0)
                start(self.scatter(p, 1))
            elif number == 3:
                self.add(p, 1)
                start(self.across(p))
                self.keep_own(p)
            elif number == 4:
                self.add_across(p)
                start(self.back(p, 1))
            elif number == 5:
                arrived(self.back(p, 1))
                start(self.back(p, 0))
            elif number == 6:
                arrived(self.back(p, 0))
                start(self.last(p))
            else:
                arrived(self.last(p))

    def all_sent(self):
        for p in range(2):
            sent(self.cores(p))
            for stage in range(2):
                sent(self.scatter(p, stage))
                sent(self.back(p, stage))
            sent(self.across(p))
            sent(self.last(p))


def back_kernel(
    images,
    heads,
    qkv_ref, prob_ref, normed_ref, att_ref, gmid_ref, tok_ref, w_ref, vec_ref, rel_ref, small_in, fc_ref,
    tg_ref, f_out, small_out,
    qkv_s, prob_s, gmid_s, acts_s, f_ref, place_ref, hmask_ref, small_ref, pair_ref, fold_s, gatt_s, dqkv_s, acts, low_ref,
    fc_own, fc_pair, fc_sums, fc_got, fc_sum_one, fc_got_one, fc_sum_two, fc_got_two,
    lo_pair, lo_sums, lo_got, lo_sum_one, lo_got_one, lo_sum_two, lo_got_two,
    small_pair, small_halves, small_x, small_y, small_z, own_sem, out_sem, send_sem, recv_sem,
):
    step = pl.program_id(0)
    me = Place()
    scale = (tok_ref.shape[2] // heads) ** (-0.5)
    sems = (send_sem, recv_sem)
    high = Reduce(
        me, fc_ref, fc_own, fc_pair, fc_sums, fc_got, fc_sum_one, fc_got_one, fc_sum_two, fc_got_two, f_ref, 4, sems, 0
    )
    low = Reduce(
        me, low_ref, None, lo_pair, lo_sums, lo_got, lo_sum_one, lo_got_one, lo_sum_two, lo_got_two, f_ref, 0, sems, 36
    )

    def own_copies():
        return [
            pltpu.make_async_copy(fc_ref.at[high.blocks(p, me.core)], fc_own.at[p], own_sem.at[p])
            for p in range(2)
        ]

    def weight(n):
        return w_ref[n].reshape(BLOCK, BLOCK)

    def vec(row):
        return both_halves(vec_ref, row)

    def note(row, values):
        small_ref[row : row + 1, :] += col_sum(values)

    @pl.when(step == 0)
    def _():
        start(own_copies())
        peers = [me.other_core()]
        peers += [me.along(axis, s) for axis in ("x", "y", "z") for s in (1, 2, 3)]
        greet(peers)
        high.step(0)
        place_ref[...] = place_matrix().astype(BF16)
        hmask_ref[...] = head_mask().astype(BF16)
        small_ref[...] = small_in[...]
        pair_ref[...] = jnp.zeros_like(pair_ref)

    @pl.when(step == 1)
    def _():
        for copy in own_copies():
            copy.wait()

    for at_step, moves in PLAN:
        @pl.when(step == at_step)
        def _(moves=moves):
            for group, number in moves:
                (high if group == "high" else low).step(number)

    @pl.when(step < images)
    def _():
        hmask = hmask_ref[...]
        rows = pl.ds(pl.multiple_of(step * (4 * ROWS), 16), 4 * ROWS)

        def keep(block, values):
            acts_s[block] = values

        qkv_s[...] = qkv_ref[0]
        prob_s[...] = prob_ref[0]
        gmid_s[...] = gmid_ref[0]
        keep(4, att_ref[0])
        keep(0, normed_ref[0])
        grad_middle = gmid_s[...]
        proj_low = grad_middle.astype(BF16)
        keep(5, proj_low)
        grad_att = nt(proj_low, weight(3))
        for w in range(4):
            gatt_s[w] = pad_window(grad_att[w * ROWS : (w + 1) * ROWS]).astype(BF16)
        groups = range(heads // 4)
        ats = [slice(g * 128, (g + 1) * 128) for g in groups]
        wides = [slice(g * 4 * WPAD, (g + 1) * 4 * WPAD) for g in groups]
        for w in range(4):
            here = slice(w * ROWS, (w + 1) * ROWS)

            def part(n, g, w=w):
                return qkv_s[w, :, n * BLOCK + g * 128 : n * BLOCK + (g + 1) * 128]

            spread_grad = [spread(gatt_s[w, :, ats[g]], hmask) for g in groups]
            grad_probs = [nt(part(2, g), spread_grad[g]) for g in groups]
            grad_v = [nn(prob_s[w, :, wides[g]].astype(BF16), spread_grad[g]) for g in groups]
            scores_low = []
            for g in groups:
                probs = prob_s[w, :, wides[g]]
                weighted = probs * grad_probs[g]
                grad_scores = weighted - probs * jnp.sum(weighted, 0, keepdims=True)
                pair_ref[:, wides[g]] += grad_scores
                scores_low.append(grad_scores.astype(BF16))
            grad_k = [nn(scores_low[g], spread(part(0, g), hmask)) for g in groups]
            grad_q = [tn(scores_low[g], part(1, g)) for g in groups]
            for g in groups:
                dqkv_s[here, 2 * BLOCK + g * 128 : 2 * BLOCK + (g + 1) * 128] = grad_v[g][:ROWS]
                dqkv_s[here, BLOCK + g * 128 : BLOCK + (g + 1) * 128] = grad_k[g][:ROWS]
                dqkv_s[here, g * 128 : (g + 1) * 128] = fold(grad_q[g], hmask) * scale
        for n in range(3):
            part = dqkv_s[:, n * BLOCK : (n + 1) * BLOCK]
            if n == 0:
                note(2, part)
            if n == 2:
                note(3, part)
            keep(1 + n, part.astype(BF16))
        for block in range(6):
            acts[block, rows, :] = acts_s[block]

    @pl.when(step > images)
    def _():
        rows = pl.ds(pl.multiple_of((step - images - 1) * (4 * ROWS), 16), 4 * ROWS)
        unit, rate = normalize(nn(place_ref[...], tok_ref[0]))
        grad = None
        for n in range(3):
            term = nt(acts[1 + n, rows, :], weight(n))
            grad = term if n == 0 else grad + term
        note(0, grad * unit)
        note(1, grad)
        tg_ref[0] = gmid_ref[0] + norm_back(grad, unit, rate, vec(0))

    small_bufs = {"x": small_x, "y": small_y, "z": small_z}
    small_base = 72

    def small_cores():
        part = small_pair.at[me.core]
        return [remote(part, part, *sems, small_base, me.other_core())]

    def small_copies(axis):
        part = small_bufs[axis].at[me.at[axis]]
        first = small_base + 1 + 3 * "xyz".index(axis)
        return [remote(part, part, *sems, first + s - 1, me.along(axis, s)) for s in (1, 2, 3)]

    def small_across():
        copies = []
        for s in (1, 2, 3):
            peer = lax.rem(me.at["x"] + s, SIDE_CHIPS)
            source, target = small_halves.at[peer // 2], small_x.at[me.at["x"]]
            copies.append(remote(source, target, *sems, small_base + s, me.along("x", s)))
        return copies

    def small_start(axis, values):
        small_bufs[axis][pl.ds(me.at[axis], 1)] = values[None]
        start(small_copies(axis))

    def small_sum(axis):
        arrived(small_across() if axis == "x" else small_copies(axis))
        buf = small_bufs[axis]
        return (buf[0] + buf[1]) + (buf[2] + buf[3])

    @pl.when(step == images)
    def _():
        for p in range(2):
            for n in (2 * p, 2 * p + 1):
                left, right = ((0, 1), (0, 2), (0, 3), (4, 5))[n]
                low_ref[n] = tn(acts[left], acts[right]).astype(BF16).reshape(2, 256, BLOCK)
            start(low.cores(p))
            if p == 0:
                for number in DURING_GRADS:
                    high.step(number)
        half = WPAD // 2
        for h in range(heads):
            at = slice(h * WPAD, (h + 1) * WPAD)
            both = jnp.concatenate([pair_ref[:half, at], pair_ref[half:, at]], 1)
            fold_s[pl.ds(h, half, stride=heads), :] = both

        def body(j, total):
            values = fold_s[pl.ds(pl.multiple_of(j * heads, heads), heads), :]
            upper = values.astype(BF16)
            rest = (values - upper.astype(F32)).astype(BF16)
            return total + nt(jnp.concatenate([upper, rest], 0), pair_rows(rel_ref, j))

        total = lax.fori_loop(0, half, body, jnp.zeros((2 * heads, 256), F32), unroll=4)
        table = total[:heads] + total[heads:]
        small_ref[12 : 12 + heads // 2, :256] = table[: heads // 2]
        small_ref[12 : 12 + heads // 2, 256:] = table[heads // 2 :]

    @pl.when(step == 2 * images)
    def _():
        small_pair[pl.ds(me.core, 1)] = small_ref[...][None]
        start(small_cores())
        high.step(7)
        high_out = pltpu.make_async_copy(f_ref.at[pl.ds(4, 8)], f_out.at[pl.ds(4, 8)], out_sem.at[0])
        high_out.start()
        arrived(small_cores())
        small_total = small_pair[0] + small_pair[1]
        small_halves[0] = small_total[:, :256]
        small_halves[1] = small_total[:, 256:]
        start(small_across())
        small_x[pl.ds(me.at["x"], 1)] = small_halves[pl.ds(me.hi, 1)]
        low.step(2)
        small_start("y", small_sum("x"))
        low.step(3)
        small_start("z", small_sum("y"))
        low.step(4)
        small_out[...] = small_sum("z")
        low.step(5)
        low.step(6)
        low.step(7)
        low_out = pltpu.make_async_copy(f_ref.at[pl.ds(0, 4)], f_out.at[pl.ds(0, 4)], out_sem.at[1])
        low_out.start()
        high_out.wait()
        low_out.wait()
        high.all_sent()
        low.all_sent()
        sent(small_cores())
        sent(small_across())
        sent(small_copies("y"))
        sent(small_copies("z"))


PLAN = (
    (1, (("high", 1),)),
    (4, (("high", 2),)),
    (5, (("high", 3),)),
    (6, (("high", 4),)),
    (8, (("low", 1),)),
    (9, (("high", 6),)),
)
DURING_GRADS = (5,)


def run_back(qkv, prob, normed, att, gmid, tokens, weights, vecs, rel_rows, small, fc):
    images, tokens_image, width = tokens.shape
    heads = prob.shape[3] // WPAD
    rows = 4 * ROWS
    vmem = pl.BlockSpec(memory_space=pltpu.VMEM)
    far = pl.BlockSpec(memory_space=pltpu.HBM)

    def per_image(shape, index):
        return pl.BlockSpec((1,) + shape, lambda b: (index(b),) + (0,) * len(shape))

    def early(b):
        return jnp.minimum(b, images - 1)

    def late(b):
        return jnp.maximum(b - images - 1, 0)

    def twice(b):
        return jnp.where(b < images, b, late(b))

    def whole(array):
        return pl.BlockSpec(array.shape, lambda b: (0,) * array.ndim, pipeline_mode=pl.Buffered(1))

    def reduce_scratch(count):
        return [
            pltpu.VMEM((2, count, 2, 256, BLOCK), BF16),
            pltpu.VMEM((2, count, 2, 256, BLOCK), BF16),
            pltpu.VMEM((2, 3, count, 2, 64, BLOCK), BF16),
            pltpu.VMEM((2, count, 2, 64, BLOCK), BF16),
            pltpu.VMEM((2, 3, count, 2, 16, BLOCK), BF16),
            pltpu.VMEM((2, count, 2, 16, BLOCK), BF16),
            pltpu.VMEM((2, 4, count, 16, BLOCK), BF16),
        ]

    return pl.pallas_call(
        partial(back_kernel, images, heads),
        grid=(2 * images + 1,),
        in_specs=[
            per_image(qkv.shape[1:], early),
            per_image(prob.shape[1:], early),
            per_image(normed.shape[1:], early),
            per_image(att.shape[1:], early),
            per_image(gmid.shape[1:], twice),
            per_image((tokens_image, width), late),
            whole(weights),
            whole(vecs),
            whole(rel_rows),
            whole(small),
            far,
        ],
        out_specs=[per_image((rows, width), late), far, vmem],
        out_shape=[
            jax.ShapeDtypeStruct((images, rows, width), F32),
            jax.ShapeDtypeStruct((12, 256, BLOCK), BF16),
            jax.ShapeDtypeStruct((24, 256), F32),
        ],
        scratch_shapes=[
            pltpu.VMEM((4, WPAD, 3 * BLOCK), BF16),
            pltpu.VMEM((4, WPAD, heads * WPAD), F32),
            pltpu.VMEM((rows, width), F32),
            pltpu.VMEM((6, rows, BLOCK), BF16),
            pltpu.VMEM((12, 256, BLOCK), BF16),
            pltpu.VMEM((rows, tokens_image), BF16),
            pltpu.VMEM((4 * WPAD, 128), BF16),
            pltpu.VMEM((24, BLOCK), F32),
            pltpu.VMEM((WPAD, heads * WPAD), F32),
            pltpu.VMEM((heads * WPAD // 2, 128), F32),
            pltpu.VMEM((4, WPAD, BLOCK), BF16),
            pltpu.VMEM((rows, 3 * BLOCK), F32),
            pltpu.VMEM((6, images * rows, BLOCK), BF16),
            pltpu.VMEM((4, 2, 256, BLOCK), BF16),
            pltpu.VMEM((2, 2, 2, 256, BLOCK), BF16),
        ]
        + reduce_scratch(2)
        + reduce_scratch(1)
        + [
            pltpu.VMEM((2, 24, BLOCK), F32),
            pltpu.VMEM((2, 24, 256), F32),
            pltpu.VMEM((4, 24, 256), F32),
            pltpu.VMEM((4, 24, 256), F32),
            pltpu.VMEM((4, 24, 256), F32),
            pltpu.SemaphoreType.DMA((2,)),
            pltpu.SemaphoreType.DMA((2,)),
            pltpu.SemaphoreType.DMA((82,)),
            pltpu.SemaphoreType.DMA((82,)),
        ],
        compiler_params=pltpu.CompilerParams(
            collective_id=1, has_side_effects=True, vmem_limit_bytes=56 * 1024 * 1024
        ),
        name="back",
    )(qkv, prob, normed, att, gmid, tokens, weights, vecs, rel_rows, small, fc)


def finish_kernel(
    per_step,
    out_win, tg_win, f_ref, small_ref,
    out_ref, tg_ref, n1g, n1b, qkv, qb, vb, table, proj, pb, n2g, n2b, fc1, f1b, fc2, f2b,
    back_ref, wide, sem,
):
    step = pl.program_id(0)
    targets = []
    for n in range(12):
        if n < 3:
            targets.append([(slice(None), qkv.at[:, pl.ds(n * BLOCK, BLOCK)])])
        elif n == 3:
            targets.append([(slice(None), proj)])
        elif n < 8:
            targets.append(
                [
                    (pl.ds(half * 256, 256), fc1.at[:, pl.ds(half * 1024 + (n - 4) * 256, 256)])
                    for half in range(2)
                ]
            )
        else:
            targets.append([(slice(None), fc2.at[pl.ds((n - 8) * 256, 256)])])

    def stores(n):
        return [
            pltpu.make_async_copy(wide.at[n, :, lanes], target, sem.at[n, i])
            for i, (lanes, target) in enumerate(targets[n])
        ]

    for n in range(12):
        @pl.when(step == n // per_step)
        def _(n=n):
            wide[n] = f_ref[n % per_step].astype(F32)
            start(stores(n))

    @pl.when(step == 0)
    def _():
        back_ref[...] = back_matrix().astype(BF16)
        for row, ref in enumerate((n1g, n1b, qb, vb, pb, n2g, n2b, f2b)):
            ref[...] = small_ref[row : row + 1, :].reshape(256)
        for m in range(4):
            f1b[pl.ds(m * 256, 256)] = small_ref[8 + m : 9 + m, :].reshape(256)
        table[...] = small_ref[12:20, 0 : table.shape[1]]

    out_ref[0] = nn(back_ref[...], out_win[0]).astype(BF16)
    total = tg_win[0]
    upper = total.astype(BF16)
    rest = (total - upper.astype(F32)).astype(BF16)
    tg_ref[0] = nn(back_ref[...], upper) + nn(back_ref[...], rest)

    @pl.when(step == pl.num_programs(0) - 1)
    def _():
        for n in range(12):
            for copy in stores(n):
                copy.wait()


def finish(out_win, tg_win, grads, small, table_rows, heads_here):
    images, rows, width = out_win.shape
    tokens_image = SIDE * SIDE
    per_step = -(-12 // images)
    last_block = 12 // per_step - 1
    vmem = pl.BlockSpec(memory_space=pltpu.VMEM)
    far = pl.BlockSpec(memory_space=pltpu.HBM)
    vector, hidden = ((256,), vmem), ((1024,), vmem)
    image = pl.BlockSpec((1, rows, width), lambda b: (b, 0, 0))
    image_out = pl.BlockSpec((1, tokens_image, width), lambda b: (b, 0, 0))
    outs = [
        vector, vector, ((256, 3 * BLOCK), far), vector, vector, ((heads_here, table_rows), vmem),
        ((256, BLOCK), far), vector, vector, vector, ((256, 4 * BLOCK), far), hidden,
        ((1024, BLOCK), far), vector,
    ]
    return pl.pallas_call(
        partial(finish_kernel, per_step),
        grid=(images,),
        in_specs=[
            image,
            image,
            pl.BlockSpec((per_step, 256, BLOCK), lambda b: (jnp.minimum(b, last_block), 0, 0)),
            pl.BlockSpec(small.shape, lambda b: (0, 0)),
        ],
        out_specs=[image_out, image_out] + [spec for _, spec in outs],
        out_shape=[
            jax.ShapeDtypeStruct((images, tokens_image, width), BF16),
            jax.ShapeDtypeStruct((images, tokens_image, width), F32),
        ]
        + [jax.ShapeDtypeStruct(shape, F32) for shape, _ in outs],
        scratch_shapes=[
            pltpu.VMEM((tokens_image, rows), BF16),
            pltpu.VMEM((12, 256, BLOCK), F32),
            pltpu.SemaphoreType.DMA((12, 2)),
        ],
        compiler_params=pltpu.CompilerParams(vmem_limit_bytes=40 * 1024 * 1024),
        name="finish",
    )(out_win, tg_win, grads, small)


def local(
    tokens, image_counts, shift_mask, rel_index, norm1_gain, norm1_bias, qkv_weight, q_bias, v_bias,
    rel_table, proj_weight, proj_bias, norm2_gain, norm2_bias, fc1_weight, fc1_bias, fc2_weight,
    fc2_bias, out_grad,
):
    table_rows, heads_here = rel_table.shape
    qkv, prob, normed, att, block_out, gmid, fc, small, vecs, rel_rows, low_weights = run_front(
        [qkv_weight, proj_weight, fc1_weight, fc2_weight],
        [norm1_gain, norm1_bias, q_bias, v_bias, proj_bias, norm2_gain, norm2_bias, fc2_bias],
        fc1_bias, rel_table.T, rel_index, shift_mask.transpose(1, 0, 2), tokens, out_grad, image_counts,
    )
    tokens_grad, grads, small = run_back(
        qkv, prob, normed, att, gmid, tokens, low_weights, vecs, rel_rows, small, fc.reshape(8, 2, 256, BLOCK)
    )
    outs = finish(block_out, tokens_grad, grads, small, table_rows, heads_here)
    return (*outs[:7], outs[7].T, *outs[8:])


def solution(mesh):
    split = P(("replica", "shard"), None, None)
    vector, matrix, table = P("shard"), P("shard", None), P(None, "shard")
    return jax.shard_map(
        local,
        mesh=mesh,
        in_specs=(
            split, P(("replica", "shard")), P(), P(), vector, vector, matrix, vector, vector, table,
            matrix, vector, vector, vector, matrix, vector, matrix, vector, split,
        ),
        out_specs=(
            split, split, vector, vector, matrix, vector, vector, table, matrix, vector, vector,
            vector, matrix, vector, matrix, vector,
        ),
        check_vma=False,
    )
```

```python
from functools import partial

import jax
import jax.numpy as jnp
from jax import lax
from jax.experimental import pallas as pl
from jax.experimental.pallas import tpu as pltpu
from jax.sharding import PartitionSpec as P

WIN = 7
SIDE = 14
SHIFT = 3
EPSILON = 1e-05
MASKED = -1e30
WTOK = WIN * WIN
ROWS = 56
WPAD = 64
BLOCK = 512
F32 = jnp.float32
BF16 = jnp.bfloat16


def nn(left, right):
    return jnp.dot(left, right, preferred_element_type=F32)


def nt(left, right):
    return lax.dot_general(left, right, (((1,), (1,)), ((), ())), preferred_element_type=F32)


def tn(left, right):
    return lax.dot_general(left, right, (((0,), (0,)), ((), ())), preferred_element_type=F32)


def normalize(values):
    center = values - jnp.mean(values, -1, keepdims=True)
    rate = lax.rsqrt(jnp.mean(center * center, -1, keepdims=True) + EPSILON)
    return center * rate, rate


def norm_back(grad, unit, rate, gain):
    scaled = grad * gain
    return rate * (
        scaled
        - jnp.mean(scaled, -1, keepdims=True)
        - unit * jnp.mean(scaled * unit, -1, keepdims=True)
    )


def normal_parts(v):
    bell = jnp.exp2(v * v * -0.7213475204444817)
    t = 1.0 / (1.0 + 0.23164189 * jnp.abs(v))
    tail = t * (
        0.127414796
        + t * (-0.142248368 + t * (0.7107068705 + t * (-0.7265760135 + t * 0.5307027145)))
    )
    half = tail * bell
    return jnp.where(v < 0, half, 1.0 - half), 0.3989422804014327 * bell


def col_sum(values):
    return jnp.sum(values, 0, keepdims=True)


MESH = pl.DeviceIdType.MESH
SIDE_CHIPS = 4


class Place:
    def __init__(self):
        replica = lax.axis_index("replica")
        self.hi = lax.axis_index("shard")
        self.core = lax.rem(replica, 2)
        self.at = {
            "x": self.hi * 2 + lax.rem(replica // 2, 2),
            "z": lax.rem(replica // 4, SIDE_CHIPS),
            "y": replica // 16,
        }
        self.lo = lax.rem(replica // 2, 2)

    def id_of(self, core=None, **at):
        place = dict(self.at, **at)
        core = self.core if core is None else core
        lo, hi = lax.rem(place["x"], 2), place["x"] // 2
        return (((place["y"] * SIDE_CHIPS + place["z"]) * 2 + lo) * 2 + core, hi)

    def other_core(self):
        return self.id_of(core=1 - self.core)

    def along(self, axis, step):
        return self.id_of(**{axis: lax.rem(self.at[axis] + step, SIDE_CHIPS)})


def greet(devices):
    barrier = pltpu.get_barrier_semaphore()
    for device in devices:
        pl.semaphore_signal(barrier, inc=1, device_id=device, device_id_type=MESH)
    pl.semaphore_wait(barrier, len(devices))


def pad_window(values):
    return jnp.concatenate([values, jnp.zeros((WPAD - ROWS, values.shape[1]), F32)], 0)


def source_of(row):
    window = jnp.floor((row + 0.5) / ROWS)
    cell = row - window * ROWS
    across = jnp.floor((window + 0.5) / 2)
    down = jnp.floor((cell + 0.5) / WIN)
    i = across * WIN + down + SHIFT
    j = (window - 2 * across) * WIN + (cell - down * WIN) + SHIFT
    i = jnp.where(i >= SIDE, i - SIDE, i)
    j = jnp.where(j >= SIDE, j - SIDE, j)
    return jnp.where(cell < WTOK, i * SIDE + j, -1.0)


def iota(shape, axis):
    return lax.broadcasted_iota(jnp.int32, shape, axis).astype(F32)


def place_matrix():
    rows, tokens = 4 * ROWS, SIDE * SIDE
    return jnp.where(source_of(iota((rows, tokens), 0)) == iota((rows, tokens), 1), 1.0, 0.0)


def back_matrix():
    rows, tokens = 4 * ROWS, SIDE * SIDE
    return jnp.where(source_of(iota((tokens, rows), 1)) == iota((tokens, rows), 0), 1.0, 0.0)


def head_mask():
    shape = (4 * WPAD, 128)
    row, lane = iota(shape, 0), iota(shape, 1)
    return jnp.where(jnp.floor((row + 0.5) / WPAD) == jnp.floor((lane + 0.5) / 32), 1.0, 0.0)


def pair_rows(rel_ref, j):
    return jnp.where(iota((256, 128), 0) == rel_ref[pl.ds(j, 1), :], 1.0, 0.0).astype(BF16)


def spread(part, hmask):
    return jnp.concatenate([part] * 4, 0) * hmask


def fold(full, hmask):
    full = full * hmask.astype(F32)
    total = full[:WPAD]
    for h in range(1, 4):
        total = total + full[h * WPAD : (h + 1) * WPAD]
    return total[:ROWS]


def both_halves(vec_ref, row):
    return jnp.concatenate([vec_ref[0, row : row + 1, :], vec_ref[1, row : row + 1, :]], 1)


def remote(source, target, send_sem, recv_sem, number, device):
    return pltpu.make_async_remote_copy(
        src_ref=source,
        dst_ref=target,
        send_sem=send_sem.at[number],
        recv_sem=recv_sem.at[number],
        device_id=device,
        device_id_type=MESH,
    )


def start(copies):
    for copy in copies:
        copy.start()


def arrived(copies):
    for copy in copies:
        copy.wait_recv()


def sent(copies):
    for copy in copies:
        copy.wait_send()


class Gather:
    SEMAPHORES = 37

    def __init__(self, me, w_ref, v_ref, send_sem, recv_sem):
        self.me, self.w, self.v = me, w_ref, v_ref
        self.sems = (send_sem, recv_sem)

    def flows(self, group):
        count = 1 + group
        for flow, (first, second) in enumerate((("z", "y"), ("y", "z"))):
            block = 4 * group + 2 * count * flow + self.me.core * count
            yield 16 * group + 8 * flow, pl.ds(block, count), first, second

    def copy(self, number, part, device):
        return remote(part, part, *self.sems, number, device)

    def facing(self):
        return self.me.id_of(x=3 - self.me.at["x"])

    def cross(self, group):
        me = self.me
        return [
            self.copy(
                number,
                self.w.at[blocks, me.hi, pl.ds(me.at[second] * 64 + me.at[first] * 16, 16)],
                self.facing(),
            )
            for number, blocks, first, second in self.flows(group)
        ]

    def vectors(self):
        return [self.copy(32, self.v.at[self.me.hi], self.facing())]

    def first(self, group):
        me = self.me
        return [
            self.copy(
                number + step,
                self.w.at[blocks, 1 - me.hi, pl.ds(me.at[second] * 64 + me.at[first] * 16, 16)],
                me.along(first, step),
            )
            for number, blocks, first, second in self.flows(group)
            for step in (1, 2, 3)
        ]

    def second(self, group):
        me = self.me
        return [
            self.copy(
                number + 3 + step,
                self.w.at[blocks, 1 - me.hi, pl.ds(me.at[second] * 64, 64)],
                me.along(second, step),
            )
            for number, blocks, first, second in self.flows(group)
            for step in (1, 2, 3)
        ]

    def last(self, group):
        return [
            self.copy(number + 7, self.w.at[blocks, 1 - self.me.hi], self.me.other_core())
            for number, blocks, _, _ in self.flows(group)
        ]


def front_kernel(
    images,
    count_ref,
    qkv_w, proj_w, fc1_w, fc2_w, n1g, n1b, qb, vb, pb, n2g, n2b, f2b, f1b, table_w, index_w, mask_w,
    tok_hbm, up_ref,
    qkv_ref, prob_ref, normed_ref, att_ref, out_ref, gmid_ref, fc_ref, small_ref, vec_out, rel_ref, low_ref,
    vec_ref, w_ref, acts, bias_ref, place_ref, hmask_ref, att_s, qkv_s, prob_s, acts_s, fc_send, fc_pair, tok_s, normed_s,
    v0, v1, v2, v3, v4, v5, v6, v7, v8, table_v, index_v, mask_v, square, square_mask, pairs,
    w_sem, in_sem, low_sem, send_sem, recv_sem,
):
    step = pl.program_id(0)
    me = Place()
    hi = me.hi
    gather = Gather(me, w_ref, vec_ref, send_sem, recv_sem)
    heads = table_w.shape[0] * 2
    scale = (up_ref.shape[2] // heads) ** (-0.5)

    def own_weights(group):
        pairs = []
        if group == 0:
            for n in range(3):
                pairs.append((qkv_w.at[:, pl.ds(n * BLOCK, BLOCK)], w_ref.at[n, hi]))
            pairs.append((proj_w, w_ref.at[3, hi]))
        else:
            for m in range(4):
                for half in range(2):
                    pairs.append(
                        (
                            fc1_w.at[:, pl.ds(half * 1024 + m * 256, 256)],
                            w_ref.at[4 + m, hi, :, pl.ds(half * 256, 256)],
                        )
                    )
                pairs.append((fc2_w.at[pl.ds(m * 256, 256)], w_ref.at[8 + m, hi]))
        return [
            pltpu.make_async_copy(source, target, w_sem.at[4 * group + i])
            for i, (source, target) in enumerate(pairs)
        ]

    def own_small():
        sources = (n1g, n1b, qb, vb, pb, n2g, n2b, f2b, f1b, table_w, index_w, mask_w)
        targets = (v0, v1, v2, v3, v4, v5, v6, v7, v8, table_v, index_v, mask_v)
        return [
            pltpu.make_async_copy(source, target, in_sem.at[i])
            for i, (source, target) in enumerate(zip(sources, targets))
        ]

    def token_copy():
        return pltpu.make_async_copy(tok_hbm, tok_s, low_sem.at[1])

    def low_copy():
        return pltpu.make_async_copy(w_ref.at[pl.ds(0, 4)], low_ref, low_sem.at[0])

    def weight(n):
        return w_ref[n].reshape(BLOCK, BLOCK)

    def vec(row):
        return both_halves(vec_ref, row)

    def note(row, values):
        small_ref[row : row + 1, :] += col_sum(values)

    @pl.when(step == 0)
    def _():
        small_copies = own_small()
        start(own_weights(0))
        start(small_copies)
        start(own_weights(1))
        token_copy().start()
        peers = [gather.facing(), me.other_core()]
        peers += [me.along(axis, s) for axis in ("y", "z") for s in (1, 2, 3)]
        greet(peers)
        for copy in own_weights(0):
            copy.wait()
        start(gather.cross(0))
        for copy in small_copies:
            copy.wait()
        rows = [ref[...].astype(F32).reshape(1, 256) for ref in (v0, v1, v2, v3, v4, v5, v6, v7)]
        rows += [v8[pl.ds(m * 256, 256)].astype(F32).reshape(1, 256) for m in range(4)]
        rows.append(jnp.zeros((4, 256), F32))
        vec_ref[pl.ds(hi, 1), 0:16] = jnp.concatenate(rows, 0)[None]
        heads_here, table_rows = table_v.shape
        vec_ref[pl.ds(hi, 1), 16:24] = jnp.zeros((1, 8, 256), F32)
        vec_ref[pl.ds(hi, 1), 16:24, 0:table_rows] = table_v[...].astype(F32)[None]
        start(gather.vectors())
        for copy in own_weights(1):
            copy.wait()
        start(gather.cross(1))
        arrived(gather.cross(0))
        start(gather.first(0))
        arrived(gather.cross(1))
        start(gather.first(1))
        square[...] = jnp.full((128, 128), -1.0, F32)
        square[0:WTOK, 0:WTOK] = index_v[...].astype(F32)
        turned = square[...].T
        half = WPAD // 2
        rel_ref[...] = jnp.concatenate([turned[:half, :WPAD], turned[half:WPAD, :WPAD]], 1)
        for w in range(4):
            square_mask[w] = jnp.where(iota((WPAD, WPAD), 0) < WTOK, 0.0, MASKED)
            square_mask[w, 0:WTOK, 0:WTOK] = jnp.where(mask_v[:, w, :] == 1, 0.0, -100.0)
        place_ref[...] = place_matrix().astype(BF16)
        hmask_ref[...] = head_mask().astype(BF16)
        small_ref[...] = jnp.zeros_like(small_ref)
        arrived(gather.first(0))
        start(gather.second(0))
        arrived(gather.first(1))
        start(gather.second(1))
        arrived(gather.vectors())
        vec_out[...] = vec_ref[...]
        table = jnp.concatenate([vec_ref[0, 16:24], vec_ref[1, 16:24]], 0).astype(BF16)

        def body(j, carry):
            pairs[pl.ds(pl.multiple_of(j * heads, heads), heads), :] = nn(table, pair_rows(rel_ref, j))
            return carry

        lax.fori_loop(0, half, body, 0, unroll=4)
        arrived(gather.second(0))
        start(gather.last(0))
        for h in range(heads):
            at = slice(h * WPAD, (h + 1) * WPAD)
            both = pairs[pl.ds(h, half, stride=heads), :]
            for w in range(4):
                bias_ref[w, :half, at] = both[:, :WPAD] + square_mask[w, :half]
                bias_ref[w, half:, at] = both[:, WPAD:] + square_mask[w, half:]
        token_copy().wait()

        def norm(b, carry):
            unit, _ = normalize(nn(place_ref[...], tok_s[b]))
            normed_s[b] = (unit * vec(0) + vec(1)).astype(BF16)
            return carry

        lax.fori_loop(0, images, norm, 0)
        arrived(gather.last(0))
        low_copy().start()

    @pl.when(step == SECOND_STEP)
    def _():
        arrived(gather.second(1))
        start(gather.last(1))

    @pl.when(step == images)
    def _():
        arrived(gather.last(1))

    @pl.when(step < images)
    def _():
        hmask = hmask_ref[...]
        normed = normed_s[step]
        for n in range(3):
            part = nn(normed, weight(n))
            if n == 0:
                part = (part + vec(2)) * scale
            if n == 2:
                part = part + vec(3)
            for w in range(4):
                qkv_s[w, :, n * BLOCK : (n + 1) * BLOCK] = pad_window(
                    part[w * ROWS : (w + 1) * ROWS]
                ).astype(BF16)
        for w in range(4):
            for g in range(heads // 4):
                at = slice(g * 128, (g + 1) * 128)
                wide = slice(g * 4 * WPAD, (g + 1) * 4 * WPAD)
                q = qkv_s[w, :, g * 128 : (g + 1) * 128]
                k = qkv_s[w, :, BLOCK + g * 128 : BLOCK + (g + 1) * 128]
                v = qkv_s[w, :, 2 * BLOCK + g * 128 : 2 * BLOCK + (g + 1) * 128]
                scores = nt(k, spread(q, hmask)) + bias_ref[w, :, wide]
                raised = jnp.exp(scores - jnp.max(scores, 0, keepdims=True))
                probs = raised * (1.0 / jnp.sum(raised, 0, keepdims=True))
                prob_s[w, :, wide] = probs
                att_s[w * ROWS : (w + 1) * ROWS, at] = fold(tn(probs.astype(BF16), v), hmask)
        att_ref[step] = att_s[...].astype(BF16)
        normed_ref[0] = normed
        qkv_ref[0] = qkv_s[...]
        prob_ref[0] = prob_s[...]

    @pl.when((step >= images) & (step < 2 * images))
    def _():
        image = step - images
        valid = (image < count_ref[0]).astype(F32)
        rows = pl.ds(pl.multiple_of(image * (4 * ROWS), 16), 4 * ROWS)

        def keep(block, values):
            acts[block, rows, :] = values

        middle = nn(place_ref[...], tok_s[image]) + (nn(att_ref[image], weight(3)) + vec(4))
        unit, rate = normalize(middle)
        normed = (unit * vec(5) + vec(6)).astype(BF16)
        keep(0, normed)
        upstream = nn(place_ref[...], up_ref[0]) * valid
        up_low = upstream.astype(BF16)
        keep(9, up_low)
        note(7, upstream)
        branch = None
        grad = None
        for c in range(4):
            pre = nn(normed, weight(4 + c)) + vec(8 + c)
            below, density = normal_parts(pre)
            act = (pre * below).astype(BF16)
            keep(5 + c, act)
            grad_pre = nt(up_low, weight(8 + c)) * (below + pre * density)
            note(8 + c, grad_pre)
            pre_low = grad_pre.astype(BF16)
            keep(1 + c, pre_low)
            first = nn(act, weight(8 + c))
            second = nt(pre_low, weight(4 + c))
            branch = first if c == 0 else branch + first
            grad = second if c == 0 else grad + second
        result = middle + (branch + vec(7))
        note(5, grad * unit)
        note(6, grad)
        grad_middle = upstream + norm_back(grad, unit, rate, vec(5))
        note(4, grad_middle)
        gmid_ref[0] = grad_middle
        out_ref[0] = (result * valid).astype(BF16)

    def grad_block(number, core):
        block = 4 * (number // 2) + 2 * core + lax.rem(number, 2)
        left = jnp.where(block < 4, 0, block + 1)
        right = jnp.where(block < 4, block + 1, 9)
        return tn(acts[left], acts[right])

    def pair_copy(number):
        return remote(
            fc_send.at[number], fc_pair.at[number], send_sem, recv_sem, 33 + number, me.other_core()
        )

    @pl.when((step >= 2 * images) & (step < 2 * images + 4))
    def _():
        number = step - 2 * images
        fc_send[number] = grad_block(number, 1 - me.core).astype(BF16)

    for number in range(4):
        @pl.when(step == 2 * images + number)
        def _(number=number):
            start([pair_copy(number)])

        @pl.when(step == 2 * images + 4 + number)
        def _(number=number):
            arrived([pair_copy(number)])

    @pl.when(step >= 2 * images + 4)
    def _():
        number = step - 2 * images - 4
        fc_ref[0] = (grad_block(number, me.core) + fc_pair[number].astype(F32)).astype(BF16)

    @pl.when(step == pl.num_programs(0) - 1)
    def _():
        for group in range(2):
            for copies in (gather.cross, gather.first, gather.second, gather.last):
                sent(copies(group))
        sent(gather.vectors())
        sent([pair_copy(number) for number in range(4)])
        low_copy().wait()


SECOND_STEP = 3


def run_front(matrices, vectors, hidden_bias, table, rel_index, shift_mask, tokens, out_grad, count):
    images, tokens_image, width = tokens.shape
    heads = table.shape[0] * 2
    rows = 4 * ROWS
    far = pl.BlockSpec(memory_space=pltpu.HBM)
    small = vectors + [hidden_bias, table, rel_index, shift_mask]

    def per_image(shape, index):
        return pl.BlockSpec((1,) + shape, lambda b: (index(b),) + (0,) * len(shape))

    def whole(shape):
        return pl.BlockSpec(shape, lambda b: (0,) * len(shape), pipeline_mode=pl.Buffered(1))

    def early(b):
        return jnp.minimum(b, images - 1)

    def late(b):
        return jnp.clip(b - images, 0, images - 1)

    return pl.pallas_call(
        partial(front_kernel, images),
        grid=(2 * images + 8,),
        in_specs=[pl.BlockSpec(memory_space=pltpu.SMEM)]
        + [far] * (4 + len(small))
        + [far, per_image((tokens_image, width), late)],
        out_specs=[
            per_image((4, WPAD, 3 * BLOCK), early),
            per_image((4, WPAD, heads * WPAD), early),
            per_image((rows, width), early),
            whole((images, rows, width)),
            per_image((rows, width), late),
            per_image((rows, width), late),
            per_image((BLOCK, BLOCK), lambda b: jnp.maximum(b - 2 * images - 4, 0)),
            whole((24, BLOCK)),
            whole((2, 24, 256)),
            whole((WPAD // 2, 2 * WPAD)),
            far,
        ],
        out_shape=[
            jax.ShapeDtypeStruct((images, 4, WPAD, 3 * BLOCK), BF16),
            jax.ShapeDtypeStruct((images, 4, WPAD, heads * WPAD), F32),
            jax.ShapeDtypeStruct((images, rows, width), BF16),
            jax.ShapeDtypeStruct((images, rows, width), BF16),
            jax.ShapeDtypeStruct((images, rows, width), BF16),
            jax.ShapeDtypeStruct((images, rows, width), F32),
            jax.ShapeDtypeStruct((4, BLOCK, BLOCK), BF16),
            jax.ShapeDtypeStruct((24, BLOCK), F32),
            jax.ShapeDtypeStruct((2, 24, 256), F32),
            jax.ShapeDtypeStruct((WPAD // 2, 2 * WPAD), F32),
            jax.ShapeDtypeStruct((4, 2, 256, BLOCK), BF16),
        ],
        scratch_shapes=[
            pltpu.VMEM((2, 24, 256), F32),
            pltpu.VMEM((12, 2, 256, BLOCK), BF16),
            pltpu.VMEM((10, images * rows, BLOCK), BF16),
            pltpu.VMEM((4, WPAD, heads * WPAD), F32),
            pltpu.VMEM((rows, tokens_image), BF16),
            pltpu.VMEM((4 * WPAD, 128), BF16),
            pltpu.VMEM((rows, BLOCK), F32),
            pltpu.VMEM((4, WPAD, 3 * BLOCK), BF16),
            pltpu.VMEM((4, WPAD, heads * WPAD), F32),
            pltpu.VMEM((10, rows, BLOCK), BF16),
            pltpu.VMEM((4, BLOCK, BLOCK), BF16),
            pltpu.VMEM((4, BLOCK, BLOCK), BF16),
            pltpu.VMEM(tokens.shape, BF16),
            pltpu.VMEM((images, rows, BLOCK), BF16),
        ]
        + [pltpu.VMEM(item.shape, item.dtype) for item in small]
        + [
            pltpu.VMEM((128, 128), F32),
            pltpu.VMEM((4, WPAD, WPAD), F32),
            pltpu.VMEM((heads * WPAD // 2, 2 * WPAD), F32),
            pltpu.SemaphoreType.DMA((16,)),
            pltpu.SemaphoreType.DMA((len(small),)),
            pltpu.SemaphoreType.DMA((2,)),
            pltpu.SemaphoreType.DMA((Gather.SEMAPHORES,)),
            pltpu.SemaphoreType.DMA((Gather.SEMAPHORES,)),
        ],
        compiler_params=pltpu.CompilerParams(
            collective_id=0, has_side_effects=True, vmem_limit_bytes=56 * 1024 * 1024
        ),
        name="front",
    )(count, *matrices, *small, tokens, out_grad)


class Reduce:
    SEMAPHORES = 36

    def __init__(self, me, sums, got, sum_one, got_one, sum_two, got_two, f_ref, first_block, sems, base):
        self.me, self.sums = me, sums
        self.got, self.sum_one, self.got_one = got, sum_one, got_one
        self.sum_two, self.got_two, self.f_ref = sum_two, got_two, f_ref
        self.first_block, self.sems, self.base = first_block, sems, base
        self.count = sums.shape[1]

    def axes(self, p):
        return (("y", "z"), ("z", "y"))[p]

    def copy(self, p, number, source, target, device):
        return remote(source, target, *self.sems, self.base + 18 * p + number, device)

    def target(self, p):
        return pl.ds(self.first_block + (2 * p + self.me.core) * self.count, self.count)

    def scatter(self, p, stage):
        me, axis = self.me, self.axes(p)[stage]
        rows = (64, 16)[stage]
        source, target = ((self.sums, self.got), (self.sum_one, self.got_one))[stage]
        return [
            self.copy(
                p,
                1 + 3 * stage + s - 1,
                source.at[p, :, :, pl.ds(lax.rem(me.at[axis] + s, SIDE_CHIPS) * rows, rows)],
                target.at[p, s - 1],
                me.along(axis, s),
            )
            for s in (1, 2, 3)
        ]

    def add(self, p, stage):
        arrived(self.scatter(p, stage))
        rows = (64, 16)[stage]
        source, got, target = (
            (self.sums, self.got, self.sum_one),
            (self.sum_one, self.got_one, self.sum_two),
        )[stage]
        at = pl.ds(pl.multiple_of(self.me.at[self.axes(p)[stage]] * rows, 16), rows)
        for b in range(self.count):
            for half in range(2):
                total = source[p, b, half, at, :].astype(F32)
                for s in range(3):
                    total = total + got[p, s, b, half].astype(F32)
                target[p, b, half] = total.astype(BF16)

    def across(self, p):
        me = self.me
        copies = []
        for s in (1, 2, 3):
            peer = lax.rem(me.at["x"] + s, SIDE_CHIPS)
            copies.append(
                self.copy(
                    p, 6 + s, self.sum_two.at[p, :, peer // 2], self.got_two.at[p, me.at["x"]], me.along("x", s)
                )
            )
        return copies

    def keep_own(self, p):
        for b in range(self.count):
            self.got_two[p, pl.ds(self.me.at["x"], 1), b] = self.sum_two[p, b, pl.ds(self.me.hi, 1)]

    def place(self, p):
        first, second = self.axes(p)
        return self.me.at[first] * 64, self.me.at[first] * 64 + self.me.at[second] * 16

    def add_across(self, p):
        arrived(self.across(p))
        _, row = self.place(p)
        at = pl.ds(pl.multiple_of(row, 16), 16)
        for b in range(self.count):
            parts = [self.got_two[p, x, b].astype(F32) for x in range(4)]
            total = (parts[0] + parts[1]) + (parts[2] + parts[3])
            block = self.first_block + (2 * p + self.me.core) * self.count + b
            self.f_ref[pl.ds(block, 1), at] = total.astype(BF16)[None]

    def back(self, p, stage):
        outer, inner = self.place(p)
        axis = self.axes(p)[stage]
        at = pl.ds(outer, 64) if stage == 0 else pl.ds(inner, 16)
        part = self.f_ref.at[self.target(p), at]
        return [
            self.copy(p, 10 + 3 * (1 - stage) + s - 1, part, part, self.me.along(axis, s)) for s in (1, 2, 3)
        ]

    def last(self, p):
        part = self.f_ref.at[self.target(p)]
        return [self.copy(p, 16, part, part, self.me.other_core())]

    def step(self, number):
        for p in range(2):
            if number == 1:
                start(self.scatter(p, 0))
            elif number == 2:
                self.add(p, 0)
                start(self.scatter(p, 1))
            elif number == 3:
                self.add(p, 1)
                start(self.across(p))
                self.keep_own(p)
            elif number == 4:
                self.add_across(p)
                start(self.back(p, 1))
            elif number == 5:
                arrived(self.back(p, 1))
                start(self.back(p, 0))
            elif number == 6:
                arrived(self.back(p, 0))
                start(self.last(p))
            else:
                arrived(self.last(p))

    def all_sent(self):
        for p in range(2):
            for stage in range(2):
                sent(self.scatter(p, stage))
                sent(self.back(p, stage))
            sent(self.across(p))
            sent(self.last(p))


def back_kernel(
    images,
    heads,
    qkv_ref, prob_ref, normed_ref, att_ref, gmid_ref, tok_ref, w_ref, vec_ref, rel_ref, small_in, fc_ref,
    tg_ref, f_out, small_out,
    qkv_s, prob_s, gmid_s, acts_s, f_ref, place_ref, hmask_ref, small_ref, pair_ref, fold_s, gatt_s, dqkv_s, acts,
    fc_sums, fc_got, fc_sum_one, fc_got_one, fc_sum_two, fc_got_two,
    low_send, low_own, lo_pair, lo_sums, lo_got, lo_sum_one, lo_got_one, lo_sum_two, lo_got_two,
    small_pair, small_halves, small_x, small_y, small_z, own_sem, out_sem, send_sem, recv_sem,
):
    step = pl.program_id(0)
    me = Place()
    scale = (tok_ref.shape[2] // heads) ** (-0.5)
    sems = (send_sem, recv_sem)
    high = Reduce(me, fc_sums, fc_got, fc_sum_one, fc_got_one, fc_sum_two, fc_got_two, f_ref, 4, sems, 0)
    low = Reduce(me, lo_sums, lo_got, lo_sum_one, lo_got_one, lo_sum_two, lo_got_two, f_ref, 0, sems, 36)

    def own_copies():
        return [
            pltpu.make_async_copy(fc_ref.at[pl.ds(2 * p, 2)], fc_sums.at[p], own_sem.at[p])
            for p in range(2)
        ]

    def low_pair(p):
        return remote(low_send.at[p], lo_pair.at[p], *sems, 36 + 18 * p, me.other_core())

    def weight(n):
        return w_ref[n].reshape(BLOCK, BLOCK)

    def vec(row):
        return both_halves(vec_ref, row)

    def note(row, values):
        small_ref[row : row + 1, :] += col_sum(values)

    @pl.when(step == 0)
    def _():
        start(own_copies())
        peers = [me.other_core()]
        peers += [me.along(axis, s) for axis in ("x", "y", "z") for s in (1, 2, 3)]
        greet(peers)
        for copy in own_copies():
            copy.wait()
        high.step(1)
        place_ref[...] = place_matrix().astype(BF16)
        hmask_ref[...] = head_mask().astype(BF16)
        small_ref[...] = small_in[...]
        pair_ref[...] = jnp.zeros_like(pair_ref)

    for at_step, moves in PLAN:
        @pl.when(step == at_step)
        def _(moves=moves):
            for group, number in moves:
                (high if group == "high" else low).step(number)

    @pl.when(step < images)
    def _():
        hmask = hmask_ref[...]
        rows = pl.ds(pl.multiple_of(step * (4 * ROWS), 16), 4 * ROWS)

        def keep(block, values):
            acts_s[block] = values

        qkv_s[...] = qkv_ref[0]
        prob_s[...] = prob_ref[0]
        gmid_s[...] = gmid_ref[0]
        keep(4, att_ref[0])
        keep(0, normed_ref[0])
        grad_middle = gmid_s[...]
        proj_low = grad_middle.astype(BF16)
        keep(5, proj_low)
        grad_att = nt(proj_low, weight(3))
        for w in range(4):
            gatt_s[w] = pad_window(grad_att[w * ROWS : (w + 1) * ROWS]).astype(BF16)
        groups = range(heads // 4)
        ats = [slice(g * 128, (g + 1) * 128) for g in groups]
        wides = [slice(g * 4 * WPAD, (g + 1) * 4 * WPAD) for g in groups]
        for w in range(4):
            here = slice(w * ROWS, (w + 1) * ROWS)

            def part(n, g, w=w):
                return qkv_s[w, :, n * BLOCK + g * 128 : n * BLOCK + (g + 1) * 128]

            spread_grad = [spread(gatt_s[w, :, ats[g]], hmask) for g in groups]
            grad_probs = [nt(part(2, g), spread_grad[g]) for g in groups]
            grad_v = [nn(prob_s[w, :, wides[g]].astype(BF16), spread_grad[g]) for g in groups]
            scores_low = []
            for g in groups:
                probs = prob_s[w, :, wides[g]]
                weighted = probs * grad_probs[g]
                grad_scores = weighted - probs * jnp.sum(weighted, 0, keepdims=True)
                pair_ref[:, wides[g]] += grad_scores
                scores_low.append(grad_scores.astype(BF16))
            grad_k = [nn(scores_low[g], spread(part(0, g), hmask)) for g in groups]
            grad_q = [tn(scores_low[g], part(1, g)) for g in groups]
            for g in groups:
                dqkv_s[here, 2 * BLOCK + g * 128 : 2 * BLOCK + (g + 1) * 128] = grad_v[g][:ROWS]
                dqkv_s[here, BLOCK + g * 128 : BLOCK + (g + 1) * 128] = grad_k[g][:ROWS]
                dqkv_s[here, g * 128 : (g + 1) * 128] = fold(grad_q[g], hmask) * scale
        for n in range(3):
            part = dqkv_s[:, n * BLOCK : (n + 1) * BLOCK]
            if n == 0:
                note(2, part)
            if n == 2:
                note(3, part)
            keep(1 + n, part.astype(BF16))
        for block in range(6):
            acts[block, rows, :] = acts_s[block]

    @pl.when(step > images)
    def _():
        rows = pl.ds(pl.multiple_of((step - images - 1) * (4 * ROWS), 16), 4 * ROWS)
        unit, rate = normalize(nn(place_ref[...], tok_ref[0]))
        grad = None
        for n in range(3):
            term = nt(acts[1 + n, rows, :], weight(n))
            grad = term if n == 0 else grad + term
        note(0, grad * unit)
        note(1, grad)
        tg_ref[0] = gmid_ref[0] + norm_back(grad, unit, rate, vec(0))

    small_bufs = {"x": small_x, "y": small_y, "z": small_z}
    small_base = 72

    def small_cores():
        part = small_pair.at[me.core]
        return [remote(part, part, *sems, small_base, me.other_core())]

    def small_copies(axis):
        part = small_bufs[axis].at[me.at[axis]]
        first = small_base + 1 + 3 * "xyz".index(axis)
        return [remote(part, part, *sems, first + s - 1, me.along(axis, s)) for s in (1, 2, 3)]

    def small_across():
        copies = []
        for s in (1, 2, 3):
            peer = lax.rem(me.at["x"] + s, SIDE_CHIPS)
            source, target = small_halves.at[peer // 2], small_x.at[me.at["x"]]
            copies.append(remote(source, target, *sems, small_base + s, me.along("x", s)))
        return copies

    def small_start(axis, values):
        small_bufs[axis][pl.ds(me.at[axis], 1)] = values[None]
        start(small_copies(axis))

    def small_sum(axis):
        arrived(small_across() if axis == "x" else small_copies(axis))
        buf = small_bufs[axis]
        return (buf[0] + buf[1]) + (buf[2] + buf[3])

    @pl.when(step == images)
    def _():
        def grad_block(n):
            left = jnp.where(n < 3, 0, 4)
            right = jnp.where(n < 3, n + 1, 5)
            return tn(acts[left], acts[right]).reshape(2, 256, BLOCK)

        for p in range(2):
            low_send[p] = grad_block(2 * p + 1 - me.core).astype(BF16)
            start([low_pair(p)])
        for number in DURING_GRADS[0]:
            high.step(number)
        for p in range(2):
            low_own[p] = grad_block(2 * p + me.core)
        for number in DURING_GRADS[1]:
            high.step(number)
        half = WPAD // 2
        for h in range(heads):
            at = slice(h * WPAD, (h + 1) * WPAD)
            both = jnp.concatenate([pair_ref[:half, at], pair_ref[half:, at]], 1)
            fold_s[pl.ds(h, half, stride=heads), :] = both

        def body(j, total):
            values = fold_s[pl.ds(pl.multiple_of(j * heads, heads), heads), :]
            upper = values.astype(BF16)
            rest = (values - upper.astype(F32)).astype(BF16)
            return total + nt(jnp.concatenate([upper, rest], 0), pair_rows(rel_ref, j))

        total = lax.fori_loop(0, half, body, jnp.zeros((2 * heads, 256), F32), unroll=4)
        table = total[:heads] + total[heads:]
        small_ref[12 : 12 + heads // 2, :256] = table[: heads // 2]
        small_ref[12 : 12 + heads // 2, 256:] = table[heads // 2 :]
        for p in range(2):
            arrived([low_pair(p)])
            for part in range(2):
                total = low_own[p, part] + lo_pair[p, part].astype(F32)
                lo_sums[p, 0, part] = total.astype(BF16)
        low.step(1)

    @pl.when(step == 2 * images)
    def _():
        small_pair[pl.ds(me.core, 1)] = small_ref[...][None]
        start(small_cores())
        high_out = pltpu.make_async_copy(f_ref.at[pl.ds(4, 8)], f_out.at[pl.ds(4, 8)], out_sem.at[0])
        arrived(small_cores())
        small_total = small_pair[0] + small_pair[1]
        small_halves[0] = small_total[:, :256]
        small_halves[1] = small_total[:, 256:]
        start(small_across())
        small_x[pl.ds(me.at["x"], 1)] = small_halves[pl.ds(me.hi, 1)]
        low.step(2)
        small_start("y", small_sum("x"))
        low.step(3)
        high.step(6)
        small_start("z", small_sum("y"))
        low.step(4)
        small_out[...] = small_sum("z")
        low.step(5)
        high.step(7)
        high_out.start()
        low.step(6)
        low.step(7)
        low_out = pltpu.make_async_copy(f_ref.at[pl.ds(0, 4)], f_out.at[pl.ds(0, 4)], out_sem.at[1])
        low_out.start()
        high_out.wait()
        low_out.wait()
        high.all_sent()
        low.all_sent()
        sent([low_pair(p) for p in range(2)])
        sent(small_cores())
        sent(small_across())
        sent(small_copies("y"))
        sent(small_copies("z"))


PLAN = (
    (4, (("high", 2),)),
    (5, (("high", 3),)),
    (6, (("high", 4),)),
)
DURING_GRADS = ((), (5,))


def run_back(qkv, prob, normed, att, gmid, tokens, weights, vecs, rel_rows, small, fc):
    images, tokens_image, width = tokens.shape
    heads = prob.shape[3] // WPAD
    rows = 4 * ROWS
    vmem = pl.BlockSpec(memory_space=pltpu.VMEM)
    far = pl.BlockSpec(memory_space=pltpu.HBM)

    def per_image(shape, index):
        return pl.BlockSpec((1,) + shape, lambda b: (index(b),) + (0,) * len(shape))

    def early(b):
        return jnp.minimum(b, images - 1)

    def late(b):
        return jnp.maximum(b - images - 1, 0)

    def twice(b):
        return jnp.where(b < images, b, late(b))

    def whole(array):
        return pl.BlockSpec(array.shape, lambda b: (0,) * array.ndim, pipeline_mode=pl.Buffered(1))

    def reduce_scratch(count):
        return [
            pltpu.VMEM((2, count, 2, 256, BLOCK), BF16),
            pltpu.VMEM((2, 3, count, 2, 64, BLOCK), BF16),
            pltpu.VMEM((2, count, 2, 64, BLOCK), BF16),
            pltpu.VMEM((2, 3, count, 2, 16, BLOCK), BF16),
            pltpu.VMEM((2, count, 2, 16, BLOCK), BF16),
            pltpu.VMEM((2, 4, count, 16, BLOCK), BF16),
        ]

    return pl.pallas_call(
        partial(back_kernel, images, heads),
        grid=(2 * images + 1,),
        in_specs=[
            per_image(qkv.shape[1:], early),
            per_image(prob.shape[1:], early),
            per_image(normed.shape[1:], early),
            per_image(att.shape[1:], early),
            per_image(gmid.shape[1:], twice),
            per_image((tokens_image, width), late),
            whole(weights),
            whole(vecs),
            whole(rel_rows),
            whole(small),
            far,
        ],
        out_specs=[per_image((rows, width), late), far, vmem],
        out_shape=[
            jax.ShapeDtypeStruct((images, rows, width), F32),
            jax.ShapeDtypeStruct((12, 256, BLOCK), BF16),
            jax.ShapeDtypeStruct((24, 256), F32),
        ],
        scratch_shapes=[
            pltpu.VMEM((4, WPAD, 3 * BLOCK), BF16),
            pltpu.VMEM((4, WPAD, heads * WPAD), F32),
            pltpu.VMEM((rows, width), F32),
            pltpu.VMEM((6, rows, BLOCK), BF16),
            pltpu.VMEM((12, 256, BLOCK), BF16),
            pltpu.VMEM((rows, tokens_image), BF16),
            pltpu.VMEM((4 * WPAD, 128), BF16),
            pltpu.VMEM((24, BLOCK), F32),
            pltpu.VMEM((WPAD, heads * WPAD), F32),
            pltpu.VMEM((heads * WPAD // 2, 128), F32),
            pltpu.VMEM((4, WPAD, BLOCK), BF16),
            pltpu.VMEM((rows, 3 * BLOCK), F32),
            pltpu.VMEM((6, images * rows, BLOCK), BF16),
        ]
        + reduce_scratch(2)
        + [
            pltpu.VMEM((2, 2, 256, BLOCK), BF16),
            pltpu.VMEM((2, 2, 256, BLOCK), F32),
            pltpu.VMEM((2, 2, 256, BLOCK), BF16),
        ]
        + reduce_scratch(1)
        + [
            pltpu.VMEM((2, 24, BLOCK), F32),
            pltpu.VMEM((2, 24, 256), F32),
            pltpu.VMEM((4, 24, 256), F32),
            pltpu.VMEM((4, 24, 256), F32),
            pltpu.VMEM((4, 24, 256), F32),
            pltpu.SemaphoreType.DMA((2,)),
            pltpu.SemaphoreType.DMA((2,)),
            pltpu.SemaphoreType.DMA((82,)),
            pltpu.SemaphoreType.DMA((82,)),
        ],
        compiler_params=pltpu.CompilerParams(
            collective_id=1, has_side_effects=True, vmem_limit_bytes=56 * 1024 * 1024
        ),
        name="back",
    )(qkv, prob, normed, att, gmid, tokens, weights, vecs, rel_rows, small, fc)


def finish_kernel(
    out_win, tg_win, f_ref, small_ref,
    out_ref, tg_ref, n1g, n1b, qkv, qb, vb, table, proj, pb, n2g, n2b, fc1, f1b, fc2, f2b,
    out_in, tg_in, f_in, small_in, out_s, tg_s, wide, in_sem, out_sem, sem,
):
    images = out_win.shape[0]
    per_step = -(-12 // images)
    targets = []
    for n in range(12):
        if n < 3:
            targets.append([(slice(None), qkv.at[:, pl.ds(n * BLOCK, BLOCK)])])
        elif n == 3:
            targets.append([(slice(None), proj)])
        elif n < 8:
            targets.append(
                [
                    (pl.ds(half * 256, 256), fc1.at[:, pl.ds(half * 1024 + (n - 4) * 256, 256)])
                    for half in range(2)
                ]
            )
        else:
            targets.append([(slice(None), fc2.at[pl.ds((n - 8) * 256, 256)])])
    blocks = [range(b * per_step, min(12, (b + 1) * per_step)) for b in range(images)]
    small_copy = pltpu.make_async_copy(small_ref, small_in, in_sem.at[3 * images])
    loads = []
    for b in range(images):
        copies = [
            pltpu.make_async_copy(tg_win.at[b], tg_in.at[b], in_sem.at[3 * b]),
            pltpu.make_async_copy(out_win.at[b], out_in.at[b], in_sem.at[3 * b + 1]),
        ]
        if len(blocks[b]):
            part = pl.ds(blocks[b][0], len(blocks[b]))
            copies.append(pltpu.make_async_copy(f_ref.at[part], f_in.at[part], in_sem.at[3 * b + 2]))
        start(copies)
        loads.append(copies)
    small_copy.start()
    back = back_matrix().astype(BF16)
    stores = []
    for b in range(images):
        for copy in loads[b]:
            copy.wait()
        for n in blocks[b]:
            wide[n] = f_in[n].astype(F32)
            for i, (lanes, target) in enumerate(targets[n]):
                stores.append(pltpu.make_async_copy(wide.at[n, :, lanes], target, sem.at[n, i]))
                stores[-1].start()
        total = tg_in[b]
        upper = total.astype(BF16)
        rest = (total - upper.astype(F32)).astype(BF16)
        tg_s[b] = nn(back, upper) + nn(back, rest)
        stores.append(pltpu.make_async_copy(tg_s.at[b], tg_ref.at[b], out_sem.at[2 * b]))
        stores[-1].start()
        out_s[b] = nn(back, out_in[b]).astype(BF16)
        stores.append(pltpu.make_async_copy(out_s.at[b], out_ref.at[b], out_sem.at[2 * b + 1]))
        stores[-1].start()
    small_copy.wait()
    for row, ref in enumerate((n1g, n1b, qb, vb, pb, n2g, n2b, f2b)):
        ref[...] = small_in[row : row + 1, :].reshape(256)
    for m in range(4):
        f1b[pl.ds(m * 256, 256)] = small_in[8 + m : 9 + m, :].reshape(256)
    table[...] = small_in[12:20, 0 : table.shape[1]]
    for copy in stores:
        copy.wait()


def finish(out_win, tg_win, grads, small, table_rows, heads_here):
    images, rows, width = out_win.shape
    tokens_image = SIDE * SIDE
    vmem = pl.BlockSpec(memory_space=pltpu.VMEM)
    far = pl.BlockSpec(memory_space=pltpu.HBM)
    vector, hidden = ((256,), vmem), ((1024,), vmem)
    outs = [
        vector, vector, ((256, 3 * BLOCK), far), vector, vector, ((heads_here, table_rows), vmem),
        ((256, BLOCK), far), vector, vector, vector, ((256, 4 * BLOCK), far), hidden,
        ((1024, BLOCK), far), vector,
    ]
    return pl.pallas_call(
        finish_kernel,
        in_specs=[far] * 4,
        out_specs=[far, far] + [spec for _, spec in outs],
        out_shape=[
            jax.ShapeDtypeStruct((images, tokens_image, width), BF16),
            jax.ShapeDtypeStruct((images, tokens_image, width), F32),
        ]
        + [jax.ShapeDtypeStruct(shape, F32) for shape, _ in outs],
        scratch_shapes=[
            pltpu.VMEM(out_win.shape, BF16),
            pltpu.VMEM(tg_win.shape, F32),
            pltpu.VMEM(grads.shape, BF16),
            pltpu.VMEM(small.shape, F32),
            pltpu.VMEM((images, tokens_image, width), BF16),
            pltpu.VMEM((images, tokens_image, width), F32),
            pltpu.VMEM((12, 256, BLOCK), F32),
            pltpu.SemaphoreType.DMA((3 * images + 1,)),
            pltpu.SemaphoreType.DMA((2 * images,)),
            pltpu.SemaphoreType.DMA((12, 2)),
        ],
        compiler_params=pltpu.CompilerParams(vmem_limit_bytes=40 * 1024 * 1024),
        name="finish",
    )(out_win, tg_win, grads, small)


def local(
    tokens, image_counts, shift_mask, rel_index, norm1_gain, norm1_bias, qkv_weight, q_bias, v_bias,
    rel_table, proj_weight, proj_bias, norm2_gain, norm2_bias, fc1_weight, fc1_bias, fc2_weight,
    fc2_bias, out_grad,
):
    table_rows, heads_here = rel_table.shape
    qkv, prob, normed, att, block_out, gmid, fc, small, vecs, rel_rows, low_weights = run_front(
        [qkv_weight, proj_weight, fc1_weight, fc2_weight],
        [norm1_gain, norm1_bias, q_bias, v_bias, proj_bias, norm2_gain, norm2_bias, fc2_bias],
        fc1_bias, rel_table.T, rel_index, shift_mask.transpose(1, 0, 2), tokens, out_grad, image_counts,
    )
    tokens_grad, grads, small = run_back(
        qkv, prob, normed, att, gmid, tokens, low_weights, vecs, rel_rows, small, fc.reshape(4, 2, 256, BLOCK)
    )
    outs = finish(block_out, tokens_grad, grads, small, table_rows, heads_here)
    return (*outs[:7], outs[7].T, *outs[8:])


def solution(mesh):
    split = P(("replica", "shard"), None, None)
    vector, matrix, table = P("shard"), P("shard", None), P(None, "shard")
    return jax.shard_map(
        local,
        mesh=mesh,
        in_specs=(
            split, P(("replica", "shard")), P(), P(), vector, vector, matrix, vector, vector, table,
            matrix, vector, vector, vector, matrix, vector, matrix, vector, split,
        ),
        out_specs=(
            split, split, vector, vector, matrix, vector, vector, table, matrix, vector, vector,
            vector, matrix, vector, matrix, vector,
        ),
        check_vma=False,
    )
```

```python
from functools import partial

import jax
import jax.numpy as jnp
from jax import lax
from jax.experimental import pallas as pl
from jax.experimental.pallas import tpu as pltpu
from jax.sharding import PartitionSpec as P

WIN = 7
SIDE = 14
SHIFT = 3
EPSILON = 1e-05
MASKED = -1e30
WTOK = WIN * WIN
ROWS = 56
WPAD = 64
BLOCK = 512
F32 = jnp.float32
BF16 = jnp.bfloat16


def nn(left, right):
    return jnp.dot(left, right, preferred_element_type=F32)


def nt(left, right):
    return lax.dot_general(left, right, (((1,), (1,)), ((), ())), preferred_element_type=F32)


def tn(left, right):
    return lax.dot_general(left, right, (((0,), (0,)), ((), ())), preferred_element_type=F32)


def normalize(values):
    center = values - jnp.mean(values, -1, keepdims=True)
    rate = lax.rsqrt(jnp.mean(center * center, -1, keepdims=True) + EPSILON)
    return center * rate, rate


def norm_back(grad, unit, rate, gain):
    scaled = grad * gain
    return rate * (
        scaled
        - jnp.mean(scaled, -1, keepdims=True)
        - unit * jnp.mean(scaled * unit, -1, keepdims=True)
    )


def normal_parts(v):
    bell = jnp.exp2(v * v * -0.7213475204444817)
    t = 1.0 / (1.0 + 0.23164189 * jnp.abs(v))
    tail = t * (
        0.127414796
        + t * (-0.142248368 + t * (0.7107068705 + t * (-0.7265760135 + t * 0.5307027145)))
    )
    half = tail * bell
    return jnp.where(v < 0, half, 1.0 - half), 0.3989422804014327 * bell


def col_sum(values):
    return jnp.sum(values, 0, keepdims=True)


MESH = pl.DeviceIdType.MESH
SIDE_CHIPS = 4


class Place:
    def __init__(self):
        replica = lax.axis_index("replica")
        self.hi = lax.axis_index("shard")
        self.core = lax.rem(replica, 2)
        self.at = {
            "x": self.hi * 2 + lax.rem(replica // 2, 2),
            "z": lax.rem(replica // 4, SIDE_CHIPS),
            "y": replica // 16,
        }
        self.lo = lax.rem(replica // 2, 2)

    def id_of(self, core=None, **at):
        place = dict(self.at, **at)
        core = self.core if core is None else core
        lo, hi = lax.rem(place["x"], 2), place["x"] // 2
        return (((place["y"] * SIDE_CHIPS + place["z"]) * 2 + lo) * 2 + core, hi)

    def other_core(self):
        return self.id_of(core=1 - self.core)

    def along(self, axis, step):
        return self.id_of(**{axis: lax.rem(self.at[axis] + step, SIDE_CHIPS)})


def greet(devices):
    barrier = pltpu.get_barrier_semaphore()
    for device in devices:
        pl.semaphore_signal(barrier, inc=1, device_id=device, device_id_type=MESH)
    pl.semaphore_wait(barrier, len(devices))


def pad_window(values):
    return jnp.concatenate([values, jnp.zeros((WPAD - ROWS, values.shape[1]), F32)], 0)


def source_of(row):
    window = jnp.floor((row + 0.5) / ROWS)
    cell = row - window * ROWS
    across = jnp.floor((window + 0.5) / 2)
    down = jnp.floor((cell + 0.5) / WIN)
    i = across * WIN + down + SHIFT
    j = (window - 2 * across) * WIN + (cell - down * WIN) + SHIFT
    i = jnp.where(i >= SIDE, i - SIDE, i)
    j = jnp.where(j >= SIDE, j - SIDE, j)
    return jnp.where(cell < WTOK, i * SIDE + j, -1.0)


def iota(shape, axis):
    return lax.broadcasted_iota(jnp.int32, shape, axis).astype(F32)


def place_matrix():
    rows, tokens = 4 * ROWS, SIDE * SIDE
    return jnp.where(source_of(iota((rows, tokens), 0)) == iota((rows, tokens), 1), 1.0, 0.0)


def back_matrix():
    rows, tokens = 4 * ROWS, SIDE * SIDE
    return jnp.where(source_of(iota((tokens, rows), 1)) == iota((tokens, rows), 0), 1.0, 0.0)


def head_mask():
    shape = (4 * WPAD, 128)
    row, lane = iota(shape, 0), iota(shape, 1)
    return jnp.where(jnp.floor((row + 0.5) / WPAD) == jnp.floor((lane + 0.5) / 32), 1.0, 0.0)


def pair_rows(rel_ref, j):
    return jnp.where(iota((256, 128), 0) == rel_ref[pl.ds(j, 1), :], 1.0, 0.0).astype(BF16)


def spread(part, hmask):
    return jnp.concatenate([part] * 4, 0) * hmask


def fold(full, hmask):
    full = full * hmask.astype(F32)
    total = full[:WPAD]
    for h in range(1, 4):
        total = total + full[h * WPAD : (h + 1) * WPAD]
    return total[:ROWS]


def both_halves(vec_ref, row):
    return jnp.concatenate([vec_ref[0, row : row + 1, :], vec_ref[1, row : row + 1, :]], 1)


def remote(source, target, send_sem, recv_sem, number, device):
    return pltpu.make_async_remote_copy(
        src_ref=source,
        dst_ref=target,
        send_sem=send_sem.at[number],
        recv_sem=recv_sem.at[number],
        device_id=device,
        device_id_type=MESH,
    )


def start(copies):
    for copy in copies:
        copy.start()


def arrived(copies):
    for copy in copies:
        copy.wait_recv()


def sent(copies):
    for copy in copies:
        copy.wait_send()


class Gather:
    SEMAPHORES = 37

    def __init__(self, me, w_ref, v_ref, send_sem, recv_sem):
        self.me, self.w, self.v = me, w_ref, v_ref
        self.sems = (send_sem, recv_sem)

    def flows(self, group):
        count = 1 + group
        for flow, (first, second) in enumerate((("z", "y"), ("y", "z"))):
            block = 4 * group + 2 * count * flow + self.me.core * count
            yield 16 * group + 8 * flow, pl.ds(block, count), first, second

    def copy(self, number, part, device):
        return remote(part, part, *self.sems, number, device)

    def facing(self):
        return self.me.id_of(x=3 - self.me.at["x"])

    def cross(self, group):
        me = self.me
        return [
            self.copy(
                number,
                self.w.at[blocks, me.hi, pl.ds(me.at[second] * 64 + me.at[first] * 16, 16)],
                self.facing(),
            )
            for number, blocks, first, second in self.flows(group)
        ]

    def vectors(self):
        return [self.copy(32, self.v.at[self.me.hi], self.facing())]

    def first(self, group):
        me = self.me
        return [
            self.copy(
                number + step,
                self.w.at[blocks, 1 - me.hi, pl.ds(me.at[second] * 64 + me.at[first] * 16, 16)],
                me.along(first, step),
            )
            for number, blocks, first, second in self.flows(group)
            for step in (1, 2, 3)
        ]

    def second(self, group):
        me = self.me
        return [
            self.copy(
                number + 3 + step,
                self.w.at[blocks, 1 - me.hi, pl.ds(me.at[second] * 64, 64)],
                me.along(second, step),
            )
            for number, blocks, first, second in self.flows(group)
            for step in (1, 2, 3)
        ]

    def last(self, group):
        return [
            self.copy(number + 7, self.w.at[blocks, 1 - self.me.hi], self.me.other_core())
            for number, blocks, _, _ in self.flows(group)
        ]


def front_kernel(
    images,
    count_ref,
    qkv_w, proj_w, fc1_w, fc2_w, n1g, n1b, qb, vb, pb, n2g, n2b, f2b, f1b, table_w, index_w, mask_w,
    tok_hbm, up_ref,
    qkv_ref, prob_ref, normed_ref, att_ref, out_ref, gmid_ref, fc_ref, small_ref, vec_out, rel_ref, low_ref,
    vec_ref, w_ref, acts, bias_ref, place_ref, hmask_ref, att_s, qkv_s, prob_s, acts_s, fc_send, fc_pair, tok_s, normed_s,
    v0, v1, v2, v3, v4, v5, v6, v7, v8, table_v, index_v, mask_v, square, square_mask, pairs,
    w_sem, in_sem, low_sem, send_sem, recv_sem,
):
    step = pl.program_id(0)
    me = Place()
    hi = me.hi
    gather = Gather(me, w_ref, vec_ref, send_sem, recv_sem)
    heads = table_w.shape[0] * 2
    scale = (up_ref.shape[2] // heads) ** (-0.5)

    def own_weights(group):
        pairs = []
        if group == 0:
            for n in range(3):
                pairs.append((qkv_w.at[:, pl.ds(n * BLOCK, BLOCK)], w_ref.at[n, hi]))
            pairs.append((proj_w, w_ref.at[3, hi]))
        else:
            for m in range(4):
                for half in range(2):
                    pairs.append(
                        (
                            fc1_w.at[:, pl.ds(half * 1024 + m * 256, 256)],
                            w_ref.at[4 + m, hi, :, pl.ds(half * 256, 256)],
                        )
                    )
                pairs.append((fc2_w.at[pl.ds(m * 256, 256)], w_ref.at[8 + m, hi]))
        return [
            pltpu.make_async_copy(source, target, w_sem.at[4 * group + i])
            for i, (source, target) in enumerate(pairs)
        ]

    def own_small():
        sources = (n1g, n1b, qb, vb, pb, n2g, n2b, f2b, f1b, table_w, index_w, mask_w)
        targets = (v0, v1, v2, v3, v4, v5, v6, v7, v8, table_v, index_v, mask_v)
        return [
            pltpu.make_async_copy(source, target, in_sem.at[i])
            for i, (source, target) in enumerate(zip(sources, targets))
        ]

    def token_copy():
        return pltpu.make_async_copy(tok_hbm, tok_s, low_sem.at[1])

    def low_copy():
        return pltpu.make_async_copy(w_ref.at[pl.ds(0, 4)], low_ref, low_sem.at[0])

    def weight(n):
        return w_ref[n].reshape(BLOCK, BLOCK)

    def vec(row):
        return both_halves(vec_ref, row)

    def note(row, values):
        small_ref[row : row + 1, :] += col_sum(values)

    @pl.when(step == 0)
    def _():
        small_copies = own_small()
        start(own_weights(0))
        start(small_copies)
        start(own_weights(1))
        token_copy().start()
        peers = [gather.facing(), me.other_core()]
        peers += [me.along(axis, s) for axis in ("y", "z") for s in (1, 2, 3)]
        greet(peers)
        for copy in own_weights(0):
            copy.wait()
        start(gather.cross(0))
        for copy in small_copies:
            copy.wait()
        rows = [ref[...].astype(F32).reshape(1, 256) for ref in (v0, v1, v2, v3, v4, v5, v6, v7)]
        rows += [v8[pl.ds(m * 256, 256)].astype(F32).reshape(1, 256) for m in range(4)]
        rows.append(jnp.zeros((4, 256), F32))
        vec_ref[pl.ds(hi, 1), 0:16] = jnp.concatenate(rows, 0)[None]
        heads_here, table_rows = table_v.shape
        vec_ref[pl.ds(hi, 1), 16:24] = jnp.zeros((1, 8, 256), F32)
        vec_ref[pl.ds(hi, 1), 16:24, 0:table_rows] = table_v[...].astype(F32)[None]
        start(gather.vectors())
        for copy in own_weights(1):
            copy.wait()
        start(gather.cross(1))
        arrived(gather.cross(0))
        start(gather.first(0))
        arrived(gather.cross(1))
        start(gather.first(1))
        square[...] = jnp.full((128, 128), -1.0, F32)
        square[0:WTOK, 0:WTOK] = index_v[...].astype(F32)
        turned = square[...].T
        half = WPAD // 2
        rel_ref[...] = jnp.concatenate([turned[:half, :WPAD], turned[half:WPAD, :WPAD]], 1)
        for w in range(4):
            square_mask[w] = jnp.where(iota((WPAD, WPAD), 0) < WTOK, 0.0, MASKED)
            square_mask[w, 0:WTOK, 0:WTOK] = jnp.where(mask_v[:, w, :] == 1, 0.0, -100.0)
        place_ref[...] = place_matrix().astype(BF16)
        hmask_ref[...] = head_mask().astype(BF16)
        small_ref[...] = jnp.zeros_like(small_ref)
        arrived(gather.first(0))
        start(gather.second(0))
        arrived(gather.first(1))
        start(gather.second(1))
        arrived(gather.vectors())
        vec_out[...] = vec_ref[...]
        table = jnp.concatenate([vec_ref[0, 16:24], vec_ref[1, 16:24]], 0).astype(BF16)

        def body(j, carry):
            pairs[pl.ds(pl.multiple_of(j * heads, heads), heads), :] = nn(table, pair_rows(rel_ref, j))
            return carry

        lax.fori_loop(0, half, body, 0, unroll=4)
        arrived(gather.second(0))
        start(gather.last(0))
        for h in range(heads):
            at = slice(h * WPAD, (h + 1) * WPAD)
            both = pairs[pl.ds(h, half, stride=heads), :]
            for w in range(4):
                bias_ref[w, :half, at] = both[:, :WPAD] + square_mask[w, :half]
                bias_ref[w, half:, at] = both[:, WPAD:] + square_mask[w, half:]
        token_copy().wait()

        def norm(b, carry):
            unit, _ = normalize(nn(place_ref[...], tok_s[b]))
            normed_s[b] = (unit * vec(0) + vec(1)).astype(BF16)
            return carry

        lax.fori_loop(0, images, norm, 0)
        arrived(gather.last(0))
        low_copy().start()

    @pl.when(step == SECOND_STEP)
    def _():
        arrived(gather.second(1))
        start(gather.last(1))

    @pl.when(step == images)
    def _():
        arrived(gather.last(1))

    @pl.when(step < images)
    def _():
        hmask = hmask_ref[...]
        normed = normed_s[step]
        for n in range(3):
            part = nn(normed, weight(n))
            if n == 0:
                part = (part + vec(2)) * scale
            if n == 2:
                part = part + vec(3)
            for w in range(4):
                qkv_s[w, :, n * BLOCK : (n + 1) * BLOCK] = pad_window(
                    part[w * ROWS : (w + 1) * ROWS]
                ).astype(BF16)
        for w in range(4):
            for g in range(heads // 4):
                at = slice(g * 128, (g + 1) * 128)
                wide = slice(g * 4 * WPAD, (g + 1) * 4 * WPAD)
                q = qkv_s[w, :, g * 128 : (g + 1) * 128]
                k = qkv_s[w, :, BLOCK + g * 128 : BLOCK + (g + 1) * 128]
                v = qkv_s[w, :, 2 * BLOCK + g * 128 : 2 * BLOCK + (g + 1) * 128]
                scores = nt(k, spread(q, hmask)) + bias_ref[w, :, wide]
                raised = jnp.exp(scores - jnp.max(scores, 0, keepdims=True))
                probs = raised * (1.0 / jnp.sum(raised, 0, keepdims=True))
                prob_s[w, :, wide] = probs
                att_s[w * ROWS : (w + 1) * ROWS, at] = fold(tn(probs.astype(BF16), v), hmask)
        att_ref[step] = att_s[...].astype(BF16)
        normed_ref[0] = normed
        qkv_ref[0] = qkv_s[...]
        prob_ref[0] = prob_s[...]

    @pl.when((step >= images) & (step < 2 * images))
    def _():
        image = step - images
        valid = (image < count_ref[0]).astype(F32)
        rows = pl.ds(pl.multiple_of(image * (4 * ROWS), 16), 4 * ROWS)

        def keep(block, values):
            acts[block, rows, :] = values

        middle = nn(place_ref[...], tok_s[image]) + (nn(att_ref[image], weight(3)) + vec(4))
        unit, rate = normalize(middle)
        normed = (unit * vec(5) + vec(6)).astype(BF16)
        keep(0, normed)
        upstream = nn(place_ref[...], up_ref[0]) * valid
        up_low = upstream.astype(BF16)
        keep(9, up_low)
        note(7, upstream)
        act_parts, pre_parts = [], []
        for c in range(4):
            pre = nn(normed, weight(4 + c)) + vec(8 + c)
            below, density = normal_parts(pre)
            act = (pre * below).astype(BF16)
            keep(5 + c, act)
            grad_pre = nt(up_low, weight(8 + c)) * (below + pre * density)
            note(8 + c, grad_pre)
            pre_low = grad_pre.astype(BF16)
            keep(1 + c, pre_low)
            act_parts.append(act)
            pre_parts.append(pre_low)
        branch = nn(jnp.concatenate(act_parts, 1), w_ref[8:12].reshape(4 * BLOCK, BLOCK))
        grad = nt(
            jnp.concatenate(pre_parts, 1), jnp.concatenate([weight(4 + c) for c in range(4)], 1)
        )
        result = middle + (branch + vec(7))
        note(5, grad * unit)
        note(6, grad)
        grad_middle = upstream + norm_back(grad, unit, rate, vec(5))
        note(4, grad_middle)
        gmid_ref[0] = grad_middle
        out_ref[0] = (result * valid).astype(BF16)

    def grad_block(number, core):
        block = 4 * (number // 2) + 2 * core + lax.rem(number, 2)
        left = jnp.where(block < 4, 0, block + 1)
        right = jnp.where(block < 4, block + 1, 9)
        return tn(acts[left], acts[right])

    def pair_copy(number):
        return remote(
            fc_send.at[number], fc_pair.at[number], send_sem, recv_sem, 33 + number, me.other_core()
        )

    @pl.when((step >= 2 * images) & (step < 2 * images + 4))
    def _():
        number = step - 2 * images
        fc_send[number] = grad_block(number, 1 - me.core).astype(BF16)

    for number in range(4):
        @pl.when(step == 2 * images + number)
        def _(number=number):
            start([pair_copy(number)])

        @pl.when(step == 2 * images + 4 + number)
        def _(number=number):
            arrived([pair_copy(number)])

    @pl.when(step >= 2 * images + 4)
    def _():
        number = step - 2 * images - 4
        fc_ref[0] = (grad_block(number, me.core) + fc_pair[number].astype(F32)).astype(BF16)

    @pl.when(step == pl.num_programs(0) - 1)
    def _():
        for group in range(2):
            for copies in (gather.cross, gather.first, gather.second, gather.last):
                sent(copies(group))
        sent(gather.vectors())
        sent([pair_copy(number) for number in range(4)])
        low_copy().wait()


SECOND_STEP = 3


def run_front(matrices, vectors, hidden_bias, table, rel_index, shift_mask, tokens, out_grad, count):
    images, tokens_image, width = tokens.shape
    heads = table.shape[0] * 2
    rows = 4 * ROWS
    far = pl.BlockSpec(memory_space=pltpu.HBM)
    small = vectors + [hidden_bias, table, rel_index, shift_mask]

    def per_image(shape, index):
        return pl.BlockSpec((1,) + shape, lambda b: (index(b),) + (0,) * len(shape))

    def whole(shape):
        return pl.BlockSpec(shape, lambda b: (0,) * len(shape), pipeline_mode=pl.Buffered(1))

    def early(b):
        return jnp.minimum(b, images - 1)

    def late(b):
        return jnp.clip(b - images, 0, images - 1)

    return pl.pallas_call(
        partial(front_kernel, images),
        grid=(2 * images + 8,),
        in_specs=[pl.BlockSpec(memory_space=pltpu.SMEM)]
        + [far] * (4 + len(small))
        + [far, per_image((tokens_image, width), late)],
        out_specs=[
            per_image((4, WPAD, 3 * BLOCK), early),
            per_image((4, WPAD, heads * WPAD), early),
            per_image((rows, width), early),
            whole((images, rows, width)),
            per_image((rows, width), late),
            per_image((rows, width), late),
            per_image((BLOCK, BLOCK), lambda b: jnp.maximum(b - 2 * images - 4, 0)),
            whole((24, BLOCK)),
            whole((2, 24, 256)),
            whole((WPAD // 2, 2 * WPAD)),
            far,
        ],
        out_shape=[
            jax.ShapeDtypeStruct((images, 4, WPAD, 3 * BLOCK), BF16),
            jax.ShapeDtypeStruct((images, 4, WPAD, heads * WPAD), F32),
            jax.ShapeDtypeStruct((images, rows, width), BF16),
            jax.ShapeDtypeStruct((images, rows, width), BF16),
            jax.ShapeDtypeStruct((images, rows, width), BF16),
            jax.ShapeDtypeStruct((images, rows, width), F32),
            jax.ShapeDtypeStruct((4, BLOCK, BLOCK), BF16),
            jax.ShapeDtypeStruct((24, BLOCK), F32),
            jax.ShapeDtypeStruct((2, 24, 256), F32),
            jax.ShapeDtypeStruct((WPAD // 2, 2 * WPAD), F32),
            jax.ShapeDtypeStruct((4, 2, 256, BLOCK), BF16),
        ],
        scratch_shapes=[
            pltpu.VMEM((2, 24, 256), F32),
            pltpu.VMEM((12, 2, 256, BLOCK), BF16),
            pltpu.VMEM((10, images * rows, BLOCK), BF16),
            pltpu.VMEM((4, WPAD, heads * WPAD), F32),
            pltpu.VMEM((rows, tokens_image), BF16),
            pltpu.VMEM((4 * WPAD, 128), BF16),
            pltpu.VMEM((rows, BLOCK), F32),
            pltpu.VMEM((4, WPAD, 3 * BLOCK), BF16),
            pltpu.VMEM((4, WPAD, heads * WPAD), F32),
            pltpu.VMEM((10, rows, BLOCK), BF16),
            pltpu.VMEM((4, BLOCK, BLOCK), BF16),
            pltpu.VMEM((4, BLOCK, BLOCK), BF16),
            pltpu.VMEM(tokens.shape, BF16),
            pltpu.VMEM((images, rows, BLOCK), BF16),
        ]
        + [pltpu.VMEM(item.shape, item.dtype) for item in small]
        + [
            pltpu.VMEM((128, 128), F32),
            pltpu.VMEM((4, WPAD, WPAD), F32),
            pltpu.VMEM((heads * WPAD // 2, 2 * WPAD), F32),
            pltpu.SemaphoreType.DMA((16,)),
            pltpu.SemaphoreType.DMA((len(small),)),
            pltpu.SemaphoreType.DMA((2,)),
            pltpu.SemaphoreType.DMA((Gather.SEMAPHORES,)),
            pltpu.SemaphoreType.DMA((Gather.SEMAPHORES,)),
        ],
        compiler_params=pltpu.CompilerParams(
            collective_id=0, has_side_effects=True, vmem_limit_bytes=56 * 1024 * 1024
        ),
        name="front",
    )(count, *matrices, *small, tokens, out_grad)


class Reduce:
    SEMAPHORES = 36

    def __init__(self, me, sums, got, sum_one, got_one, sum_two, got_two, f_ref, first_block, sems, base):
        self.me, self.sums = me, sums
        self.got, self.sum_one, self.got_one = got, sum_one, got_one
        self.sum_two, self.got_two, self.f_ref = sum_two, got_two, f_ref
        self.first_block, self.sems, self.base = first_block, sems, base
        self.count = sums.shape[1]

    def axes(self, p):
        return (("y", "z"), ("z", "y"))[p]

    def copy(self, p, number, source, target, device):
        return remote(source, target, *self.sems, self.base + 18 * p + number, device)

    def target(self, p):
        return pl.ds(self.first_block + (2 * p + self.me.core) * self.count, self.count)

    def scatter(self, p, stage):
        me, axis = self.me, self.axes(p)[stage]
        rows = (64, 16)[stage]
        source, target = ((self.sums, self.got), (self.sum_one, self.got_one))[stage]
        return [
            self.copy(
                p,
                1 + 3 * stage + s - 1,
                source.at[p, :, :, pl.ds(lax.rem(me.at[axis] + s, SIDE_CHIPS) * rows, rows)],
                target.at[p, s - 1],
                me.along(axis, s),
            )
            for s in (1, 2, 3)
        ]

    def add(self, p, stage):
        arrived(self.scatter(p, stage))
        rows = (64, 16)[stage]
        source, got, target = (
            (self.sums, self.got, self.sum_one),
            (self.sum_one, self.got_one, self.sum_two),
        )[stage]
        at = pl.ds(pl.multiple_of(self.me.at[self.axes(p)[stage]] * rows, 16), rows)
        for b in range(self.count):
            for half in range(2):
                total = source[p, b, half, at, :].astype(F32)
                for s in range(3):
                    total = total + got[p, s, b, half].astype(F32)
                target[p, b, half] = total.astype(BF16)

    def across(self, p):
        me = self.me
        copies = []
        for s in (1, 2, 3):
            peer = lax.rem(me.at["x"] + s, SIDE_CHIPS)
            copies.append(
                self.copy(
                    p, 6 + s, self.sum_two.at[p, :, peer // 2], self.got_two.at[p, me.at["x"]], me.along("x", s)
                )
            )
        return copies

    def keep_own(self, p):
        for b in range(self.count):
            self.got_two[p, pl.ds(self.me.at["x"], 1), b] = self.sum_two[p, b, pl.ds(self.me.hi, 1)]

    def place(self, p):
        first, second = self.axes(p)
        return self.me.at[first] * 64, self.me.at[first] * 64 + self.me.at[second] * 16

    def add_across(self, p):
        arrived(self.across(p))
        _, row = self.place(p)
        at = pl.ds(pl.multiple_of(row, 16), 16)
        for b in range(self.count):
            parts = [self.got_two[p, x, b].astype(F32) for x in range(4)]
            total = (parts[0] + parts[1]) + (parts[2] + parts[3])
            block = self.first_block + (2 * p + self.me.core) * self.count + b
            self.f_ref[pl.ds(block, 1), at] = total.astype(BF16)[None]

    def back(self, p, stage):
        outer, inner = self.place(p)
        axis = self.axes(p)[stage]
        at = pl.ds(outer, 64) if stage == 0 else pl.ds(inner, 16)
        part = self.f_ref.at[self.target(p), at]
        return [
            self.copy(p, 10 + 3 * (1 - stage) + s - 1, part, part, self.me.along(axis, s)) for s in (1, 2, 3)
        ]

    def last(self, p):
        part = self.f_ref.at[self.target(p)]
        return [self.copy(p, 16, part, part, self.me.other_core())]

    def step(self, number):
        for p in range(2):
            if number == 1:
                start(self.scatter(p, 0))
            elif number == 2:
                self.add(p, 0)
                start(self.scatter(p, 1))
            elif number == 3:
                self.add(p, 1)
                start(self.across(p))
                self.keep_own(p)
            elif number == 4:
                self.add_across(p)
                start(self.back(p, 1))
            elif number == 5:
                arrived(self.back(p, 1))
                start(self.back(p, 0))
            elif number == 6:
                arrived(self.back(p, 0))
                start(self.last(p))
            else:
                arrived(self.last(p))

    def all_sent(self):
        for p in range(2):
            for stage in range(2):
                sent(self.scatter(p, stage))
                sent(self.back(p, stage))
            sent(self.across(p))
            sent(self.last(p))


def back_kernel(
    images,
    heads,
    qkv_ref, prob_ref, normed_ref, att_ref, gmid_ref, tok_ref, w_ref, vec_ref, rel_ref, small_in, fc_ref,
    tg_ref, f_out, small_out,
    qkv_s, prob_s, gmid_s, acts_s, f_ref, place_ref, hmask_ref, small_ref, pair_ref, fold_s, gatt_s, dqkv_s, acts,
    fc_sums, fc_got, fc_sum_one, fc_got_one, fc_sum_two, fc_got_two,
    low_send, low_own, lo_pair, lo_sums, lo_got, lo_sum_one, lo_got_one, lo_sum_two, lo_got_two,
    small_pair, small_halves, small_x, small_y, small_z, own_sem, out_sem, send_sem, recv_sem,
):
    step = pl.program_id(0)
    me = Place()
    scale = (tok_ref.shape[2] // heads) ** (-0.5)
    sems = (send_sem, recv_sem)
    high = Reduce(me, fc_sums, fc_got, fc_sum_one, fc_got_one, fc_sum_two, fc_got_two, f_ref, 4, sems, 0)
    low = Reduce(me, lo_sums, lo_got, lo_sum_one, lo_got_one, lo_sum_two, lo_got_two, f_ref, 0, sems, 36)

    def own_copies():
        return [
            pltpu.make_async_copy(fc_ref.at[pl.ds(2 * p, 2)], fc_sums.at[p], own_sem.at[p])
            for p in range(2)
        ]

    def low_pair(p):
        return remote(low_send.at[p], lo_pair.at[p], *sems, 36 + 18 * p, me.other_core())

    def weight(n):
        return w_ref[n].reshape(BLOCK, BLOCK)

    def vec(row):
        return both_halves(vec_ref, row)

    def note(row, values):
        small_ref[row : row + 1, :] += col_sum(values)

    @pl.when(step == 0)
    def _():
        start(own_copies())
        peers = [me.other_core()]
        peers += [me.along(axis, s) for axis in ("x", "y", "z") for s in (1, 2, 3)]
        greet(peers)
        for copy in own_copies():
            copy.wait()
        high.step(1)
        place_ref[...] = place_matrix().astype(BF16)
        hmask_ref[...] = head_mask().astype(BF16)
        small_ref[...] = small_in[...]
        pair_ref[...] = jnp.zeros_like(pair_ref)

    for at_step, moves in PLAN:
        @pl.when(step == at_step)
        def _(moves=moves):
            for group, number in moves:
                (high if group == "high" else low).step(number)

    @pl.when(step < images)
    def _():
        hmask = hmask_ref[...]
        rows = pl.ds(pl.multiple_of(step * (4 * ROWS), 16), 4 * ROWS)

        def keep(block, values):
            acts_s[block] = values

        qkv_s[...] = qkv_ref[0]
        prob_s[...] = prob_ref[0]
        gmid_s[...] = gmid_ref[0]
        keep(4, att_ref[0])
        keep(0, normed_ref[0])
        grad_middle = gmid_s[...]
        proj_low = grad_middle.astype(BF16)
        keep(5, proj_low)
        grad_att = nt(proj_low, weight(3))
        for w in range(4):
            gatt_s[w] = pad_window(grad_att[w * ROWS : (w + 1) * ROWS]).astype(BF16)
        groups = range(heads // 4)
        ats = [slice(g * 128, (g + 1) * 128) for g in groups]
        wides = [slice(g * 4 * WPAD, (g + 1) * 4 * WPAD) for g in groups]
        for w in range(4):
            here = slice(w * ROWS, (w + 1) * ROWS)

            def part(n, g, w=w):
                return qkv_s[w, :, n * BLOCK + g * 128 : n * BLOCK + (g + 1) * 128]

            spread_grad = [spread(gatt_s[w, :, ats[g]], hmask) for g in groups]
            grad_probs = [nt(part(2, g), spread_grad[g]) for g in groups]
            grad_v = [nn(prob_s[w, :, wides[g]].astype(BF16), spread_grad[g]) for g in groups]
            scores_low = []
            for g in groups:
                probs = prob_s[w, :, wides[g]]
                weighted = probs * grad_probs[g]
                grad_scores = weighted - probs * jnp.sum(weighted, 0, keepdims=True)
                pair_ref[:, wides[g]] += grad_scores
                scores_low.append(grad_scores.astype(BF16))
            grad_k = [nn(scores_low[g], spread(part(0, g), hmask)) for g in groups]
            grad_q = [tn(scores_low[g], part(1, g)) for g in groups]
            for g in groups:
                dqkv_s[here, 2 * BLOCK + g * 128 : 2 * BLOCK + (g + 1) * 128] = grad_v[g][:ROWS]
                dqkv_s[here, BLOCK + g * 128 : BLOCK + (g + 1) * 128] = grad_k[g][:ROWS]
                dqkv_s[here, g * 128 : (g + 1) * 128] = fold(grad_q[g], hmask) * scale
        for n in range(3):
            part = dqkv_s[:, n * BLOCK : (n + 1) * BLOCK]
            if n == 0:
                note(2, part)
            if n == 2:
                note(3, part)
            keep(1 + n, part.astype(BF16))
        for block in range(6):
            acts[block, rows, :] = acts_s[block]

    @pl.when(step > images)
    def _():
        rows = pl.ds(pl.multiple_of((step - images - 1) * (4 * ROWS), 16), 4 * ROWS)
        unit, rate = normalize(nn(place_ref[...], tok_ref[0]))
        grad = None
        for n in range(3):
            term = nt(acts[1 + n, rows, :], weight(n))
            grad = term if n == 0 else grad + term
        note(0, grad * unit)
        note(1, grad)
        tg_ref[0] = gmid_ref[0] + norm_back(grad, unit, rate, vec(0))

    small_bufs = {"x": small_x, "y": small_y, "z": small_z}
    small_base = 72

    def small_cores():
        part = small_pair.at[me.core]
        return [remote(part, part, *sems, small_base, me.other_core())]

    def small_copies(axis):
        part = small_bufs[axis].at[me.at[axis]]
        first = small_base + 1 + 3 * "xyz".index(axis)
        return [remote(part, part, *sems, first + s - 1, me.along(axis, s)) for s in (1, 2, 3)]

    def small_across():
        copies = []
        for s in (1, 2, 3):
            peer = lax.rem(me.at["x"] + s, SIDE_CHIPS)
            source, target = small_halves.at[peer // 2], small_x.at[me.at["x"]]
            copies.append(remote(source, target, *sems, small_base + s, me.along("x", s)))
        return copies

    def small_start(axis, values):
        small_bufs[axis][pl.ds(me.at[axis], 1)] = values[None]
        start(small_copies(axis))

    def small_sum(axis):
        arrived(small_across() if axis == "x" else small_copies(axis))
        buf = small_bufs[axis]
        return (buf[0] + buf[1]) + (buf[2] + buf[3])

    @pl.when(step == images)
    def _():
        def grad_block(n):
            left = jnp.where(n < 3, 0, 4)
            right = jnp.where(n < 3, n + 1, 5)
            return tn(acts[left], acts[right]).reshape(2, 256, BLOCK)

        for p in range(2):
            low_send[p] = grad_block(2 * p + 1 - me.core).astype(BF16)
            start([low_pair(p)])
        for number in DURING_GRADS[0]:
            high.step(number)
        for p in range(2):
            low_own[p] = grad_block(2 * p + me.core)
        for number in DURING_GRADS[1]:
            high.step(number)
        half = WPAD // 2
        for h in range(heads):
            at = slice(h * WPAD, (h + 1) * WPAD)
            both = jnp.concatenate([pair_ref[:half, at], pair_ref[half:, at]], 1)
            fold_s[pl.ds(h, half, stride=heads), :] = both

        def body(j, total):
            values = fold_s[pl.ds(pl.multiple_of(j * heads, heads), heads), :]
            upper = values.astype(BF16)
            rest = (values - upper.astype(F32)).astype(BF16)
            return total + nt(jnp.concatenate([upper, rest], 0), pair_rows(rel_ref, j))

        total = lax.fori_loop(0, half, body, jnp.zeros((2 * heads, 256), F32), unroll=4)
        table = total[:heads] + total[heads:]
        small_ref[12 : 12 + heads // 2, :256] = table[: heads // 2]
        small_ref[12 : 12 + heads // 2, 256:] = table[heads // 2 :]
        for p in range(2):
            arrived([low_pair(p)])
            for part in range(2):
                total = low_own[p, part] + lo_pair[p, part].astype(F32)
                lo_sums[p, 0, part] = total.astype(BF16)
        low.step(1)

    @pl.when(step == 2 * images)
    def _():
        small_pair[pl.ds(me.core, 1)] = small_ref[...][None]
        start(small_cores())
        high_out = pltpu.make_async_copy(f_ref.at[pl.ds(4, 8)], f_out.at[pl.ds(4, 8)], out_sem.at[0])
        arrived(small_cores())
        small_total = small_pair[0] + small_pair[1]
        small_halves[0] = small_total[:, :256]
        small_halves[1] = small_total[:, 256:]
        start(small_across())
        small_x[pl.ds(me.at["x"], 1)] = small_halves[pl.ds(me.hi, 1)]
        low.step(2)
        small_start("y", small_sum("x"))
        low.step(3)
        high.step(6)
        small_start("z", small_sum("y"))
        low.step(4)
        small_out[...] = small_sum("z")
        low.step(5)
        high.step(7)
        high_out.start()
        low.step(6)
        low.step(7)
        low_out = pltpu.make_async_copy(f_ref.at[pl.ds(0, 4)], f_out.at[pl.ds(0, 4)], out_sem.at[1])
        low_out.start()
        high_out.wait()
        low_out.wait()
        high.all_sent()
        low.all_sent()
        sent([low_pair(p) for p in range(2)])
        sent(small_cores())
        sent(small_across())
        sent(small_copies("y"))
        sent(small_copies("z"))


PLAN = (
    (4, (("high", 2),)),
    (5, (("high", 3),)),
    (6, (("high", 4),)),
)
DURING_GRADS = ((), (5,))


def run_back(qkv, prob, normed, att, gmid, tokens, weights, vecs, rel_rows, small, fc):
    images, tokens_image, width = tokens.shape
    heads = prob.shape[3] // WPAD
    rows = 4 * ROWS
    vmem = pl.BlockSpec(memory_space=pltpu.VMEM)
    far = pl.BlockSpec(memory_space=pltpu.HBM)

    def per_image(shape, index):
        return pl.BlockSpec((1,) + shape, lambda b: (index(b),) + (0,) * len(shape))

    def early(b):
        return jnp.minimum(b, images - 1)

    def late(b):
        return jnp.maximum(b - images - 1, 0)

    def twice(b):
        return jnp.where(b < images, b, late(b))

    def whole(array):
        return pl.BlockSpec(array.shape, lambda b: (0,) * array.ndim, pipeline_mode=pl.Buffered(1))

    def reduce_scratch(count):
        return [
            pltpu.VMEM((2, count, 2, 256, BLOCK), BF16),
            pltpu.VMEM((2, 3, count, 2, 64, BLOCK), BF16),
            pltpu.VMEM((2, count, 2, 64, BLOCK), BF16),
            pltpu.VMEM((2, 3, count, 2, 16, BLOCK), BF16),
            pltpu.VMEM((2, count, 2, 16, BLOCK), BF16),
            pltpu.VMEM((2, 4, count, 16, BLOCK), BF16),
        ]

    return pl.pallas_call(
        partial(back_kernel, images, heads),
        grid=(2 * images + 1,),
        in_specs=[
            per_image(qkv.shape[1:], early),
            per_image(prob.shape[1:], early),
            per_image(normed.shape[1:], early),
            per_image(att.shape[1:], early),
            per_image(gmid.shape[1:], twice),
            per_image((tokens_image, width), late),
            whole(weights),
            whole(vecs),
            whole(rel_rows),
            whole(small),
            far,
        ],
        out_specs=[per_image((rows, width), late), far, vmem],
        out_shape=[
            jax.ShapeDtypeStruct((images, rows, width), F32),
            jax.ShapeDtypeStruct((12, 256, BLOCK), BF16),
            jax.ShapeDtypeStruct((24, 256), F32),
        ],
        scratch_shapes=[
            pltpu.VMEM((4, WPAD, 3 * BLOCK), BF16),
            pltpu.VMEM((4, WPAD, heads * WPAD), F32),
            pltpu.VMEM((rows, width), F32),
            pltpu.VMEM((6, rows, BLOCK), BF16),
            pltpu.VMEM((12, 256, BLOCK), BF16),
            pltpu.VMEM((rows, tokens_image), BF16),
            pltpu.VMEM((4 * WPAD, 128), BF16),
            pltpu.VMEM((24, BLOCK), F32),
            pltpu.VMEM((WPAD, heads * WPAD), F32),
            pltpu.VMEM((heads * WPAD // 2, 128), F32),
            pltpu.VMEM((4, WPAD, BLOCK), BF16),
            pltpu.VMEM((rows, 3 * BLOCK), F32),
            pltpu.VMEM((6, images * rows, BLOCK), BF16),
        ]
        + reduce_scratch(2)
        + [
            pltpu.VMEM((2, 2, 256, BLOCK), BF16),
            pltpu.VMEM((2, 2, 256, BLOCK), F32),
            pltpu.VMEM((2, 2, 256, BLOCK), BF16),
        ]
        + reduce_scratch(1)
        + [
            pltpu.VMEM((2, 24, BLOCK), F32),
            pltpu.VMEM((2, 24, 256), F32),
            pltpu.VMEM((4, 24, 256), F32),
            pltpu.VMEM((4, 24, 256), F32),
            pltpu.VMEM((4, 24, 256), F32),
            pltpu.SemaphoreType.DMA((2,)),
            pltpu.SemaphoreType.DMA((2,)),
            pltpu.SemaphoreType.DMA((82,)),
            pltpu.SemaphoreType.DMA((82,)),
        ],
        compiler_params=pltpu.CompilerParams(
            collective_id=1, has_side_effects=True, vmem_limit_bytes=56 * 1024 * 1024
        ),
        name="back",
    )(qkv, prob, normed, att, gmid, tokens, weights, vecs, rel_rows, small, fc)


def finish_kernel(
    out_win, tg_win, f_ref, small_ref,
    out_ref, tg_ref, n1g, n1b, qkv, qb, vb, table, proj, pb, n2g, n2b, fc1, f1b, fc2, f2b,
    out_in, tg_in, f_in, small_in, out_s, tg_s, wide, in_sem, out_sem, sem,
):
    images = out_win.shape[0]
    per_step = -(-12 // images)
    targets = []
    for n in range(12):
        if n < 3:
            targets.append([(slice(None), qkv.at[:, pl.ds(n * BLOCK, BLOCK)])])
        elif n == 3:
            targets.append([(slice(None), proj)])
        elif n < 8:
            targets.append(
                [
                    (pl.ds(half * 256, 256), fc1.at[:, pl.ds(half * 1024 + (n - 4) * 256, 256)])
                    for half in range(2)
                ]
            )
        else:
            targets.append([(slice(None), fc2.at[pl.ds((n - 8) * 256, 256)])])
    blocks = [range(b * per_step, min(12, (b + 1) * per_step)) for b in range(images)]
    small_copy = pltpu.make_async_copy(small_ref, small_in, in_sem.at[3 * images])
    loads = []
    for b in range(images):
        copies = [
            pltpu.make_async_copy(tg_win.at[b], tg_in.at[b], in_sem.at[3 * b]),
            pltpu.make_async_copy(out_win.at[b], out_in.at[b], in_sem.at[3 * b + 1]),
        ]
        if len(blocks[b]):
            part = pl.ds(blocks[b][0], len(blocks[b]))
            copies.append(pltpu.make_async_copy(f_ref.at[part], f_in.at[part], in_sem.at[3 * b + 2]))
        start(copies)
        loads.append(copies)
    small_copy.start()
    back = back_matrix().astype(BF16)
    stores = []
    for b in range(images):
        for copy in loads[b]:
            copy.wait()
        for n in blocks[b]:
            wide[n] = f_in[n].astype(F32)
            for i, (lanes, target) in enumerate(targets[n]):
                stores.append(pltpu.make_async_copy(wide.at[n, :, lanes], target, sem.at[n, i]))
                stores[-1].start()
        total = tg_in[b]
        upper = total.astype(BF16)
        rest = (total - upper.astype(F32)).astype(BF16)
        tg_s[b] = nn(back, upper) + nn(back, rest)
        stores.append(pltpu.make_async_copy(tg_s.at[b], tg_ref.at[b], out_sem.at[2 * b]))
        stores[-1].start()
        out_s[b] = nn(back, out_in[b]).astype(BF16)
        stores.append(pltpu.make_async_copy(out_s.at[b], out_ref.at[b], out_sem.at[2 * b + 1]))
        stores[-1].start()
    small_copy.wait()
    for row, ref in enumerate((n1g, n1b, qb, vb, pb, n2g, n2b, f2b)):
        ref[...] = small_in[row : row + 1, :].reshape(256)
    for m in range(4):
        f1b[pl.ds(m * 256, 256)] = small_in[8 + m : 9 + m, :].reshape(256)
    table[...] = small_in[12:20, 0 : table.shape[1]]
    for copy in stores:
        copy.wait()


def finish(out_win, tg_win, grads, small, table_rows, heads_here):
    images, rows, width = out_win.shape
    tokens_image = SIDE * SIDE
    vmem = pl.BlockSpec(memory_space=pltpu.VMEM)
    far = pl.BlockSpec(memory_space=pltpu.HBM)
    vector, hidden = ((256,), vmem), ((1024,), vmem)
    outs = [
        vector, vector, ((256, 3 * BLOCK), far), vector, vector, ((heads_here, table_rows), vmem),
        ((256, BLOCK), far), vector, vector, vector, ((256, 4 * BLOCK), far), hidden,
        ((1024, BLOCK), far), vector,
    ]
    return pl.pallas_call(
        finish_kernel,
        in_specs=[far] * 4,
        out_specs=[far, far] + [spec for _, spec in outs],
        out_shape=[
            jax.ShapeDtypeStruct((images, tokens_image, width), BF16),
            jax.ShapeDtypeStruct((images, tokens_image, width), F32),
        ]
        + [jax.ShapeDtypeStruct(shape, F32) for shape, _ in outs],
        scratch_shapes=[
            pltpu.VMEM(out_win.shape, BF16),
            pltpu.VMEM(tg_win.shape, F32),
            pltpu.VMEM(grads.shape, BF16),
            pltpu.VMEM(small.shape, F32),
            pltpu.VMEM((images, tokens_image, width), BF16),
            pltpu.VMEM((images, tokens_image, width), F32),
            pltpu.VMEM((12, 256, BLOCK), F32),
            pltpu.SemaphoreType.DMA((3 * images + 1,)),
            pltpu.SemaphoreType.DMA((2 * images,)),
            pltpu.SemaphoreType.DMA((12, 2)),
        ],
        compiler_params=pltpu.CompilerParams(vmem_limit_bytes=60 * 1024 * 1024),
        name="finish",
    )(out_win, tg_win, grads, small)


def local(
    tokens, image_counts, shift_mask, rel_index, norm1_gain, norm1_bias, qkv_weight, q_bias, v_bias,
    rel_table, proj_weight, proj_bias, norm2_gain, norm2_bias, fc1_weight, fc1_bias, fc2_weight,
    fc2_bias, out_grad,
):
    table_rows, heads_here = rel_table.shape
    qkv, prob, normed, att, block_out, gmid, fc, small, vecs, rel_rows, low_weights = run_front(
        [qkv_weight, proj_weight, fc1_weight, fc2_weight],
        [norm1_gain, norm1_bias, q_bias, v_bias, proj_bias, norm2_gain, norm2_bias, fc2_bias],
        fc1_bias, rel_table.T, rel_index, shift_mask.transpose(1, 0, 2), tokens, out_grad, image_counts,
    )
    tokens_grad, grads, small = run_back(
        qkv, prob, normed, att, gmid, tokens, low_weights, vecs, rel_rows, small, fc.reshape(4, 2, 256, BLOCK)
    )
    outs = finish(block_out, tokens_grad, grads, small, table_rows, heads_here)
    return (*outs[:7], outs[7].T, *outs[8:])


def solution(mesh):
    split = P(("replica", "shard"), None, None)
    vector, matrix, table = P("shard"), P("shard", None), P(None, "shard")
    return jax.shard_map(
        local,
        mesh=mesh,
        in_specs=(
            split, P(("replica", "shard")), P(), P(), vector, vector, matrix, vector, vector, table,
            matrix, vector, vector, vector, matrix, vector, matrix, vector, split,
        ),
        out_specs=(
            split, split, vector, vector, matrix, vector, vector, table, matrix, vector, vector,
            vector, matrix, vector, matrix, vector,
        ),
        check_vma=False,
    )
```
